32 devices in a mesh: groups: 2 (over y), tiles: 4 (over z), cols: 2 (over core), dates: 2 (over x).
Axes of the slice: x: 2, y: 2, z: 4, core: 2. Of those that a mesh axis runs over, the one named last changes fastest.
Arguments:
- imagery: bfloat16 [8, 4, 432, 4096], P(('groups', 'tiles'), 'cols', 'dates'), parts along dimension 0, may hold values from -6 to 6
- pixel_mask: int32 [8, 4, 4096], P(('groups', 'tiles'), ('cols', 'dates')), parts along dimension 0, may hold values 0 or 1
- point_pixel: int32 [8, 4, 4096], P(('groups', 'tiles'), ('cols', 'dates')), parts along dimension 0, may hold values from 0 to 4095
- point_yield: float32 [8, 4, 4096], P(('groups', 'tiles'), ('cols', 'dates')), parts along dimension 0, may hold values from -6 to 6
Outputs:
- prediction: float32 [8, 4, 4096], P(('groups', 'tiles'), ('cols', 'dates')), parts along dimension 0
- distance: float32 [8, 4, 4096], P(('groups', 'tiles'), ('cols', 'dates')), parts along dimension 0
- residual: float32 [8, 4, 4096], P(('groups', 'tiles'), ('cols', 'dates')), parts along dimension 0
The draws below stay inside these ranges and needn't reach their ends.
There are 2 independent parts, one for each index of `groups`. The reference program is written for one: setup_inputs(seed, part) draws one part's arguments, and reference() takes and returns one part's arrays. A program takes and returns all parts, laid end to end along the dimension named above; each array names one. Nothing has to cross between parts.
All inputs are finite; a program needn't handle non-finite values. No bound on the sum of `pixel_mask` on one device may be relied on, other than what follows from the above.
Results may differ from the reference program's by a relative error of at most 0.0003.
Values may be sent and summed in bfloat16 or wider, within the bound.
A program may use at most 128 MiB of HBM per device.

```python
import math
import jax
import jax.numpy as jnp
from jax import lax

F = 432
PIX = 4096
NPTS = 4096
GRID_ROWS = 4
GRID_COLS = 4


def draw_imagery(key, part):
    subkeys = jax.random.split(key, 5)
    full_shape = (GRID_ROWS, GRID_COLS, F, PIX)
    pixel_shape = (GRID_ROWS, GRID_COLS, 1, PIX)
    noise_scale = jnp.exp(jax.random.uniform(subkeys[0], (1, 1, F, 1), jnp.float32, math.log(0.1), 0.0))
    loading = jax.random.uniform(subkeys[1], (1, 1, F, 1), jnp.float32, -1.2, 1.2)
    tile_gain = jnp.exp(jax.random.uniform(subkeys[2], (GRID_ROWS, GRID_COLS, 1, 1), jnp.float32, math.log(0.7), math.log(1.4)))
    shared = jax.random.normal(subkeys[3], pixel_shape, jnp.float32)
    independent = jax.random.normal(subkeys[4], full_shape, jnp.float32)
    values = tile_gain * loading * shared + noise_scale * independent
    return jnp.clip(values, -6.0, 6.0).astype(jnp.bfloat16)


def with_ends(array, rng, smallest, top_value):
    place = [jax.random.randint(jax.random.fold_in(rng, axis), (), 0, length) for axis, length in enumerate(array.shape)]
    main_axis = array.shape.index(max(array.shape))
    neighbour = place[:main_axis] + [(place[main_axis] + 1) % array.shape[main_axis]] + place[main_axis + 1:]
    return array.at[tuple(place)].set(smallest).at[tuple(neighbour)].set(top_value)


def block_levels(key, dims, cuts, low, largest):
    def one(dim, parts):
        draws = jax.random.uniform(jax.random.fold_in(jax.random.fold_in(key, 6), dim), (parts,), jnp.float32, low / len(cuts), largest / len(cuts))
        return jnp.repeat(jnp.exp(draws), dims[dim] // parts).reshape((-1,) + (1,) * (len(dims) - dim - 1))

    loudness = one(*cuts[0])
    for cut in cuts[1:]:
        loudness = loudness * one(*cut)
    return loudness


def centred(rng, shape, scale, most, cuts=(), kind=jnp.bfloat16):
    loudness = block_levels(rng, shape, cuts, -0.22, 0.18) if cuts else 1.0
    entries = jax.random.normal(rng, shape, jnp.float32) * scale * loudness
    return jnp.minimum(jnp.maximum(entries, -most), most).astype(kind)


def setup_inputs(seed: int = 0, part: int = 0) -> dict:
    seeds = jax.random.split(jax.random.key(seed), 5)
    part_splits = jax.random.split(jax.random.fold_in(seeds[4], part), 5)
    return {
        "imagery": draw_imagery(jax.random.fold_in(jax.random.fold_in(seeds[4], part), 71), part),
        "pixel_mask": with_ends((jax.random.randint(part_splits[1], (GRID_ROWS, GRID_COLS, PIX), 0, 4) < 3).astype(jnp.int32), jax.random.fold_in(part_splits[1], 1), 0, 1),
        "point_pixel": with_ends(jax.random.randint(part_splits[2], (GRID_ROWS, GRID_COLS, NPTS), 0, PIX), jax.random.fold_in(part_splits[2], 1), 0, PIX - 1).astype(jnp.int32),
        "point_yield": centred(part_splits[3], (GRID_ROWS, GRID_COLS, NPTS), 1.0, 6.0, ((0, 4), (1, 4)), jnp.float32),
    }


ridge_term = 0.05

def lower_solve(factor, right):
    return lax.linalg.triangular_solve(factor, right, left_side=True, lower=True)

def chol_solve(factor, right):
    first = lower_solve(factor, right[:, None])
    second = lax.linalg.triangular_solve(factor, first, left_side=True, lower=True, transpose_a=True)
    return second[:, 0]

def tile_stats(args):
    feats, mask, index, yields = args
    feats32 = feats.astype(jnp.float32)
    counts = jax.ops.segment_sum(jnp.ones_like(index), index, num_segments=PIX)
    totals = jax.ops.segment_sum(yields, index, num_segments=PIX)
    weight = mask.astype(jnp.float32) * (counts > 0).astype(jnp.float32)
    target = totals / jnp.maximum(counts, 1).astype(jnp.float32)
    gram = jnp.dot(feats32 * weight[None, :], feats32.T, precision=lax.Precision.HIGHEST)
    moment = jnp.dot(feats32, weight * target, precision=lax.Precision.HIGHEST)
    return jnp.concatenate([gram, moment[None, :]], 0)

def tile_solve(args):
    feats, packed, index, yields = args
    feats32 = feats.astype(jnp.float32)
    system = packed[:F] / PIX + ridge_term * jnp.eye(F, dtype=jnp.float32)
    rhs = packed[F] / PIX
    factor = jnp.linalg.cholesky(system)
    beta = chol_solve(factor, rhs)
    fitted = jnp.dot(beta, feats32, precision=lax.Precision.HIGHEST)
    solved = lower_solve(factor, feats32)
    spread = jnp.sum(solved * solved, axis=0) / F
    return (fitted, spread, yields - fitted[index])

def reference(imagery, pixel_mask, point_pixel, point_yield):
    count = GRID_ROWS * GRID_COLS
    feats = imagery.reshape(count, F, PIX)
    masks = pixel_mask.reshape(count, PIX)
    index = point_pixel.reshape(count, NPTS)
    yields = point_yield.reshape(count, NPTS)
    packed = lax.map(tile_stats, (feats, masks, index, yields)).reshape(GRID_ROWS, GRID_COLS, F + 1, F)
    padded = jnp.pad(packed, ((1, 1), (1, 1), (0, 0), (0, 0)))
    kernel = (0.5, 1.0, 0.5)
    window = jnp.zeros_like(packed)
    for row in range(3):
        for col in range(3):
            window = window + kernel[row] * kernel[col] * padded[row:row + GRID_ROWS, col:col + GRID_COLS]
    fitted, spread, resid = lax.map(tile_solve, (feats, window.reshape(count, F + 1, F), index, yields))
    return (fitted.reshape(GRID_ROWS, GRID_COLS, PIX), spread.reshape(GRID_ROWS, GRID_COLS, PIX), resid.reshape(GRID_ROWS, GRID_COLS, NPTS))
```

```python
import functools

import jax
import jax.numpy as jnp
from jax import lax
from jax.experimental import pallas as pl
from jax.experimental.pallas import tpu as pltpu
from jax.sharding import PartitionSpec as P

ridge_term = 0.05
LANES = 128
CHUNK = 512
PIECES = 8
F32 = jnp.float32
BF16 = jnp.bfloat16
NT = (((1,), (1,)), ((), ()))


def split3(x):
    a = x.astype(BF16)
    rest = x - a.astype(F32)
    b = rest.astype(BF16)
    c = (rest - b.astype(F32)).astype(BF16)
    return a, b, c


def one_hots(index, rows):
    points = index.shape[1]
    high = lax.broadcasted_iota(jnp.int32, (rows, points), 0) == index // LANES
    low = lax.broadcasted_iota(jnp.int32, (LANES, points), 0) == index % LANES
    return high, low


def segment_kernel(index_ref, yield_ref, mask_ref, weight_ref, product_ref):
    rows = mask_ref.shape[0]
    high, low = one_hots(index_ref[...], rows)
    low = jnp.where(low, 1.0, 0.0).astype(BF16)
    pieces = [jnp.where(high, 1.0, 0.0).astype(BF16)]
    for piece in split3(yield_ref[...]):
        pieces.append(jnp.where(high, piece.astype(F32), 0.0).astype(BF16))
    sums = lax.dot_general(
        jnp.concatenate(pieces, 0), low, NT, preferred_element_type=F32
    )
    counts = sums[:rows]
    totals = sums[rows : 2 * rows] + sums[2 * rows : 3 * rows] + sums[3 * rows :]
    weight = jnp.where(counts > 0, mask_ref[...].astype(F32), 0.0)
    weight_ref[...] = weight
    product_ref[...] = weight * (totals / jnp.maximum(counts, 1.0))


def bands(width):
    blocks, offset = [], 0
    for i in range(pl.cdiv(width, LANES)):
        height = min(LANES, width - i * LANES)
        for j in range(i + 1):
            blocks.append((i, j, height, offset))
            offset += height
    return blocks, offset


def gram_kernel(feats_ref, weight_ref, product_ref, out_ref, acc):
    width, pixels = feats_ref.shape
    acc[...] = jnp.zeros_like(acc)

    def step(c, _):
        at = pl.multiple_of(c * CHUNK, CHUNK)
        feats = feats_ref[:, pl.ds(at, CHUNK)]
        left = []
        for s in range(CHUNK // LANES):
            row = pl.ds(c * (CHUNK // LANES) + s, 1)
            part = feats[:, s * LANES : (s + 1) * LANES]
            scaled = part * weight_ref[row, :].astype(BF16)
            a, b, d = (p.astype(F32) for p in split3(product_ref[row, :]))
            line = lax.broadcasted_iota(jnp.int32, (16, LANES), 0)
            extra = jnp.where(
                line == 0, a, jnp.where(line == 1, b, jnp.where(line == 2, d, 0.0))
            )
            left.append(jnp.concatenate([scaled, extra.astype(BF16)], 0))
        acc[...] += lax.dot_general(
            jnp.concatenate(left, 1), feats, NT, preferred_element_type=F32
        )
        return 0

    lax.fori_loop(0, pixels // CHUNK, step, 0)
    blocks, offset = bands(width)
    out_ref[...] = jnp.zeros_like(out_ref)
    for i, j, height, at in blocks:
        wide = min(LANES, width - j * LANES)
        out_ref[at : at + height, :wide] = acc[
            i * LANES : i * LANES + height, j * LANES : j * LANES + wide
        ]
    moment = acc[width : width + 1] + acc[width + 1 : width + 2]
    moment = moment + acc[width + 2 : width + 3]
    for j in range(pl.cdiv(width, LANES)):
        wide = min(LANES, width - j * LANES)
        out_ref[offset + j : offset + j + 1, :wide] = moment[
            :, j * LANES : j * LANES + wide
        ]


def small_inverse(p):
    n = len(p)
    for k in range(n):
        d = 1.0 / p[k][k]
        row = [d if j == k else p[k][j] * d for j in range(n)]
        new = []
        for i in range(n):
            if i == k:
                new.append(row)
            else:
                new.append(
                    [
                        -p[i][k] * d if j == k else p[i][j] - p[i][k] * row[j]
                        for j in range(n)
                    ]
                )
        p = new
    return p


def block_inverse(block, pivots, group=8):
    tiles = [block[8 * g : 8 * g + 8] for g in range(LANES // 8)]
    lane = lax.broadcasted_iota(jnp.int32, (8, LANES), 1)
    line = lax.broadcasted_iota(jnp.int32, (8, LANES), 0)
    for k in range(0, pivots, group):
        g, r = divmod(k, 8)
        cols = [
            [
                jnp.broadcast_to(t[:, k + j : k + j + 1], (8, LANES))
                for t in tiles
            ]
            for j in range(group)
        ]
        small = [
            [cols[j][g][r + i : r + i + 1] for j in range(group)]
            for i in range(group)
        ]
        small = small_inverse(small)
        rows = []
        for i in range(group):
            old = tiles[g][r + i : r + i + 1]
            old = jnp.where((lane[:1] >= k) & (lane[:1] < k + group), 0.0, old)
            rows.append(jnp.where(lane[:1] == k + i, 1.0, old))
        new_rows = []
        for i in range(group):
            total = small[i][0] * rows[0]
            for j in range(1, group):
                total = total + small[i][j] * rows[j]
            new_rows.append(jnp.broadcast_to(total, (8, LANES)))
        keep = (lane < k) | (lane >= k + group)
        for t in range(LANES // 8):
            value = jnp.where(keep, tiles[t], 0.0)
            for j in range(group):
                value = value - cols[j][t] * new_rows[j]
            if t == g:
                for i in range(group):
                    value = jnp.where(line == r + i, new_rows[i], value)
            tiles[t] = value
    return jnp.concatenate(tiles, 0)


NN = (((1,), (0,)), ((), ()))


def dot32(a, b, dims=NN):
    return lax.dot_general(
        a, b, dims, precision=lax.Precision.HIGHEST, preferred_element_type=F32
    )


def solve_kernel(
    packed_ref,
    feats_ref,
    index_ref,
    yield_ref,
    fitted_ref,
    spread_ref,
    resid_ref,
    system,
    base,
    high_ref,
    low_ref,
    fit,
):
    width, pixels = feats_ref.shape
    count = pl.cdiv(width, LANES)
    size = count * LANES
    blocks, offset = bands(width)
    scale = 1.0 / pixels
    line = lax.broadcasted_iota(jnp.int32, (LANES, LANES), 0)
    lane = lax.broadcasted_iota(jnp.int32, (LANES, LANES), 1)
    for i, j, height, at in blocks:
        value = packed_ref[at : at + height] * scale
        if height < LANES:
            value = jnp.concatenate(
                [value, jnp.zeros((LANES - height, LANES), F32)], 0
            )
        if i == j:
            diagonal = jnp.where(line < height, ridge_term, 1.0)
            value = value + jnp.where(line == lane, diagonal, 0.0)
        system[i * LANES : (i + 1) * LANES, j * LANES : (j + 1) * LANES] = value
        if i != j:
            system[j * LANES : (j + 1) * LANES, i * LANES : (i + 1) * LANES] = value.T

    base[...] = system[...]
    column = lax.broadcasted_iota(jnp.int32, (LANES, size), 1)
    wide_line = lax.broadcasted_iota(jnp.int32, (LANES, size), 0)

    def eliminate(k, pivots):
        at = k * LANES if isinstance(k, int) else pl.multiple_of(k * LANES, LANES)
        here = pl.ds(at, LANES)
        inverse = block_inverse(system[here, here], pivots)
        inside = (column >= at) & (column < at + LANES)
        unit = jnp.where(column == wide_line + at, 1.0, 0.0)
        right = dot32(inverse, jnp.where(inside, unit, system[here, :]))
        left = system[:, here]
        system[:, here] = jnp.zeros_like(left)
        system[...] -= dot32(left, right)
        system[here, :] = right

    full = width // LANES

    def body(k, _):
        eliminate(k, LANES)
        return 0

    lax.fori_loop(0, full, body, 0)
    if width % LANES:
        eliminate(full, width % LANES)

    rhs = jnp.concatenate(
        [packed_ref[offset + j : offset + j + 1] for j in range(count)], 1
    )
    rhs = jnp.broadcast_to(rhs * scale, (8, size))
    beta = dot32(rhs, system[...])
    beta = beta + dot32(rhs - dot32(beta, base[...]), system[...])
    beta = beta[:1, :width]
    inverse = system[:width, :width]
    upper = inverse.astype(BF16)
    a, b, d = (p.astype(F32) for p in split3(beta))
    row16 = lax.broadcasted_iota(jnp.int32, (16, width), 0)
    extra = jnp.where(row16 == 0, a, jnp.where(row16 == 1, b, jnp.where(row16 == 2, d, 0.0)))
    high_ref[...] = jnp.concatenate([upper, extra.astype(BF16)], 0)
    low_ref[...] = (inverse - upper.astype(F32)).astype(BF16)

    def step(c, _):
        at = pl.multiple_of(c * CHUNK, CHUNK)
        feats = feats_ref[:, pl.ds(at, CHUNK)]
        first = jnp.dot(high_ref[...], feats, preferred_element_type=F32)
        second = jnp.dot(low_ref[...], feats, preferred_element_type=F32)
        total = (first[:width] + second) * feats.astype(F32)
        spread_ref[:, pl.ds(at, CHUNK)] = jnp.sum(total, 0, keepdims=True) / width
        fitted = first[width : width + 1] + (
            first[width + 1 : width + 2] + first[width + 2 : width + 3]
        )
        fitted_ref[:, pl.ds(at, CHUNK)] = fitted
        for s in range(CHUNK // LANES):
            fit[pl.ds(c * (CHUNK // LANES) + s, 1), :] = fitted[
                :, s * LANES : (s + 1) * LANES
            ]
        return 0

    lax.fori_loop(0, pixels // CHUNK, step, 0)

    rows = pixels // LANES
    high, low = one_hots(index_ref[...], rows)
    low = jnp.where(low, 1.0, 0.0).astype(BF16)
    table = jnp.concatenate(split3(fit[...]), 0)
    found = jnp.dot(table, low, preferred_element_type=F32)
    found = found[:rows] + (found[rows : 2 * rows] + found[2 * rows :])
    value = jnp.sum(jnp.where(high, found, 0.0), 0, keepdims=True)
    resid_ref[...] = yield_ref[...] - value


PARAMS = pltpu.CompilerParams(vmem_limit_bytes=48 * 1024 * 1024)


def segments(index, yields, mask):
    shape = jax.ShapeDtypeStruct(mask.shape, F32)
    return pl.pallas_call(
        segment_kernel,
        out_shape=(shape, shape),
        compiler_params=PARAMS,
        cost_estimate=pl.CostEstimate(
            flops=2 * 128 * 128 * index.shape[1],
            bytes_accessed=16 * index.shape[1],
            transcendentals=0,
        ),
        name="segments",
    )(index, yields, mask)


def grams(feats, weight, product):
    width, pixels = feats.shape
    rows = bands(width)[1] + 8 * pl.cdiv(pl.cdiv(width, LANES), 8)
    return pl.pallas_call(
        gram_kernel,
        out_shape=jax.ShapeDtypeStruct((rows, LANES), F32),
        scratch_shapes=[pltpu.VMEM((width + 16, width), F32)],
        compiler_params=PARAMS,
        name="grams",
    )(feats, weight, product)


def solves(packed, feats, index, yields):
    width, pixels = feats.shape
    size = pl.cdiv(width, LANES) * LANES
    shape = jax.ShapeDtypeStruct((1, pixels), F32)
    return pl.pallas_call(
        solve_kernel,
        out_shape=(shape, shape, jax.ShapeDtypeStruct(yields.shape, F32)),
        scratch_shapes=[
            pltpu.VMEM((size, size), F32),
            pltpu.VMEM((size, size), F32),
            pltpu.VMEM((width + 16, width), BF16),
            pltpu.VMEM((width, width), BF16),
            pltpu.VMEM((pixels // LANES, LANES), F32),
        ],
        compiler_params=PARAMS,
        name="solves",
    )(packed, feats, index, yields)


def window_kernel(shape, own_ref, out_ref, landed, middle, send_sem, recv_sem):
    tiles, cols, dates = shape
    row = lax.axis_index("tiles")
    col = lax.axis_index("cols") * dates + lax.axis_index("dates")
    total = own_ref.shape[0]
    step = -(-total // (8 * PIECES)) * 8
    pieces = [pl.ds(at, min(step, total - at)) for at in range(0, total, step)]

    def place(c):
        return {"cols": c // dates, "dates": c % dates}

    links = (
        (row < tiles - 1, lambda: {"tiles": row + 1}, row > 0, lambda: {"tiles": row - 1}),
        (row > 0, lambda: {"tiles": row - 1}, row < tiles - 1, lambda: {"tiles": row + 1}),
        (col < cols * dates - 1, lambda: place(col + 1), col > 0, lambda: place(col - 1)),
        (col > 0, lambda: place(col - 1), col < cols * dates - 1, lambda: place(col + 1)),
    )

    def copy(d, i, source, device):
        return pltpu.make_async_remote_copy(
            src_ref=source.at[pieces[i]],
            dst_ref=landed.at[d, pieces[i]],
            send_sem=send_sem.at[d, i],
            recv_sem=recv_sem.at[d, i],
            device_id=device,
            device_id_type=pl.DeviceIdType.MESH,
        )

    barrier = pltpu.get_barrier_semaphore()
    for there, target, _, _ in links:

        @pl.when(there)
        def _(target=target):
            pl.semaphore_signal(
                barrier, inc=1, device_id=target(), device_id_type=pl.DeviceIdType.MESH
            )

    peers = sum(there.astype(jnp.int32) for there, _, _, _ in links)
    pl.semaphore_wait(barrier, peers)

    def send(d, i, source):
        there, target, _, _ = links[d]

        @pl.when(there)
        def _():
            copy(d, i, source, target()).start()

    def receive(d, i, source, into):
        _, _, there, origin = links[d]

        @pl.when(there)
        def _():
            copy(d, i, source, origin()).wait_recv()
            into[pieces[i]] += 0.5 * landed[d, pieces[i]]

    count = len(pieces)
    for i in range(count):
        send(0, i, own_ref)
        send(1, i, own_ref)
    for i in range(count):
        middle[pieces[i]] = own_ref[pieces[i]]
        receive(0, i, own_ref, middle)
        receive(1, i, own_ref, middle)
        send(2, i, middle)
        send(3, i, middle)
    for i in range(count):
        out_ref[pieces[i]] = middle[pieces[i]]
        receive(2, i, middle, out_ref)
        receive(3, i, middle, out_ref)
    for i in range(count):
        for d in range(4):
            there, target, _, _ = links[d]

            @pl.when(there)
            def _(d=d, i=i, target=target):
                copy(d, i, own_ref if d < 2 else middle, target()).wait_send()


def window(packed):
    shape = tuple(lax.axis_size(name) for name in ("tiles", "cols", "dates"))
    in_vmem = pl.BlockSpec(memory_space=pltpu.VMEM)
    return pl.pallas_call(
        functools.partial(window_kernel, shape),
        out_shape=jax.ShapeDtypeStruct(packed.shape, F32),
        in_specs=[in_vmem],
        out_specs=in_vmem,
        scratch_shapes=[
            pltpu.VMEM((4,) + packed.shape, F32),
            pltpu.VMEM(packed.shape, F32),
            pltpu.SemaphoreType.DMA((4, PIECES)),
            pltpu.SemaphoreType.DMA((4, PIECES)),
        ],
        compiler_params=pltpu.CompilerParams(
            collective_id=0,
            has_side_effects=True,
            vmem_limit_bytes=48 * 1024 * 1024,
        ),
        name="window",
    )(packed)


def on_device(imagery, pixel_mask, point_pixel, point_yield):
    whole = lax.all_to_all(imagery, "dates", split_axis=1, concat_axis=2, tiled=True)
    feats = whole[0, 0]
    pixels = feats.shape[1]
    index = point_pixel[0]
    yields = point_yield[0]
    mask = pixel_mask.reshape(pixels // LANES, LANES)
    weight, product = segments(index, yields, mask)
    packed = grams(feats, weight, product)
    packed = window(packed)
    fitted, spread, resid = solves(packed, feats, index, yields)
    return (fitted[None], spread[None], resid[None])


def step_rows(full, k):
    return 128 if k < full else 64


def payload_rows(full, k):
    return (128 if k < full else 48) * (k + 1) + 8


def payload_starts(full):
    starts, at = [], 0
    for k in range(full + 1):
        starts.append(at)
        at += payload_rows(full, k)
    return starts, at


def squeeze(block):
    return jnp.concatenate([block[0:24], block[32:56]], 0)


def stretch(block):
    gap = jnp.zeros((8, block.shape[1]), block.dtype)
    return jnp.concatenate([block[0:24], gap, block[24:48], gap], 0)


def factor8(small):
    plane = lax.broadcasted_iota(jnp.int32, small.shape, 0)
    line = lax.broadcasted_iota(jnp.int32, small.shape, 1)
    lower = jnp.where(plane == line, 1.0, 0.0)
    pivots = jnp.zeros(small.shape[1:], F32)
    for p in range(8):
        pivot = small[p : p + 1, p : p + 1]
        pivots = jnp.where(line[0] == p, pivot[0], pivots)
        lower = jnp.where((line == p) & (plane < p), small, lower)
        d = 1.0 / pivot
        row = small[:, p : p + 1] * d
        column = small[p : p + 1]
        rest = small - column * row
        rest = jnp.where(plane == p, -column * d, rest)
        row = jnp.where(plane[:, :1] == p, d, row)
        small = jnp.where(line == p, row, rest)
    return small, lower, lax.rsqrt(pivots)


def mix(planes, lines):
    total = planes[0] * lines[0:1]
    for j in range(1, 8):
        total = total + planes[j] * lines[j : j + 1]
    return total


def block_factor(block, groups):
    rows = block.shape[0]
    lane = lax.broadcasted_iota(jnp.int32, (8, LANES), 1)
    line = lax.broadcasted_iota(jnp.int32, (8, LANES), 0)
    result = [jnp.zeros((8, LANES), F32)] * (rows // 8)
    below, first = block, 0
    for g in groups:
        k = 8 * g
        below = below[k - first :]
        top = below[:8]
        small = jnp.stack(
            [jnp.broadcast_to(top[:, k + j : k + j + 1], (8, LANES)) for j in range(8)]
        )
        small, lower, root = factor8(small)
        inside = (lane >= k) & (lane < k + 8)
        top = jnp.where(inside, jnp.where(lane == line + k, 1.0, 0.0), top)
        result[g] = jnp.where(lane < k + 8, mix(lower, top) * root, 0.0)
        below = below[8:]
        first = k + 8
        if below.shape[0]:
            new = mix(small, top)
            cols = [below[:, k + j : k + j + 1] for j in range(8)]
            keep = (lane[:1] < k) | (lane[:1] >= k + 8)
            below = jnp.where(keep, below, 0.0)
            for j in range(8):
                below = below - cols[j] * new[j : j + 1]
    return jnp.concatenate(result, 0)


def split2(x):
    high = x.astype(BF16)
    return high, (x - high.astype(F32)).astype(BF16)


def fused_kernel(
    tiles,
    img,
    index_hbm,
    yield_hbm,
    mask_hbm,
    fitted_ref,
    spread_ref,
    resid_ref,
    feats,
    whole,
    tail,
    index_ref,
    yield_ref,
    mask_ref,
    weight_rows,
    product_rows,
    low_ref,
    acc,
    own,
    middle,
    outgoing,
    landed,
    inverse,
    high_r,
    low_r,
    rhs_ref,
    z_ref,
    fit8,
    spread8,
    fit,
    local_sem,
    bulk_send,
    bulk_recv,
    z_send,
    z_recv,
    core_send,
    core_recv,
    x_send,
    x_recv,
):
    half, pixels = img.shape[2:]
    full = half // 64
    steps = full + 1
    rows = pixels // LANES
    scale = 1.0 / pixels
    starts, _ = payload_starts(full)
    mesh_ids = pl.DeviceIdType.MESH

    z = lax.axis_index("tiles")
    c = lax.axis_index("cols")
    d = lax.axis_index("dates")
    across = {"dates": 1 - d}
    core = {"cols": 1 - c}
    up, down = {"tiles": z + 1}, {"tiles": z - 1}
    has_up, has_down = z < tiles - 1, z > 0
    joins = c == d

    def place(k, s):
        if k < full:
            return pl.multiple_of(128 * k + 64 * s, 16)
        return pl.multiple_of(128 * full + 32 * s, 16)

    height = [64] * full + [16]
    source_at = [64 * k for k in range(steps)]

    local = [
        pltpu.make_async_copy(index_hbm.at[0], index_ref, local_sem.at[0]),
        pltpu.make_async_copy(yield_hbm.at[0], yield_ref, local_sem.at[1]),
        pltpu.make_async_copy(mask_hbm, mask_ref, local_sem.at[2]),
        pltpu.make_async_copy(img.at[0], whole, local_sem.at[3]),
    ]
    for k in range(steps):
        local.append(
            pltpu.make_async_copy(
                img.at[0, d, pl.ds(source_at[k], height[k])],
                feats.at[pl.ds(place(k, d), height[k])],
                local_sem.at[4 + k],
            )
        )
    for copy in local:
        copy.start()

    barrier = pltpu.get_barrier_semaphore()
    peers = ((has_up, up), (has_down, down), (None, core), (None, across))
    for there, target in peers:

        def greet(target=target):
            pl.semaphore_signal(
                barrier, inc=1, device_id=target, device_id_type=mesh_ids
            )

        if there is None:
            greet()
        else:
            pl.when(there)(greet)
    pl.semaphore_wait(barrier, 2 + has_up.astype(jnp.int32) + has_down.astype(jnp.int32))

    bulk = []
    for k in range(steps):
        bulk.append(
            pltpu.make_async_remote_copy(
                src_ref=img.at[0, 1 - d, pl.ds(source_at[k], height[k])],
                dst_ref=feats.at[pl.ds(place(k, d), height[k])],
                send_sem=bulk_send.at[k],
                recv_sem=bulk_recv.at[k],
                device_id=across,
                device_id_type=mesh_ids,
            )
        )
    bulk.append(
        pltpu.make_async_remote_copy(
            src_ref=tail.at[1 - d],
            dst_ref=feats.at[pl.ds(pl.multiple_of(128 * full + 32 * d + 16, 16), 16)],
            send_sem=bulk_send.at[steps],
            recv_sem=bulk_recv.at[steps],
            device_id=across,
            device_id_type=mesh_ids,
        )
    )
    for k in range(steps):
        bulk[k].start()

    for copy in local[:4]:
        copy.wait()
    for s in range(2):
        end = whole[s][half - 8 : half]
        tail[s] = jnp.concatenate([end, jnp.zeros_like(end)], 0)
    bulk[steps].start()
    feats[pl.ds(pl.multiple_of(128 * full + 32 * d + 16, 16), 16), :] = tail[d]

    high, low = one_hots(index_ref[...], rows)
    low = jnp.where(low, 1.0, 0.0).astype(BF16)
    low_ref[...] = low
    parts = [jnp.where(high, 1.0, 0.0).astype(BF16)]
    for piece in split3(yield_ref[...]):
        parts.append(jnp.where(high, piece.astype(F32), 0.0).astype(BF16))
    sums = lax.dot_general(
        jnp.concatenate(parts, 0), low, NT, preferred_element_type=F32
    )
    counts = sums[:rows]
    totals = sums[rows : 2 * rows] + sums[2 * rows : 3 * rows] + sums[3 * rows :]
    weight = jnp.where(counts > 0, mask_ref[...].astype(F32), 0.0)
    product = weight * (totals / jnp.maximum(counts, 1.0))
    pa, pb, pc = (p.astype(F32) for p in split3(product))
    line16 = lax.broadcasted_iota(jnp.int32, (16, LANES), 0)
    for r in range(rows):
        at = slice(r * LANES, (r + 1) * LANES)
        weight_rows[:, at] = jnp.broadcast_to(weight[r : r + 1], (16, LANES)).astype(BF16)
        extra = jnp.where(
            line16 == 0,
            pa[r : r + 1],
            jnp.where(
                line16 == 1,
                pb[r : r + 1],
                jnp.where(line16 == 2, pc[r : r + 1], 0.0),
            ),
        )
        product_rows[:, at] = extra.astype(BF16)

    acc[...] = jnp.zeros_like(acc)
    inverse[...] = jnp.zeros_like(inverse)
    fit8[...] = jnp.zeros_like(fit8)
    spread8[...] = jnp.zeros_like(spread8)

    def payload(k):
        return pl.ds(starts[k], payload_rows(full, k))

    def z_copy(way, k, target):
        return pltpu.make_async_remote_copy(
            src_ref=own.at[payload(k)],
            dst_ref=landed.at[way, payload(k)],
            send_sem=z_send.at[way, k],
            recv_sem=z_recv.at[way, k],
            device_id=target,
            device_id_type=mesh_ids,
        )

    def core_copy(k):
        return pltpu.make_async_remote_copy(
            src_ref=middle.at[payload(k)],
            dst_ref=landed.at[2, payload(k)],
            send_sem=core_send.at[k],
            recv_sem=core_recv.at[k],
            device_id=core,
            device_id_type=mesh_ids,
        )

    def x_copy(k):
        return pltpu.make_async_remote_copy(
            src_ref=outgoing.at[payload(k)],
            dst_ref=landed.at[3, payload(k)],
            send_sem=x_send.at[k],
            recv_sem=x_recv.at[k],
            device_id=across,
            device_id_type=mesh_ids,
        )

    def gram(k):
        count = step_rows(full, k)
        base, end = 128 * k, 128 * k + count
        local[4 + k].wait()
        bulk[k].wait_recv()
        if k == full:
            bulk[steps].wait_recv()
        acc[: count + 16, :end] = jnp.zeros((count + 16, end), F32)

        def chunk(i, _):
            at = pl.ds(pl.multiple_of(i * CHUNK, CHUNK), CHUNK)
            weights = jnp.concatenate([weight_rows[:, at]] * (count // 16), 0)
            left = jnp.concatenate(
                [feats[base:end, at] * weights, product_rows[:, at]], 0
            )
            acc[: count + 16, :end] += lax.dot_general(
                left, feats[:end, at], NT, preferred_element_type=F32
            )
            return 0

        lax.fori_loop(0, pixels // CHUNK, chunk, 0)
        at = starts[k]
        for j in range(k + 1):
            block = acc[:count, 128 * j : 128 * j + 128]
            if k == full:
                block = squeeze(block)
            own[at : at + block.shape[0]] = block
            at += block.shape[0]
        moment = acc[count : count + 1, base : base + 128]
        moment = moment + acc[count + 1 : count + 2, base : base + 128]
        moment = moment + acc[count + 2 : count + 3, base : base + 128]
        own[at : at + 8] = jnp.broadcast_to(moment, (8, LANES))
        pl.when(has_up)(lambda: z_copy(0, k, up).start())
        pl.when(has_down)(lambda: z_copy(1, k, down).start())

    def z_join(k):
        at = payload(k)
        middle[at] = own[at]

        @pl.when(has_down)
        def _():
            z_copy(0, k, down).wait_recv()
            middle[at] += 0.5 * landed[0, at]

        @pl.when(has_up)
        def _():
            z_copy(1, k, up).wait_recv()
            middle[at] += 0.5 * landed[1, at]

        @pl.when(jnp.logical_not(joins))
        def _():
            core_copy(k).start()
            outgoing[at] = middle[at]

        @pl.when(joins)
        def _():
            core_copy(k).wait_recv()
            outgoing[at] = middle[at] + landed[2, at]

        x_copy(k).start()

    def solve(k):
        at = payload(k)
        x_copy(k).wait_recv()
        count = step_rows(full, k)
        base = 128 * k
        window = (middle[at] + 0.5 * landed[3, at]) * scale
        step = 128 if k < full else 48
        blocks = [window[j * step : (j + 1) * step] for j in range(k + 1)]
        if k == full:
            blocks = [stretch(block) for block in blocks]
        rhs_ref[:, base : base + 128] = window[(k + 1) * step : (k + 1) * step + 8]
        lane = lax.broadcasted_iota(jnp.int32, (count, LANES), 1)
        line = lax.broadcasted_iota(jnp.int32, (count, LANES), 0)
        pivot = blocks[k] + jnp.where(lane == line, ridge_term, 0.0)
        if k:
            left = jnp.concatenate(blocks[:k], 1)
            known = inverse[:base, :base]
            factor = dot32(left, known, NT)
            drop = dot32(factor, factor, NT)
            coupling = dot32(factor, known)
            if count < LANES:
                drop = jnp.concatenate(
                    [drop, jnp.zeros((count, LANES - count), F32)], 1
                )
            pivot = pivot - drop
        groups = range(16) if k < full else (0, 1, 2, 4, 5, 6)
        lower = block_factor(pivot, groups)
        if k:
            lower = jnp.concatenate([-dot32(lower[:, :count], coupling), lower], 1)
        z_ref[:count] = jnp.sum(
            lower * rhs_ref[:1, : base + 128], 1, keepdims=True
        )
        high, low = split2(lower)
        high_r[:count, : base + 128] = high
        low_r[:count, : base + 128] = low
        if k < full:
            inverse[base : base + count, : base + 128] = lower

    def spread(k):
        count = step_rows(full, k)
        end = 128 * k + count
        last = k == full

        def chunk(i, _):
            at = pl.ds(pl.multiple_of(i * CHUNK, CHUNK), CHUNK)
            part = feats[:end, at]
            value = jnp.dot(
                high_r[:count, :end], part, preferred_element_type=F32
            ) + jnp.dot(low_r[:count, :end], part, preferred_element_type=F32)
            square = (value * value).reshape(count // 8, 8, CHUNK)
            linear = (value * z_ref[:count]).reshape(count // 8, 8, CHUNK)
            square = spread8[:, at] + jnp.sum(square, 0)
            linear = fit8[:, at] + jnp.sum(linear, 0)
            if last:
                spread_ref[:, at] = jnp.sum(square, 0, keepdims=True) / (2 * half)
                fitted = jnp.sum(linear, 0, keepdims=True)
                fitted_ref[:, at] = fitted
                for s in range(CHUNK // LANES):
                    fit[pl.ds(i * (CHUNK // LANES) + s, 1), :] = fitted[
                        :, s * LANES : (s + 1) * LANES
                    ]
            else:
                spread8[:, at] = square
                fit8[:, at] = linear
            return 0

        lax.fori_loop(0, pixels // CHUNK, chunk, 0)

    gram(0)
    z_join(0)
    for k in range(1, steps):
        gram(k)
        z_join(k)
        solve(k - 1)
        spread(k - 1)
    solve(full)
    spread(full)

    high, _ = one_hots(index_ref[...], rows)
    table = jnp.concatenate(split3(fit[...]), 0)
    found = jnp.dot(table, low_ref[...], preferred_element_type=F32)
    found = found[:rows] + (found[rows : 2 * rows] + found[2 * rows :])
    value = jnp.sum(jnp.where(high, found, 0.0), 0, keepdims=True)
    resid_ref[...] = yield_ref[...] - value

    for copy in bulk:
        copy.wait_send()
    for k in range(steps):
        pl.when(has_up)(lambda k=k: z_copy(0, k, up).wait_send())
        pl.when(has_down)(lambda k=k: z_copy(1, k, down).wait_send())
        pl.when(jnp.logical_not(joins))(lambda k=k: core_copy(k).wait_send())
        x_copy(k).wait_send()


def fused(imagery, index, yields, mask):
    half, pixels = imagery.shape[2:]
    full = half // 64
    steps = full + 1
    rows = payload_starts(full)[1]
    size = 128 * steps
    shape = jax.ShapeDtypeStruct((1, pixels), F32)
    anywhere = pl.BlockSpec(memory_space=pl.ANY)
    in_vmem = pl.BlockSpec(memory_space=pltpu.VMEM)
    dma = pltpu.SemaphoreType.DMA
    return pl.pallas_call(
        functools.partial(fused_kernel, lax.axis_size("tiles")),
        out_shape=(shape, shape, shape),
        in_specs=[anywhere] * 4,
        out_specs=(in_vmem,) * 3,
        scratch_shapes=[
            pltpu.VMEM((128 * full + 64, pixels), BF16),
            pltpu.VMEM((2, half, pixels), BF16),
            pltpu.VMEM((2, 16, pixels), BF16),
            pltpu.VMEM((1, pixels), jnp.int32),
            pltpu.VMEM((1, pixels), F32),
            pltpu.VMEM((pixels // LANES, LANES), jnp.int32),
            pltpu.VMEM((16, pixels), BF16),
            pltpu.VMEM((16, pixels), BF16),
            pltpu.VMEM((LANES, pixels), BF16),
            pltpu.VMEM((LANES + 16, size), F32),
            pltpu.VMEM((rows, LANES), F32),
            pltpu.VMEM((rows, LANES), F32),
            pltpu.VMEM((rows, LANES), F32),
            pltpu.VMEM((4, rows, LANES), F32),
            pltpu.VMEM((size, size), F32),
            pltpu.VMEM((LANES, size), BF16),
            pltpu.VMEM((LANES, size), BF16),
            pltpu.VMEM((8, size), F32),
            pltpu.VMEM((LANES, 1), F32),
            pltpu.VMEM((8, pixels), F32),
            pltpu.VMEM((8, pixels), F32),
            pltpu.VMEM((pixels // LANES, LANES), F32),
            dma((4 + steps,)),
            dma((steps + 1,)),
            dma((steps + 1,)),
            dma((2, steps)),
            dma((2, steps)),
            dma((steps,)),
            dma((steps,)),
            dma((steps,)),
            dma((steps,)),
        ],
        compiler_params=pltpu.CompilerParams(
            collective_id=1,
            has_side_effects=True,
            vmem_limit_bytes=56 * 1024 * 1024,
        ),
        name="fused",
    )(imagery, index, yields, mask)


def on_device_fused(imagery, pixel_mask, point_pixel, point_yield):
    pixels = imagery.shape[3]
    mask = pixel_mask.reshape(pixels // LANES, LANES)
    fitted, spread, resid = fused(imagery, point_pixel, point_yield, mask)
    return (fitted[None], spread[None], resid[None])


def solution(mesh):
    features = P(("groups", "tiles"), "cols", "dates", None)
    points = P(("groups", "tiles"), ("cols", "dates"), None)
    sizes = dict(mesh.shape)

    def body(imagery, pixel_mask, point_pixel, point_yield):
        pairs = sizes["cols"] == 2 and sizes["dates"] == 2
        one_tile = imagery.shape[:2] == (1, 2)
        if pairs and one_tile and imagery.shape[2] % 64 == 24:
            run = on_device_fused
        else:
            run = on_device
        return run(imagery, pixel_mask, point_pixel, point_yield)

    return jax.shard_map(
        body,
        mesh=mesh,
        in_specs=(features, points, points, points),
        out_specs=(points, points, points),
        check_vma=False,
    )
```

```python
import functools

import jax
import jax.numpy as jnp
from jax import lax
from jax.experimental import pallas as pl
from jax.experimental.pallas import tpu as pltpu
from jax.sharding import PartitionSpec as P

ridge_term = 0.05
LANES = 128
CHUNK = 512
PIECES = 8
SPAN = 1024
F32 = jnp.float32
BF16 = jnp.bfloat16
NT = (((1,), (1,)), ((), ()))


def split3(x):
    a = x.astype(BF16)
    rest = x - a.astype(F32)
    b = rest.astype(BF16)
    c = (rest - b.astype(F32)).astype(BF16)
    return a, b, c


def one_hots(index, rows):
    points = index.shape[1]
    high = lax.broadcasted_iota(jnp.int32, (rows, points), 0) == index // LANES
    low = lax.broadcasted_iota(jnp.int32, (LANES, points), 0) == index % LANES
    return high, low


def segment_kernel(index_ref, yield_ref, mask_ref, weight_ref, product_ref):
    rows = mask_ref.shape[0]
    high, low = one_hots(index_ref[...], rows)
    low = jnp.where(low, 1.0, 0.0).astype(BF16)
    pieces = [jnp.where(high, 1.0, 0.0).astype(BF16)]
    for piece in split3(yield_ref[...]):
        pieces.append(jnp.where(high, piece.astype(F32), 0.0).astype(BF16))
    sums = lax.dot_general(
        jnp.concatenate(pieces, 0), low, NT, preferred_element_type=F32
    )
    counts = sums[:rows]
    totals = sums[rows : 2 * rows] + sums[2 * rows : 3 * rows] + sums[3 * rows :]
    weight = jnp.where(counts > 0, mask_ref[...].astype(F32), 0.0)
    weight_ref[...] = weight
    product_ref[...] = weight * (totals / jnp.maximum(counts, 1.0))


def bands(width):
    blocks, offset = [], 0
    for i in range(pl.cdiv(width, LANES)):
        height = min(LANES, width - i * LANES)
        for j in range(i + 1):
            blocks.append((i, j, height, offset))
            offset += height
    return blocks, offset


def gram_kernel(feats_ref, weight_ref, product_ref, out_ref, acc):
    width, pixels = feats_ref.shape
    acc[...] = jnp.zeros_like(acc)

    def step(c, _):
        at = pl.multiple_of(c * CHUNK, CHUNK)
        feats = feats_ref[:, pl.ds(at, CHUNK)]
        left = []
        for s in range(CHUNK // LANES):
            row = pl.ds(c * (CHUNK // LANES) + s, 1)
            part = feats[:, s * LANES : (s + 1) * LANES]
            scaled = part * weight_ref[row, :].astype(BF16)
            a, b, d = (p.astype(F32) for p in split3(product_ref[row, :]))
            line = lax.broadcasted_iota(jnp.int32, (16, LANES), 0)
            extra = jnp.where(
                line == 0, a, jnp.where(line == 1, b, jnp.where(line == 2, d, 0.0))
            )
            left.append(jnp.concatenate([scaled, extra.astype(BF16)], 0))
        acc[...] += lax.dot_general(
            jnp.concatenate(left, 1), feats, NT, preferred_element_type=F32
        )
        return 0

    lax.fori_loop(0, pixels // CHUNK, step, 0)
    blocks, offset = bands(width)
    out_ref[...] = jnp.zeros_like(out_ref)
    for i, j, height, at in blocks:
        wide = min(LANES, width - j * LANES)
        out_ref[at : at + height, :wide] = acc[
            i * LANES : i * LANES + height, j * LANES : j * LANES + wide
        ]
    moment = acc[width : width + 1] + acc[width + 1 : width + 2]
    moment = moment + acc[width + 2 : width + 3]
    for j in range(pl.cdiv(width, LANES)):
        wide = min(LANES, width - j * LANES)
        out_ref[offset + j : offset + j + 1, :wide] = moment[
            :, j * LANES : j * LANES + wide
        ]


def small_inverse(p):
    n = len(p)
    for k in range(n):
        d = 1.0 / p[k][k]
        row = [d if j == k else p[k][j] * d for j in range(n)]
        new = []
        for i in range(n):
            if i == k:
                new.append(row)
            else:
                new.append(
                    [
                        -p[i][k] * d if j == k else p[i][j] - p[i][k] * row[j]
                        for j in range(n)
                    ]
                )
        p = new
    return p


def block_inverse(block, pivots, group=8):
    tiles = [block[8 * g : 8 * g + 8] for g in range(LANES // 8)]
    lane = lax.broadcasted_iota(jnp.int32, (8, LANES), 1)
    line = lax.broadcasted_iota(jnp.int32, (8, LANES), 0)
    for k in range(0, pivots, group):
        g, r = divmod(k, 8)
        cols = [
            [
                jnp.broadcast_to(t[:, k + j : k + j + 1], (8, LANES))
                for t in tiles
            ]
            for j in range(group)
        ]
        small = [
            [cols[j][g][r + i : r + i + 1] for j in range(group)]
            for i in range(group)
        ]
        small = small_inverse(small)
        rows = []
        for i in range(group):
            old = tiles[g][r + i : r + i + 1]
            old = jnp.where((lane[:1] >= k) & (lane[:1] < k + group), 0.0, old)
            rows.append(jnp.where(lane[:1] == k + i, 1.0, old))
        new_rows = []
        for i in range(group):
            total = small[i][0] * rows[0]
            for j in range(1, group):
                total = total + small[i][j] * rows[j]
            new_rows.append(jnp.broadcast_to(total, (8, LANES)))
        keep = (lane < k) | (lane >= k + group)
        for t in range(LANES // 8):
            value = jnp.where(keep, tiles[t], 0.0)
            for j in range(group):
                value = value - cols[j][t] * new_rows[j]
            if t == g:
                for i in range(group):
                    value = jnp.where(line == r + i, new_rows[i], value)
            tiles[t] = value
    return jnp.concatenate(tiles, 0)


NN = (((1,), (0,)), ((), ()))


def dot32(a, b, dims=NN):
    return lax.dot_general(
        a, b, dims, precision=lax.Precision.HIGHEST, preferred_element_type=F32
    )


def solve_kernel(
    packed_ref,
    feats_ref,
    index_ref,
    yield_ref,
    fitted_ref,
    spread_ref,
    resid_ref,
    system,
    base,
    high_ref,
    low_ref,
    fit,
):
    width, pixels = feats_ref.shape
    count = pl.cdiv(width, LANES)
    size = count * LANES
    blocks, offset = bands(width)
    scale = 1.0 / pixels
    line = lax.broadcasted_iota(jnp.int32, (LANES, LANES), 0)
    lane = lax.broadcasted_iota(jnp.int32, (LANES, LANES), 1)
    for i, j, height, at in blocks:
        value = packed_ref[at : at + height] * scale
        if height < LANES:
            value = jnp.concatenate(
                [value, jnp.zeros((LANES - height, LANES), F32)], 0
            )
        if i == j:
            diagonal = jnp.where(line < height, ridge_term, 1.0)
            value = value + jnp.where(line == lane, diagonal, 0.0)
        system[i * LANES : (i + 1) * LANES, j * LANES : (j + 1) * LANES] = value
        if i != j:
            system[j * LANES : (j + 1) * LANES, i * LANES : (i + 1) * LANES] = value.T

    base[...] = system[...]
    column = lax.broadcasted_iota(jnp.int32, (LANES, size), 1)
    wide_line = lax.broadcasted_iota(jnp.int32, (LANES, size), 0)

    def eliminate(k, pivots):
        at = k * LANES if isinstance(k, int) else pl.multiple_of(k * LANES, LANES)
        here = pl.ds(at, LANES)
        inverse = block_inverse(system[here, here], pivots)
        inside = (column >= at) & (column < at + LANES)
        unit = jnp.where(column == wide_line + at, 1.0, 0.0)
        right = dot32(inverse, jnp.where(inside, unit, system[here, :]))
        left = system[:, here]
        system[:, here] = jnp.zeros_like(left)
        system[...] -= dot32(left, right)
        system[here, :] = right

    full = width // LANES

    def body(k, _):
        eliminate(k, LANES)
        return 0

    lax.fori_loop(0, full, body, 0)
    if width % LANES:
        eliminate(full, width % LANES)

    rhs = jnp.concatenate(
        [packed_ref[offset + j : offset + j + 1] for j in range(count)], 1
    )
    rhs = jnp.broadcast_to(rhs * scale, (8, size))
    beta = dot32(rhs, system[...])
    beta = beta + dot32(rhs - dot32(beta, base[...]), system[...])
    beta = beta[:1, :width]
    inverse = system[:width, :width]
    upper = inverse.astype(BF16)
    a, b, d = (p.astype(F32) for p in split3(beta))
    row16 = lax.broadcasted_iota(jnp.int32, (16, width), 0)
    extra = jnp.where(row16 == 0, a, jnp.where(row16 == 1, b, jnp.where(row16 == 2, d, 0.0)))
    high_ref[...] = jnp.concatenate([upper, extra.astype(BF16)], 0)
    low_ref[...] = (inverse - upper.astype(F32)).astype(BF16)

    def step(c, _):
        at = pl.multiple_of(c * CHUNK, CHUNK)
        feats = feats_ref[:, pl.ds(at, CHUNK)]
        first = jnp.dot(high_ref[...], feats, preferred_element_type=F32)
        second = jnp.dot(low_ref[...], feats, preferred_element_type=F32)
        total = (first[:width] + second) * feats.astype(F32)
        spread_ref[:, pl.ds(at, CHUNK)] = jnp.sum(total, 0, keepdims=True) / width
        fitted = first[width : width + 1] + (
            first[width + 1 : width + 2] + first[width + 2 : width + 3]
        )
        fitted_ref[:, pl.ds(at, CHUNK)] = fitted
        for s in range(CHUNK // LANES):
            fit[pl.ds(c * (CHUNK // LANES) + s, 1), :] = fitted[
                :, s * LANES : (s + 1) * LANES
            ]
        return 0

    lax.fori_loop(0, pixels // CHUNK, step, 0)

    rows = pixels // LANES
    high, low = one_hots(index_ref[...], rows)
    low = jnp.where(low, 1.0, 0.0).astype(BF16)
    table = jnp.concatenate(split3(fit[...]), 0)
    found = jnp.dot(table, low, preferred_element_type=F32)
    found = found[:rows] + (found[rows : 2 * rows] + found[2 * rows :])
    value = jnp.sum(jnp.where(high, found, 0.0), 0, keepdims=True)
    resid_ref[...] = yield_ref[...] - value


PARAMS = pltpu.CompilerParams(vmem_limit_bytes=48 * 1024 * 1024)


def segments(index, yields, mask):
    shape = jax.ShapeDtypeStruct(mask.shape, F32)
    return pl.pallas_call(
        segment_kernel,
        out_shape=(shape, shape),
        compiler_params=PARAMS,
        cost_estimate=pl.CostEstimate(
            flops=2 * 128 * 128 * index.shape[1],
            bytes_accessed=16 * index.shape[1],
            transcendentals=0,
        ),
        name="segments",
    )(index, yields, mask)


def grams(feats, weight, product):
    width, pixels = feats.shape
    rows = bands(width)[1] + 8 * pl.cdiv(pl.cdiv(width, LANES), 8)
    return pl.pallas_call(
        gram_kernel,
        out_shape=jax.ShapeDtypeStruct((rows, LANES), F32),
        scratch_shapes=[pltpu.VMEM((width + 16, width), F32)],
        compiler_params=PARAMS,
        name="grams",
    )(feats, weight, product)


def solves(packed, feats, index, yields):
    width, pixels = feats.shape
    size = pl.cdiv(width, LANES) * LANES
    shape = jax.ShapeDtypeStruct((1, pixels), F32)
    return pl.pallas_call(
        solve_kernel,
        out_shape=(shape, shape, jax.ShapeDtypeStruct(yields.shape, F32)),
        scratch_shapes=[
            pltpu.VMEM((size, size), F32),
            pltpu.VMEM((size, size), F32),
            pltpu.VMEM((width + 16, width), BF16),
            pltpu.VMEM((width, width), BF16),
            pltpu.VMEM((pixels // LANES, LANES), F32),
        ],
        compiler_params=PARAMS,
        name="solves",
    )(packed, feats, index, yields)


def window_kernel(shape, own_ref, out_ref, landed, middle, send_sem, recv_sem):
    tiles, cols, dates = shape
    row = lax.axis_index("tiles")
    col = lax.axis_index("cols") * dates + lax.axis_index("dates")
    total = own_ref.shape[0]
    step = -(-total // (8 * PIECES)) * 8
    pieces = [pl.ds(at, min(step, total - at)) for at in range(0, total, step)]

    def place(c):
        return {"cols": c // dates, "dates": c % dates}

    links = (
        (row < tiles - 1, lambda: {"tiles": row + 1}, row > 0, lambda: {"tiles": row - 1}),
        (row > 0, lambda: {"tiles": row - 1}, row < tiles - 1, lambda: {"tiles": row + 1}),
        (col < cols * dates - 1, lambda: place(col + 1), col > 0, lambda: place(col - 1)),
        (col > 0, lambda: place(col - 1), col < cols * dates - 1, lambda: place(col + 1)),
    )

    def copy(d, i, source, device):
        return pltpu.make_async_remote_copy(
            src_ref=source.at[pieces[i]],
            dst_ref=landed.at[d, pieces[i]],
            send_sem=send_sem.at[d, i],
            recv_sem=recv_sem.at[d, i],
            device_id=device,
            device_id_type=pl.DeviceIdType.MESH,
        )

    barrier = pltpu.get_barrier_semaphore()
    for there, target, _, _ in links:

        @pl.when(there)
        def _(target=target):
            pl.semaphore_signal(
                barrier, inc=1, device_id=target(), device_id_type=pl.DeviceIdType.MESH
            )

    peers = sum(there.astype(jnp.int32) for there, _, _, _ in links)
    pl.semaphore_wait(barrier, peers)

    def send(d, i, source):
        there, target, _, _ = links[d]

        @pl.when(there)
        def _():
            copy(d, i, source, target()).start()

    def receive(d, i, source, into):
        _, _, there, origin = links[d]

        @pl.when(there)
        def _():
            copy(d, i, source, origin()).wait_recv()
            into[pieces[i]] += 0.5 * landed[d, pieces[i]]

    count = len(pieces)
    for i in range(count):
        send(0, i, own_ref)
        send(1, i, own_ref)
    for i in range(count):
        middle[pieces[i]] = own_ref[pieces[i]]
        receive(0, i, own_ref, middle)
        receive(1, i, own_ref, middle)
        send(2, i, middle)
        send(3, i, middle)
    for i in range(count):
        out_ref[pieces[i]] = middle[pieces[i]]
        receive(2, i, middle, out_ref)
        receive(3, i, middle, out_ref)
    for i in range(count):
        for d in range(4):
            there, target, _, _ = links[d]

            @pl.when(there)
            def _(d=d, i=i, target=target):
                copy(d, i, own_ref if d < 2 else middle, target()).wait_send()


def window(packed):
    shape = tuple(lax.axis_size(name) for name in ("tiles", "cols", "dates"))
    in_vmem = pl.BlockSpec(memory_space=pltpu.VMEM)
    return pl.pallas_call(
        functools.partial(window_kernel, shape),
        out_shape=jax.ShapeDtypeStruct(packed.shape, F32),
        in_specs=[in_vmem],
        out_specs=in_vmem,
        scratch_shapes=[
            pltpu.VMEM((4,) + packed.shape, F32),
            pltpu.VMEM(packed.shape, F32),
            pltpu.SemaphoreType.DMA((4, PIECES)),
            pltpu.SemaphoreType.DMA((4, PIECES)),
        ],
        compiler_params=pltpu.CompilerParams(
            collective_id=0,
            has_side_effects=True,
            vmem_limit_bytes=48 * 1024 * 1024,
        ),
        name="window",
    )(packed)


def on_device(imagery, pixel_mask, point_pixel, point_yield):
    whole = lax.all_to_all(imagery, "dates", split_axis=1, concat_axis=2, tiled=True)
    feats = whole[0, 0]
    pixels = feats.shape[1]
    index = point_pixel[0]
    yields = point_yield[0]
    mask = pixel_mask.reshape(pixels // LANES, LANES)
    weight, product = segments(index, yields, mask)
    packed = grams(feats, weight, product)
    packed = window(packed)
    fitted, spread, resid = solves(packed, feats, index, yields)
    return (fitted[None], spread[None], resid[None])


def step_rows(full, k):
    return 128 if k < full else 64


def payload_rows(full, k):
    return (128 if k < full else 48) * (k + 1) + 8


def payload_starts(full):
    starts, at = [], 0
    for k in range(full + 1):
        starts.append(at)
        at += payload_rows(full, k)
    return starts, at


def squeeze(block):
    return jnp.concatenate([block[0:24], block[32:56]], 0)


def stretch(block):
    gap = jnp.zeros((8, block.shape[1]), block.dtype)
    return jnp.concatenate([block[0:24], gap, block[24:48], gap], 0)


def factor8(small):
    plane = lax.broadcasted_iota(jnp.int32, small.shape, 0)
    line = lax.broadcasted_iota(jnp.int32, small.shape, 1)
    lower = jnp.where(plane == line, 1.0, 0.0)
    pivots = jnp.zeros(small.shape[1:], F32)
    for p in range(8):
        pivot = small[p : p + 1, p : p + 1]
        pivots = jnp.where(line[0] == p, pivot[0], pivots)
        lower = jnp.where((line == p) & (plane < p), small, lower)
        d = 1.0 / pivot
        row = small[:, p : p + 1] * d
        column = small[p : p + 1]
        rest = small - column * row
        rest = jnp.where(plane == p, -column * d, rest)
        row = jnp.where(plane[:, :1] == p, d, row)
        small = jnp.where(line == p, row, rest)
    return small, lower, lax.rsqrt(pivots)


def mix(planes, lines):
    total = planes[0] * lines[0:1]
    for j in range(1, 8):
        total = total + planes[j] * lines[j : j + 1]
    return total


def block_factor(block, groups):
    rows = block.shape[0]
    lane = lax.broadcasted_iota(jnp.int32, (8, LANES), 1)
    line = lax.broadcasted_iota(jnp.int32, (8, LANES), 0)
    result = [jnp.zeros((8, LANES), F32)] * (rows // 8)
    below, first = block, 0
    for g in groups:
        k = 8 * g
        below = below[k - first :]
        top = below[:8]
        small = jnp.stack(
            [jnp.broadcast_to(top[:, k + j : k + j + 1], (8, LANES)) for j in range(8)]
        )
        small, lower, root = factor8(small)
        inside = (lane >= k) & (lane < k + 8)
        top = jnp.where(inside, jnp.where(lane == line + k, 1.0, 0.0), top)
        result[g] = jnp.where(lane < k + 8, mix(lower, top) * root, 0.0)
        below = below[8:]
        first = k + 8
        if below.shape[0]:
            new = mix(small, top)
            cols = [below[:, k + j : k + j + 1] for j in range(8)]
            keep = (lane[:1] < k) | (lane[:1] >= k + 8)
            below = jnp.where(keep, below, 0.0)
            for j in range(8):
                below = below - cols[j] * new[j : j + 1]
    return jnp.concatenate(result, 0)


def split2(x):
    high = x.astype(BF16)
    return high, (x - high.astype(F32)).astype(BF16)


def fused_kernel(
    tiles,
    img,
    index_hbm,
    yield_hbm,
    mask_hbm,
    fitted_ref,
    spread_ref,
    resid_ref,
    feats,
    whole,
    tail,
    index_ref,
    yield_ref,
    mask_ref,
    weight_rows,
    product_rows,
    low_ref,
    acc,
    own,
    middle,
    outgoing,
    landed,
    inverse,
    split_r,
    rhs_ref,
    z_ref,
    fit8,
    spread8,
    fit,
    local_sem,
    bulk_send,
    bulk_recv,
    z_send,
    z_recv,
    core_send,
    core_recv,
    x_send,
    x_recv,
):
    half, pixels = img.shape[2:]
    full = half // 64
    steps = full + 1
    rows = pixels // LANES
    scale = 1.0 / pixels
    starts, _ = payload_starts(full)
    mesh_ids = pl.DeviceIdType.MESH

    z = lax.axis_index("tiles")
    c = lax.axis_index("cols")
    d = lax.axis_index("dates")
    across = {"dates": 1 - d}
    core = {"cols": 1 - c}
    up, down = {"tiles": z + 1}, {"tiles": z - 1}
    has_up, has_down = z < tiles - 1, z > 0
    joins = c == d

    def place(k, s):
        if k < full:
            return pl.multiple_of(128 * k + 64 * s, 16)
        return pl.multiple_of(128 * full + 32 * s, 16)

    height = [64] * full + [16]
    source_at = [64 * k for k in range(steps)]

    local = [
        pltpu.make_async_copy(index_hbm.at[0], index_ref, local_sem.at[0]),
        pltpu.make_async_copy(yield_hbm.at[0], yield_ref, local_sem.at[1]),
        pltpu.make_async_copy(mask_hbm, mask_ref, local_sem.at[2]),
        pltpu.make_async_copy(img.at[0], whole, local_sem.at[3]),
    ]
    for k in range(steps):
        local.append(
            pltpu.make_async_copy(
                img.at[0, d, pl.ds(source_at[k], height[k])],
                feats.at[pl.ds(place(k, d), height[k])],
                local_sem.at[4 + k],
            )
        )
    for copy in local:
        copy.start()

    barrier = pltpu.get_barrier_semaphore()
    peers = ((has_up, up), (has_down, down), (None, core), (None, across))
    for there, target in peers:

        def greet(target=target):
            pl.semaphore_signal(
                barrier, inc=1, device_id=target, device_id_type=mesh_ids
            )

        if there is None:
            greet()
        else:
            pl.when(there)(greet)
    pl.semaphore_wait(barrier, 2 + has_up.astype(jnp.int32) + has_down.astype(jnp.int32))

    bulk = []
    for k in range(steps):
        bulk.append(
            pltpu.make_async_remote_copy(
                src_ref=img.at[0, 1 - d, pl.ds(source_at[k], height[k])],
                dst_ref=feats.at[pl.ds(place(k, d), height[k])],
                send_sem=bulk_send.at[k],
                recv_sem=bulk_recv.at[k],
                device_id=across,
                device_id_type=mesh_ids,
            )
        )
    bulk.append(
        pltpu.make_async_remote_copy(
            src_ref=tail.at[1 - d],
            dst_ref=feats.at[pl.ds(pl.multiple_of(128 * full + 32 * d + 16, 16), 16)],
            send_sem=bulk_send.at[steps],
            recv_sem=bulk_recv.at[steps],
            device_id=across,
            device_id_type=mesh_ids,
        )
    )
    bulk[0].start()
    bulk[1].start()

    for copy in local[:4]:
        copy.wait()
    for s in range(2):
        end = whole[s][half - 8 : half]
        tail[s] = jnp.concatenate([end, jnp.zeros_like(end)], 0)
    feats[pl.ds(pl.multiple_of(128 * full + 32 * d + 16, 16), 16), :] = tail[d]

    high, low = one_hots(index_ref[...], rows)
    low = jnp.where(low, 1.0, 0.0).astype(BF16)
    low_ref[...] = low
    parts = [jnp.where(high, 1.0, 0.0).astype(BF16)]
    for piece in split3(yield_ref[...]):
        parts.append(jnp.where(high, piece.astype(F32), 0.0).astype(BF16))
    sums = lax.dot_general(
        jnp.concatenate(parts, 0), low, NT, preferred_element_type=F32
    )
    counts = sums[:rows]
    totals = sums[rows : 2 * rows] + sums[2 * rows : 3 * rows] + sums[3 * rows :]
    weight = jnp.where(counts > 0, mask_ref[...].astype(F32), 0.0)
    product = weight * (totals / jnp.maximum(counts, 1.0))
    pa, pb, pc = (p.astype(F32) for p in split3(product))
    line16 = lax.broadcasted_iota(jnp.int32, (16, LANES), 0)
    for r in range(rows):
        at = slice(r * LANES, (r + 1) * LANES)
        weight_rows[:, at] = jnp.broadcast_to(weight[r : r + 1], (16, LANES)).astype(BF16)
        extra = jnp.where(
            line16 == 0,
            pa[r : r + 1],
            jnp.where(
                line16 == 1,
                pb[r : r + 1],
                jnp.where(line16 == 2, pc[r : r + 1], 0.0),
            ),
        )
        product_rows[:, at] = extra.astype(BF16)

    acc[...] = jnp.zeros_like(acc)
    inverse[...] = jnp.zeros_like(inverse)
    fit8[...] = jnp.zeros_like(fit8)
    spread8[...] = jnp.zeros_like(spread8)

    def payload(k):
        return pl.ds(starts[k], payload_rows(full, k))

    def z_copy(way, k, target):
        return pltpu.make_async_remote_copy(
            src_ref=own.at[payload(k)],
            dst_ref=landed.at[way, payload(k)],
            send_sem=z_send.at[way, k],
            recv_sem=z_recv.at[way, k],
            device_id=target,
            device_id_type=mesh_ids,
        )

    def core_copy(k):
        return pltpu.make_async_remote_copy(
            src_ref=middle.at[payload(k)],
            dst_ref=landed.at[2, payload(k)],
            send_sem=core_send.at[k],
            recv_sem=core_recv.at[k],
            device_id=core,
            device_id_type=mesh_ids,
        )

    def x_copy(k):
        return pltpu.make_async_remote_copy(
            src_ref=outgoing.at[payload(k)],
            dst_ref=landed.at[3, payload(k)],
            send_sem=x_send.at[k],
            recv_sem=x_recv.at[k],
            device_id=across,
            device_id_type=mesh_ids,
        )

    def gram(k):
        count = step_rows(full, k)
        base, end = 128 * k, 128 * k + count
        local[4 + k].wait()
        bulk[k].wait_recv()
        if k == full:
            bulk[steps].wait_recv()
        wide = count + 16
        acc[:end, :wide] = jnp.zeros((end, wide), F32)

        def chunk(i, _):
            at = pl.ds(pl.multiple_of(i * SPAN, SPAN), SPAN)
            weights = jnp.concatenate([weight_rows[:, at]] * (count // 16), 0)
            left = jnp.concatenate(
                [feats[base:end, at] * weights, product_rows[:, at]], 0
            )
            acc[:end, :wide] += lax.dot_general(
                feats[:end, at], left, NT, preferred_element_type=F32
            )
            return 0

        lax.fori_loop(0, pixels // SPAN, chunk, 0)
        at = starts[k]
        for j in range(k + 1):
            if k < full:
                block = acc[128 * j : 128 * j + 128, :LANES]
            else:
                block = acc[128 * j : 128 * j + 128, :LANES].T
                block = squeeze(block)
            own[at : at + block.shape[0]] = block
            at += block.shape[0]
        moment = acc[base : base + 128, count : count + 1]
        moment = moment + acc[base : base + 128, count + 1 : count + 2]
        moment = moment + acc[base : base + 128, count + 2 : count + 3]
        moment = jnp.broadcast_to(moment, (LANES, LANES)).T
        own[at : at + 8] = moment[:8]
        pl.when(has_up)(lambda: z_copy(0, k, up).start())
        pl.when(has_down)(lambda: z_copy(1, k, down).start())

    def z_join(k):
        at = payload(k)
        middle[at] = own[at]

        @pl.when(has_down)
        def _():
            z_copy(0, k, down).wait_recv()
            middle[at] += 0.5 * landed[0, at]

        @pl.when(has_up)
        def _():
            z_copy(1, k, up).wait_recv()
            middle[at] += 0.5 * landed[1, at]

        @pl.when(jnp.logical_not(joins))
        def _():
            core_copy(k).start()
            outgoing[at] = middle[at]

        @pl.when(joins)
        def _():
            core_copy(k).wait_recv()
            outgoing[at] = middle[at] + landed[2, at]

        x_copy(k).start()
        if k + 2 < steps:
            bulk[k + 2].start()
        if k + 2 == full:
            bulk[steps].start()

    def solve(k):
        at = payload(k)
        x_copy(k).wait_recv()
        count = step_rows(full, k)
        base = 128 * k
        window = (middle[at] + 0.5 * landed[3, at]) * scale
        step = 128 if k < full else 48
        blocks = [window[j * step : (j + 1) * step] for j in range(k + 1)]
        if k == full:
            blocks = [stretch(block) for block in blocks]
        rhs_ref[:, base : base + 128] = window[(k + 1) * step : (k + 1) * step + 8]
        lane = lax.broadcasted_iota(jnp.int32, (count, LANES), 1)
        line = lax.broadcasted_iota(jnp.int32, (count, LANES), 0)
        pivot = blocks[k] + jnp.where(lane == line, ridge_term, 0.0)
        if k:
            known = inverse[:base, :base]
            if k < full:
                raised = dot32(known, jnp.concatenate(blocks[:k], 0))
                factor = jnp.concatenate(
                    [raised[128 * j : 128 * j + 128].T for j in range(k)], 1
                )
                drop = dot32(factor, raised)
            else:
                factor = dot32(jnp.concatenate(blocks[:k], 1), known, NT)
                drop = dot32(factor, factor, NT)
            coupling = dot32(factor, known)
            if count < LANES:
                drop = jnp.concatenate(
                    [drop, jnp.zeros((count, LANES - count), F32)], 1
                )
            pivot = pivot - drop
        groups = range(16) if k < full else (0, 1, 2, 4, 5, 6)
        lower = block_factor(pivot, groups)
        if k:
            lower = jnp.concatenate([-dot32(lower[:, :count], coupling), lower], 1)
        z_ref[:count] = jnp.sum(
            lower * rhs_ref[:1, : base + 128], 1, keepdims=True
        )
        high, low = split2(lower)
        split_r[:count, : base + 128] = high
        split_r[count : 2 * count, : base + 128] = low
        if k < full:
            inverse[base : base + count, : base + 128] = lower

    def spread(k):
        count = step_rows(full, k)
        end = 128 * k + count
        last = k == full

        def chunk(i, _):
            at = pl.ds(pl.multiple_of(i * SPAN, SPAN), SPAN)
            part = feats[:end, at]
            both = jnp.dot(
                split_r[: 2 * count, :end], part, preferred_element_type=F32
            )
            value = both[:count] + both[count:]
            square = (value * value).reshape(count // 8, 8, SPAN)
            linear = (value * z_ref[:count]).reshape(count // 8, 8, SPAN)
            square = spread8[:, at] + jnp.sum(square, 0)
            linear = fit8[:, at] + jnp.sum(linear, 0)
            if last:
                spread_ref[:, at] = jnp.sum(square, 0, keepdims=True) / (2 * half)
                fitted = jnp.sum(linear, 0, keepdims=True)
                fitted_ref[:, at] = fitted
                for s in range(SPAN // LANES):
                    fit[pl.ds(i * (SPAN // LANES) + s, 1), :] = fitted[
                        :, s * LANES : (s + 1) * LANES
                    ]
            else:
                spread8[:, at] = square
                fit8[:, at] = linear
            return 0

        lax.fori_loop(0, pixels // SPAN, chunk, 0)

    gram(0)
    z_join(0)
    for k in range(1, steps - 1):
        gram(k)
        solve(k - 1)
        z_join(k)
        if k < steps - 2:
            spread(k - 1)
    gram(full)
    spread(full - 2)
    z_join(full)
    solve(full - 1)
    spread(full - 1)
    solve(full)
    spread(full)

    high, _ = one_hots(index_ref[...], rows)
    table = jnp.concatenate(split3(fit[...]), 0)
    found = jnp.dot(table, low_ref[...], preferred_element_type=F32)
    found = found[:rows] + (found[rows : 2 * rows] + found[2 * rows :])
    value = jnp.sum(jnp.where(high, found, 0.0), 0, keepdims=True)
    resid_ref[...] = yield_ref[...] - value

    for copy in bulk:
        copy.wait_send()
    for k in range(steps):
        pl.when(has_up)(lambda k=k: z_copy(0, k, up).wait_send())
        pl.when(has_down)(lambda k=k: z_copy(1, k, down).wait_send())
        pl.when(jnp.logical_not(joins))(lambda k=k: core_copy(k).wait_send())
        x_copy(k).wait_send()


def fused(imagery, index, yields, mask):
    half, pixels = imagery.shape[2:]
    full = half // 64
    steps = full + 1
    rows = payload_starts(full)[1]
    size = 128 * steps
    shape = jax.ShapeDtypeStruct((1, pixels), F32)
    anywhere = pl.BlockSpec(memory_space=pl.ANY)
    in_vmem = pl.BlockSpec(memory_space=pltpu.VMEM)
    dma = pltpu.SemaphoreType.DMA
    return pl.pallas_call(
        functools.partial(fused_kernel, lax.axis_size("tiles")),
        out_shape=(shape, shape, shape),
        in_specs=[anywhere] * 4,
        out_specs=(in_vmem,) * 3,
        scratch_shapes=[
            pltpu.VMEM((128 * full + 64, pixels), BF16),
            pltpu.VMEM((2, half, pixels), BF16),
            pltpu.VMEM((2, 16, pixels), BF16),
            pltpu.VMEM((1, pixels), jnp.int32),
            pltpu.VMEM((1, pixels), F32),
            pltpu.VMEM((pixels // LANES, LANES), jnp.int32),
            pltpu.VMEM((16, pixels), BF16),
            pltpu.VMEM((16, pixels), BF16),
            pltpu.VMEM((LANES, pixels), BF16),
            pltpu.VMEM((size, 2 * LANES), F32),
            pltpu.VMEM((rows, LANES), F32),
            pltpu.VMEM((rows, LANES), F32),
            pltpu.VMEM((rows, LANES), F32),
            pltpu.VMEM((4, rows, LANES), F32),
            pltpu.VMEM((size, size), F32),
            pltpu.VMEM((2 * LANES, size), BF16),
            pltpu.VMEM((8, size), F32),
            pltpu.VMEM((LANES, 1), F32),
            pltpu.VMEM((8, pixels), F32),
            pltpu.VMEM((8, pixels), F32),
            pltpu.VMEM((pixels // LANES, LANES), F32),
            dma((4 + steps,)),
            dma((steps + 1,)),
            dma((steps + 1,)),
            dma((2, steps)),
            dma((2, steps)),
            dma((steps,)),
            dma((steps,)),
            dma((steps,)),
            dma((steps,)),
        ],
        compiler_params=pltpu.CompilerParams(
            collective_id=1,
            has_side_effects=True,
            vmem_limit_bytes=56 * 1024 * 1024,
        ),
        name="fused",
    )(imagery, index, yields, mask)


def on_device_fused(imagery, pixel_mask, point_pixel, point_yield):
    pixels = imagery.shape[3]
    mask = pixel_mask.reshape(pixels // LANES, LANES)
    fitted, spread, resid = fused(imagery, point_pixel, point_yield, mask)
    return (fitted[None], spread[None], resid[None])


def solution(mesh):
    features = P(("groups", "tiles"), "cols", "dates", None)
    points = P(("groups", "tiles"), ("cols", "dates"), None)
    sizes = dict(mesh.shape)

    def body(imagery, pixel_mask, point_pixel, point_yield):
        pairs = sizes["cols"] == 2 and sizes["dates"] == 2
        one_tile = imagery.shape[:2] == (1, 2)
        if pairs and one_tile and imagery.shape[2] % 64 == 24:
            run = on_device_fused
        else:
            run = on_device
        return run(imagery, pixel_mask, point_pixel, point_yield)

    return jax.shard_map(
        body,
        mesh=mesh,
        in_specs=(features, points, points, points),
        out_specs=(points, points, points),
        check_vma=False,
    )
```

```python
import functools

import jax
import jax.numpy as jnp
from jax import lax
from jax.experimental import pallas as pl
from jax.experimental.pallas import tpu as pltpu
from jax.sharding import PartitionSpec as P

ridge_term = 0.05
LANES = 128
CHUNK = 512
PIECES = 8
SPAN = 4096
F32 = jnp.float32
BF16 = jnp.bfloat16
NT = (((1,), (1,)), ((), ()))


def split3(x):
    a = x.astype(BF16)
    rest = x - a.astype(F32)
    b = rest.astype(BF16)
    c = (rest - b.astype(F32)).astype(BF16)
    return a, b, c


def one_hots(index, rows):
    points = index.shape[1]
    high = lax.broadcasted_iota(jnp.int32, (rows, points), 0) == index // LANES
    low = lax.broadcasted_iota(jnp.int32, (LANES, points), 0) == index % LANES
    return high, low


def segment_kernel(index_ref, yield_ref, mask_ref, weight_ref, product_ref):
    rows = mask_ref.shape[0]
    high, low = one_hots(index_ref[...], rows)
    low = jnp.where(low, 1.0, 0.0).astype(BF16)
    pieces = [jnp.where(high, 1.0, 0.0).astype(BF16)]
    for piece in split3(yield_ref[...]):
        pieces.append(jnp.where(high, piece.astype(F32), 0.0).astype(BF16))
    sums = lax.dot_general(
        jnp.concatenate(pieces, 0), low, NT, preferred_element_type=F32
    )
    counts = sums[:rows]
    totals = sums[rows : 2 * rows] + sums[2 * rows : 3 * rows] + sums[3 * rows :]
    weight = jnp.where(counts > 0, mask_ref[...].astype(F32), 0.0)
    weight_ref[...] = weight
    product_ref[...] = weight * (totals / jnp.maximum(counts, 1.0))


def bands(width):
    blocks, offset = [], 0
    for i in range(pl.cdiv(width, LANES)):
        height = min(LANES, width - i * LANES)
        for j in range(i + 1):
            blocks.append((i, j, height, offset))
            offset += height
    return blocks, offset


def gram_kernel(feats_ref, weight_ref, product_ref, out_ref, acc):
    width, pixels = feats_ref.shape
    acc[...] = jnp.zeros_like(acc)

    def step(c, _):
        at = pl.multiple_of(c * CHUNK, CHUNK)
        feats = feats_ref[:, pl.ds(at, CHUNK)]
        left = []
        for s in range(CHUNK // LANES):
            row = pl.ds(c * (CHUNK // LANES) + s, 1)
            part = feats[:, s * LANES : (s + 1) * LANES]
            scaled = part * weight_ref[row, :].astype(BF16)
            a, b, d = (p.astype(F32) for p in split3(product_ref[row, :]))
            line = lax.broadcasted_iota(jnp.int32, (16, LANES), 0)
            extra = jnp.where(
                line == 0, a, jnp.where(line == 1, b, jnp.where(line == 2, d, 0.0))
            )
            left.append(jnp.concatenate([scaled, extra.astype(BF16)], 0))
        acc[...] += lax.dot_general(
            jnp.concatenate(left, 1), feats, NT, preferred_element_type=F32
        )
        return 0

    lax.fori_loop(0, pixels // CHUNK, step, 0)
    blocks, offset = bands(width)
    out_ref[...] = jnp.zeros_like(out_ref)
    for i, j, height, at in blocks:
        wide = min(LANES, width - j * LANES)
        out_ref[at : at + height, :wide] = acc[
            i * LANES : i * LANES + height, j * LANES : j * LANES + wide
        ]
    moment = acc[width : width + 1] + acc[width + 1 : width + 2]
    moment = moment + acc[width + 2 : width + 3]
    for j in range(pl.cdiv(width, LANES)):
        wide = min(LANES, width - j * LANES)
        out_ref[offset + j : offset + j + 1, :wide] = moment[
            :, j * LANES : j * LANES + wide
        ]


def small_inverse(p):
    n = len(p)
    for k in range(n):
        d = 1.0 / p[k][k]
        row = [d if j == k else p[k][j] * d for j in range(n)]
        new = []
        for i in range(n):
            if i == k:
                new.append(row)
            else:
                new.append(
                    [
                        -p[i][k] * d if j == k else p[i][j] - p[i][k] * row[j]
                        for j in range(n)
                    ]
                )
        p = new
    return p


def block_inverse(block, pivots, group=8):
    tiles = [block[8 * g : 8 * g + 8] for g in range(LANES // 8)]
    lane = lax.broadcasted_iota(jnp.int32, (8, LANES), 1)
    line = lax.broadcasted_iota(jnp.int32, (8, LANES), 0)
    for k in range(0, pivots, group):
        g, r = divmod(k, 8)
        cols = [
            [
                jnp.broadcast_to(t[:, k + j : k + j + 1], (8, LANES))
                for t in tiles
            ]
            for j in range(group)
        ]
        small = [
            [cols[j][g][r + i : r + i + 1] for j in range(group)]
            for i in range(group)
        ]
        small = small_inverse(small)
        rows = []
        for i in range(group):
            old = tiles[g][r + i : r + i + 1]
            old = jnp.where((lane[:1] >= k) & (lane[:1] < k + group), 0.0, old)
            rows.append(jnp.where(lane[:1] == k + i, 1.0, old))
        new_rows = []
        for i in range(group):
            total = small[i][0] * rows[0]
            for j in range(1, group):
                total = total + small[i][j] * rows[j]
            new_rows.append(jnp.broadcast_to(total, (8, LANES)))
        keep = (lane < k) | (lane >= k + group)
        for t in range(LANES // 8):
            value = jnp.where(keep, tiles[t], 0.0)
            for j in range(group):
                value = value - cols[j][t] * new_rows[j]
            if t == g:
                for i in range(group):
                    value = jnp.where(line == r + i, new_rows[i], value)
            tiles[t] = value
    return jnp.concatenate(tiles, 0)


NN = (((1,), (0,)), ((), ()))


def dot32(a, b, dims=NN):
    return lax.dot_general(
        a, b, dims, precision=lax.Precision.HIGHEST, preferred_element_type=F32
    )


def solve_kernel(
    packed_ref,
    feats_ref,
    index_ref,
    yield_ref,
    fitted_ref,
    spread_ref,
    resid_ref,
    system,
    base,
    high_ref,
    low_ref,
    fit,
):
    width, pixels = feats_ref.shape
    count = pl.cdiv(width, LANES)
    size = count * LANES
    blocks, offset = bands(width)
    scale = 1.0 / pixels
    line = lax.broadcasted_iota(jnp.int32, (LANES, LANES), 0)
    lane = lax.broadcasted_iota(jnp.int32, (LANES, LANES), 1)
    for i, j, height, at in blocks:
        value = packed_ref[at : at + height] * scale
        if height < LANES:
            value = jnp.concatenate(
                [value, jnp.zeros((LANES - height, LANES), F32)], 0
            )
        if i == j:
            diagonal = jnp.where(line < height, ridge_term, 1.0)
            value = value + jnp.where(line == lane, diagonal, 0.0)
        system[i * LANES : (i + 1) * LANES, j * LANES : (j + 1) * LANES] = value
        if i != j:
            system[j * LANES : (j + 1) * LANES, i * LANES : (i + 1) * LANES] = value.T

    base[...] = system[...]
    column = lax.broadcasted_iota(jnp.int32, (LANES, size), 1)
    wide_line = lax.broadcasted_iota(jnp.int32, (LANES, size), 0)

    def eliminate(k, pivots):
        at = k * LANES if isinstance(k, int) else pl.multiple_of(k * LANES, LANES)
        here = pl.ds(at, LANES)
        inverse = block_inverse(system[here, here], pivots)
        inside = (column >= at) & (column < at + LANES)
        unit = jnp.where(column == wide_line + at, 1.0, 0.0)
        right = dot32(inverse, jnp.where(inside, unit, system[here, :]))
        left = system[:, here]
        system[:, here] = jnp.zeros_like(left)
        system[...] -= dot32(left, right)
        system[here, :] = right

    full = width // LANES

    def body(k, _):
        eliminate(k, LANES)
        return 0

    lax.fori_loop(0, full, body, 0)
    if width % LANES:
        eliminate(full, width % LANES)

    rhs = jnp.concatenate(
        [packed_ref[offset + j : offset + j + 1] for j in range(count)], 1
    )
    rhs = jnp.broadcast_to(rhs * scale, (8, size))
    beta = dot32(rhs, system[...])
    beta = beta + dot32(rhs - dot32(beta, base[...]), system[...])
    beta = beta[:1, :width]
    inverse = system[:width, :width]
    upper = inverse.astype(BF16)
    a, b, d = (p.astype(F32) for p in split3(beta))
    row16 = lax.broadcasted_iota(jnp.int32, (16, width), 0)
    extra = jnp.where(row16 == 0, a, jnp.where(row16 == 1, b, jnp.where(row16 == 2, d, 0.0)))
    high_ref[...] = jnp.concatenate([upper, extra.astype(BF16)], 0)
    low_ref[...] = (inverse - upper.astype(F32)).astype(BF16)

    def step(c, _):
        at = pl.multiple_of(c * CHUNK, CHUNK)
        feats = feats_ref[:, pl.ds(at, CHUNK)]
        first = jnp.dot(high_ref[...], feats, preferred_element_type=F32)
        second = jnp.dot(low_ref[...], feats, preferred_element_type=F32)
        total = (first[:width] + second) * feats.astype(F32)
        spread_ref[:, pl.ds(at, CHUNK)] = jnp.sum(total, 0, keepdims=True) / width
        fitted = first[width : width + 1] + (
            first[width + 1 : width + 2] + first[width + 2 : width + 3]
        )
        fitted_ref[:, pl.ds(at, CHUNK)] = fitted
        for s in range(CHUNK // LANES):
            fit[pl.ds(c * (CHUNK // LANES) + s, 1), :] = fitted[
                :, s * LANES : (s + 1) * LANES
            ]
        return 0

    lax.fori_loop(0, pixels // CHUNK, step, 0)

    rows = pixels // LANES
    high, low = one_hots(index_ref[...], rows)
    low = jnp.where(low, 1.0, 0.0).astype(BF16)
    table = jnp.concatenate(split3(fit[...]), 0)
    found = jnp.dot(table, low, preferred_element_type=F32)
    found = found[:rows] + (found[rows : 2 * rows] + found[2 * rows :])
    value = jnp.sum(jnp.where(high, found, 0.0), 0, keepdims=True)
    resid_ref[...] = yield_ref[...] - value


PARAMS = pltpu.CompilerParams(vmem_limit_bytes=48 * 1024 * 1024)


def segments(index, yields, mask):
    shape = jax.ShapeDtypeStruct(mask.shape, F32)
    return pl.pallas_call(
        segment_kernel,
        out_shape=(shape, shape),
        compiler_params=PARAMS,
        cost_estimate=pl.CostEstimate(
            flops=2 * 128 * 128 * index.shape[1],
            bytes_accessed=16 * index.shape[1],
            transcendentals=0,
        ),
        name="segments",
    )(index, yields, mask)


def grams(feats, weight, product):
    width, pixels = feats.shape
    rows = bands(width)[1] + 8 * pl.cdiv(pl.cdiv(width, LANES), 8)
    return pl.pallas_call(
        gram_kernel,
        out_shape=jax.ShapeDtypeStruct((rows, LANES), F32),
        scratch_shapes=[pltpu.VMEM((width + 16, width), F32)],
        compiler_params=PARAMS,
        name="grams",
    )(feats, weight, product)


def solves(packed, feats, index, yields):
    width, pixels = feats.shape
    size = pl.cdiv(width, LANES) * LANES
    shape = jax.ShapeDtypeStruct((1, pixels), F32)
    return pl.pallas_call(
        solve_kernel,
        out_shape=(shape, shape, jax.ShapeDtypeStruct(yields.shape, F32)),
        scratch_shapes=[
            pltpu.VMEM((size, size), F32),
            pltpu.VMEM((size, size), F32),
            pltpu.VMEM((width + 16, width), BF16),
            pltpu.VMEM((width, width), BF16),
            pltpu.VMEM((pixels // LANES, LANES), F32),
        ],
        compiler_params=PARAMS,
        name="solves",
    )(packed, feats, index, yields)


def window_kernel(shape, own_ref, out_ref, landed, middle, send_sem, recv_sem):
    tiles, cols, dates = shape
    row = lax.axis_index("tiles")
    col = lax.axis_index("cols") * dates + lax.axis_index("dates")
    total = own_ref.shape[0]
    step = -(-total // (8 * PIECES)) * 8
    pieces = [pl.ds(at, min(step, total - at)) for at in range(0, total, step)]

    def place(c):
        return {"cols": c // dates, "dates": c % dates}

    links = (
        (row < tiles - 1, lambda: {"tiles": row + 1}, row > 0, lambda: {"tiles": row - 1}),
        (row > 0, lambda: {"tiles": row - 1}, row < tiles - 1, lambda: {"tiles": row + 1}),
        (col < cols * dates - 1, lambda: place(col + 1), col > 0, lambda: place(col - 1)),
        (col > 0, lambda: place(col - 1), col < cols * dates - 1, lambda: place(col + 1)),
    )

    def copy(d, i, source, device):
        return pltpu.make_async_remote_copy(
            src_ref=source.at[pieces[i]],
            dst_ref=landed.at[d, pieces[i]],
            send_sem=send_sem.at[d, i],
            recv_sem=recv_sem.at[d, i],
            device_id=device,
            device_id_type=pl.DeviceIdType.MESH,
        )

    barrier = pltpu.get_barrier_semaphore()
    for there, target, _, _ in links:

        @pl.when(there)
        def _(target=target):
            pl.semaphore_signal(
                barrier, inc=1, device_id=target(), device_id_type=pl.DeviceIdType.MESH
            )

    peers = sum(there.astype(jnp.int32) for there, _, _, _ in links)
    pl.semaphore_wait(barrier, peers)

    def send(d, i, source):
        there, target, _, _ = links[d]

        @pl.when(there)
        def _():
            copy(d, i, source, target()).start()

    def receive(d, i, source, into):
        _, _, there, origin = links[d]

        @pl.when(there)
        def _():
            copy(d, i, source, origin()).wait_recv()
            into[pieces[i]] += 0.5 * landed[d, pieces[i]]

    count = len(pieces)
    for i in range(count):
        send(0, i, own_ref)
        send(1, i, own_ref)
    for i in range(count):
        middle[pieces[i]] = own_ref[pieces[i]]
        receive(0, i, own_ref, middle)
        receive(1, i, own_ref, middle)
        send(2, i, middle)
        send(3, i, middle)
    for i in range(count):
        out_ref[pieces[i]] = middle[pieces[i]]
        receive(2, i, middle, out_ref)
        receive(3, i, middle, out_ref)
    for i in range(count):
        for d in range(4):
            there, target, _, _ = links[d]

            @pl.when(there)
            def _(d=d, i=i, target=target):
                copy(d, i, own_ref if d < 2 else middle, target()).wait_send()


def window(packed):
    shape = tuple(lax.axis_size(name) for name in ("tiles", "cols", "dates"))
    in_vmem = pl.BlockSpec(memory_space=pltpu.VMEM)
    return pl.pallas_call(
        functools.partial(window_kernel, shape),
        out_shape=jax.ShapeDtypeStruct(packed.shape, F32),
        in_specs=[in_vmem],
        out_specs=in_vmem,
        scratch_shapes=[
            pltpu.VMEM((4,) + packed.shape, F32),
            pltpu.VMEM(packed.shape, F32),
            pltpu.SemaphoreType.DMA((4, PIECES)),
            pltpu.SemaphoreType.DMA((4, PIECES)),
        ],
        compiler_params=pltpu.CompilerParams(
            collective_id=0,
            has_side_effects=True,
            vmem_limit_bytes=48 * 1024 * 1024,
        ),
        name="window",
    )(packed)


def on_device(imagery, pixel_mask, point_pixel, point_yield):
    whole = lax.all_to_all(imagery, "dates", split_axis=1, concat_axis=2, tiled=True)
    feats = whole[0, 0]
    pixels = feats.shape[1]
    index = point_pixel[0]
    yields = point_yield[0]
    mask = pixel_mask.reshape(pixels // LANES, LANES)
    weight, product = segments(index, yields, mask)
    packed = grams(feats, weight, product)
    packed = window(packed)
    fitted, spread, resid = solves(packed, feats, index, yields)
    return (fitted[None], spread[None], resid[None])


def step_rows(full, k):
    return 128 if k < full else 64


def payload_rows(full, k):
    return (128 if k < full else 48) * (k + 1) + 8


def payload_starts(full):
    starts, at = [], 0
    for k in range(full + 1):
        starts.append(at)
        at += payload_rows(full, k)
    return starts, at


def squeeze(block):
    return jnp.concatenate([block[0:24], block[32:56]], 0)


def stretch(block):
    gap = jnp.zeros((8, block.shape[1]), block.dtype)
    return jnp.concatenate([block[0:24], gap, block[24:48], gap], 0)


def factor8(small):
    line = lax.broadcasted_iota(jnp.int32, small.shape[1:], 0)
    lower = []
    pivots = jnp.zeros(small.shape[1:], F32)
    for p in range(0, 8, 2):
        one, two = line == p, line == p + 1
        first, second = small[p], small[p + 1]
        a, b, c = first[p : p + 1], second[p : p + 1], second[p + 1 : p + 2]
        det = a * c - b * b
        ra = 1.0 / a
        t = b * ra
        pivots = jnp.where(one, a, jnp.where(two, det * ra, pivots))
        lower = [
            jnp.where(
                one,
                small[j],
                jnp.where(two, small[j] - t * small[j][p : p + 1], lower[j]),
            )
            for j in range(p)
        ]
        lower.append(jnp.where(one, 1.0, jnp.where(two, -t, 0.0)))
        lower.append(jnp.where(two, 1.0, 0.0))
        r = 1.0 / det
        ea, eb, ec = c * r, -b * r, a * r
        left = first * ea + second * eb
        right = first * eb + second * ec
        left = jnp.where(one, -ea, jnp.where(two, -eb, left))
        right = jnp.where(one, -eb, jnp.where(two, -ec, right))
        base = jnp.where((one | two)[None], 0.0, small)
        rest = base - (
            left[None] * small[:, p : p + 1] + right[None] * small[:, p + 1 : p + 2]
        )
        parts = [rest[:p]] if p else []
        parts.append(jnp.stack([-left, -right]))
        if p < 6:
            parts.append(rest[p + 2 :])
        small = jnp.concatenate(parts, 0)
    return small, lower, lax.rsqrt(pivots)


def mix(planes, lines):
    terms = [planes[j] * lines[j : j + 1] for j in range(8)]
    while len(terms) > 1:
        terms = [a + b for a, b in zip(terms[::2], terms[1::2])]
    return terms[0]


def block_factor(block, groups):
    rows = block.shape[0]
    lane = lax.broadcasted_iota(jnp.int32, (8, LANES), 1)
    line = lax.broadcasted_iota(jnp.int32, (8, LANES), 0)
    result = [jnp.zeros((8, LANES), F32)] * (rows // 8)
    below, first = block, 0
    for g in groups:
        k = 8 * g
        below = below[k - first :]
        top = below[:8]
        small = jnp.stack(
            [jnp.broadcast_to(top[:, k + j : k + j + 1], (8, LANES)) for j in range(8)]
        )
        small, lower, root = factor8(small)
        inside = (lane >= k) & (lane < k + 8)
        top = jnp.where(inside, jnp.where(lane == line + k, 1.0, 0.0), top)
        result[g] = jnp.where(lane < k + 8, mix(lower, top) * root, 0.0)
        below = below[8:]
        first = k + 8
        if below.shape[0]:
            new = mix(small, top)
            cols = [below[:, k + j : k + j + 1] for j in range(8)]
            keep = (lane[:1] < k) | (lane[:1] >= k + 8)
            below = jnp.where(keep, below, 0.0)
            for j in range(0, 8, 2):
                below = below - (
                    cols[j] * new[j : j + 1] + cols[j + 1] * new[j + 1 : j + 2]
                )
    return jnp.concatenate(result, 0)


def split2(x):
    high = x.astype(BF16)
    return high, (x - high.astype(F32)).astype(BF16)


def fused_kernel(
    tiles,
    img,
    index_hbm,
    yield_hbm,
    mask_hbm,
    fit,
    spread_ref,
    index_out,
    yield_out,
    feats,
    whole,
    tail,
    tail_in,
    index_ref,
    yield_ref,
    mask_ref,
    weight_rows,
    product_rows,
    acc,
    own,
    middle,
    outgoing,
    landed,
    inverse,
    split_r,
    rhs_ref,
    z_ref,
    fit8,
    spread8,
    local_sem,
    bulk_send,
    bulk_recv,
    z_send,
    z_recv,
    core_send,
    core_recv,
    x_send,
    x_recv,
):
    half, pixels = img.shape[2:]
    full = half // 64
    steps = full + 1
    rows = pixels // LANES
    scale = 1.0 / pixels
    starts, _ = payload_starts(full)
    mesh_ids = pl.DeviceIdType.MESH

    z = lax.axis_index("tiles")
    c = lax.axis_index("cols")
    d = lax.axis_index("dates")
    across = {"dates": 1 - d}
    core = {"cols": 1 - c}
    up, down = {"tiles": z + 1}, {"tiles": z - 1}
    has_up, has_down = z < tiles - 1, z > 0
    joins = c == d

    def place(k, s):
        if k < full:
            return pl.multiple_of(128 * k + 64 * s, 16)
        return pl.multiple_of(128 * full + 32 * s, 16)

    height = [64] * full + [16]
    source_at = [64 * k for k in range(steps)]

    local = [
        pltpu.make_async_copy(index_hbm.at[0], index_ref, local_sem.at[0]),
        pltpu.make_async_copy(yield_hbm.at[0], yield_ref, local_sem.at[1]),
        pltpu.make_async_copy(mask_hbm, mask_ref, local_sem.at[2]),
        pltpu.make_async_copy(img.at[0], whole, local_sem.at[3]),
    ]
    for k in range(steps):
        local.append(
            pltpu.make_async_copy(
                img.at[0, d, pl.ds(source_at[k], height[k])],
                feats.at[pl.ds(place(k, d), height[k])],
                local_sem.at[4 + k],
            )
        )
    for copy in local:
        copy.start()

    barrier = pltpu.get_barrier_semaphore()
    peers = ((has_up, up), (has_down, down), (None, core), (None, across))
    for there, target in peers:

        def greet(target=target):
            pl.semaphore_signal(
                barrier, inc=1, device_id=target, device_id_type=mesh_ids
            )

        if there is None:
            greet()
        else:
            pl.when(there)(greet)
    pl.semaphore_wait(barrier, 2 + has_up.astype(jnp.int32) + has_down.astype(jnp.int32))

    bulk = []
    for k in range(steps):
        bulk.append(
            pltpu.make_async_remote_copy(
                src_ref=img.at[0, 1 - d, pl.ds(source_at[k], height[k])],
                dst_ref=feats.at[pl.ds(place(k, d), height[k])],
                send_sem=bulk_send.at[k],
                recv_sem=bulk_recv.at[k],
                device_id=across,
                device_id_type=mesh_ids,
            )
        )
    bulk.append(
        pltpu.make_async_remote_copy(
            src_ref=tail,
            dst_ref=tail_in,
            send_sem=bulk_send.at[steps],
            recv_sem=bulk_recv.at[steps],
            device_id=across,
            device_id_type=mesh_ids,
        )
    )
    bulk[0].start()
    bulk[1].start()

    for copy in local[:4]:
        copy.wait()
    end = whole[1 - d][half - 8 : half]
    tail[...] = jnp.concatenate([end[:, : pixels // 2], end[:, pixels // 2 :]], 0)

    def put_tail(s, end):
        at = pl.ds(pl.multiple_of(128 * full + 32 * s + 16, 16), 16)
        feats[at, :] = jnp.concatenate([end, jnp.zeros_like(end)], 0)

    put_tail(d, whole[d][half - 8 : half])

    high, low = one_hots(index_ref[...], rows)
    low = jnp.where(low, 1.0, 0.0).astype(BF16)
    index_out[...] = index_ref[...]
    yield_out[...] = yield_ref[...]
    parts = [jnp.where(high, 1.0, 0.0).astype(BF16)]
    for piece in split3(yield_ref[...]):
        parts.append(jnp.where(high, piece.astype(F32), 0.0).astype(BF16))
    sums = lax.dot_general(
        jnp.concatenate(parts, 0), low, NT, preferred_element_type=F32
    )
    counts = sums[:rows]
    totals = sums[rows : 2 * rows] + sums[2 * rows : 3 * rows] + sums[3 * rows :]
    weight = jnp.where(counts > 0, mask_ref[...].astype(F32), 0.0)
    product = weight * (totals / jnp.maximum(counts, 1.0))
    pa, pb, pc = (p.astype(F32) for p in split3(product))
    line16 = lax.broadcasted_iota(jnp.int32, (16, LANES), 0)
    for r in range(rows):
        at = slice(r * LANES, (r + 1) * LANES)
        weight_rows[:, at] = jnp.broadcast_to(weight[r : r + 1], (16, LANES)).astype(BF16)
        extra = jnp.where(
            line16 == 0,
            pa[r : r + 1],
            jnp.where(
                line16 == 1,
                pb[r : r + 1],
                jnp.where(line16 == 2, pc[r : r + 1], 0.0),
            ),
        )
        product_rows[:, at] = extra.astype(BF16)

    acc[...] = jnp.zeros_like(acc)
    inverse[...] = jnp.zeros_like(inverse)
    fit8[...] = jnp.zeros_like(fit8)
    spread8[...] = jnp.zeros_like(spread8)

    def payload(k):
        return pl.ds(starts[k], payload_rows(full, k))

    def z_copy(way, k, target):
        return pltpu.make_async_remote_copy(
            src_ref=own.at[payload(k)],
            dst_ref=landed.at[way, payload(k)],
            send_sem=z_send.at[way, k],
            recv_sem=z_recv.at[way, k],
            device_id=target,
            device_id_type=mesh_ids,
        )

    def core_copy(k):
        return pltpu.make_async_remote_copy(
            src_ref=middle.at[payload(k)],
            dst_ref=landed.at[2, payload(k)],
            send_sem=core_send.at[k],
            recv_sem=core_recv.at[k],
            device_id=core,
            device_id_type=mesh_ids,
        )

    def x_copy(k):
        return pltpu.make_async_remote_copy(
            src_ref=outgoing.at[payload(k)],
            dst_ref=landed.at[3, payload(k)],
            send_sem=x_send.at[k],
            recv_sem=x_recv.at[k],
            device_id=across,
            device_id_type=mesh_ids,
        )

    def gram(k):
        count = step_rows(full, k)
        base, end = 128 * k, 128 * k + count
        local[4 + k].wait()
        bulk[k].wait_recv()
        if k == full:
            bulk[steps].wait_recv()
            folded = tail_in[...]
            put_tail(1 - d, jnp.concatenate([folded[:8], folded[8:]], 1))
        wide = count + 16
        acc[:end, :wide] = jnp.zeros((end, wide), F32)

        def chunk(i, _):
            at = pl.ds(pl.multiple_of(i * SPAN, SPAN), SPAN)
            weights = jnp.concatenate([weight_rows[:, at]] * (count // 16), 0)
            left = jnp.concatenate(
                [feats[base:end, at] * weights, product_rows[:, at]], 0
            )
            acc[:end, :wide] += lax.dot_general(
                feats[:end, at], left, NT, preferred_element_type=F32
            )
            return 0

        lax.fori_loop(0, pixels // SPAN, chunk, 0)
        at = starts[k]
        for j in range(k + 1):
            if k < full:
                block = acc[128 * j : 128 * j + 128, :LANES]
            else:
                block = acc[128 * j : 128 * j + 128, :LANES].T
                block = squeeze(block)
            own[at : at + block.shape[0]] = block
            at += block.shape[0]
        moment = acc[base : base + 128, count : count + 1]
        moment = moment + acc[base : base + 128, count + 1 : count + 2]
        moment = moment + acc[base : base + 128, count + 2 : count + 3]
        moment = jnp.broadcast_to(moment, (LANES, LANES)).T
        own[at : at + 8] = moment[:8]
        pl.when(has_up)(lambda: z_copy(0, k, up).start())
        pl.when(has_down)(lambda: z_copy(1, k, down).start())

    def z_join(k):
        at = payload(k)
        middle[at] = own[at]

        @pl.when(has_down)
        def _():
            z_copy(0, k, down).wait_recv()
            middle[at] += 0.5 * landed[0, at]

        @pl.when(has_up)
        def _():
            z_copy(1, k, up).wait_recv()
            middle[at] += 0.5 * landed[1, at]

        @pl.when(jnp.logical_not(joins))
        def _():
            core_copy(k).start()
            outgoing[at] = middle[at]

        @pl.when(joins)
        def _():
            core_copy(k).wait_recv()
            outgoing[at] = middle[at] + landed[2, at]

        x_copy(k).start()
        if k + 2 < steps:
            bulk[k + 2].start()
        if k + 2 == full:
            bulk[steps].start()

    def solve(k):
        at = payload(k)
        x_copy(k).wait_recv()
        count = step_rows(full, k)
        base = 128 * k
        window = (middle[at] + 0.5 * landed[3, at]) * scale
        step = 128 if k < full else 48
        blocks = [window[j * step : (j + 1) * step] for j in range(k + 1)]
        if k == full:
            blocks = [stretch(block) for block in blocks]
        rhs_ref[:, base : base + 128] = window[(k + 1) * step : (k + 1) * step + 8]
        lane = lax.broadcasted_iota(jnp.int32, (count, LANES), 1)
        line = lax.broadcasted_iota(jnp.int32, (count, LANES), 0)
        pivot = blocks[k] + jnp.where(lane == line, ridge_term, 0.0)
        if k:
            known = inverse[:base, :base]
            if k < full:
                raised = dot32(known, jnp.concatenate(blocks[:k], 0))
                factor = jnp.concatenate(
                    [raised[128 * j : 128 * j + 128].T for j in range(k)], 1
                )
                drop = dot32(factor, raised)
            else:
                factor = dot32(jnp.concatenate(blocks[:k], 1), known, NT)
                drop = dot32(factor, factor, NT)
            coupling = dot32(factor, known)
            if count < LANES:
                drop = jnp.concatenate(
                    [drop, jnp.zeros((count, LANES - count), F32)], 1
                )
            pivot = pivot - drop
        groups = range(16) if k < full else (0, 1, 2, 4, 5, 6)
        lower = block_factor(pivot, groups)
        if k:
            lower = jnp.concatenate([-dot32(lower[:, :count], coupling), lower], 1)
        z_ref[:count] = jnp.sum(
            lower * rhs_ref[:1, : base + 128], 1, keepdims=True
        )
        high, low = split2(lower)
        split_r[:count, : base + 128] = high
        split_r[count : 2 * count, : base + 128] = low
        if k < full:
            inverse[base : base + count, : base + 128] = lower

    def spread(k):
        count = step_rows(full, k)
        end = 128 * k + count
        last = k == full

        def chunk(i, _):
            at = pl.ds(pl.multiple_of(i * SPAN, SPAN), SPAN)
            part = feats[:end, at]
            both = jnp.dot(
                split_r[: 2 * count, :end], part, preferred_element_type=F32
            )
            value = both[:count] + both[count:]
            square = (value * value).reshape(count // 8, 8, SPAN)
            linear = (value * z_ref[:count]).reshape(count // 8, 8, SPAN)
            square = spread8[:, at] + jnp.sum(square, 0)
            linear = fit8[:, at] + jnp.sum(linear, 0)
            if last:
                spread_ref[:, at] = jnp.sum(square, 0, keepdims=True) / (2 * half)
                fitted = jnp.sum(linear, 0, keepdims=True)
                for s in range(SPAN // LANES):
                    fit[pl.ds(i * (SPAN // LANES) + s, 1), :] = fitted[
                        :, s * LANES : (s + 1) * LANES
                    ]
            else:
                spread8[:, at] = square
                fit8[:, at] = linear
            return 0

        lax.fori_loop(0, pixels // SPAN, chunk, 0)

    gram(0)
    z_join(0)
    for k in range(1, steps - 1):
        gram(k)
        solve(k - 1)
        z_join(k)
        if k < steps - 2:
            spread(k - 1)
    gram(full)
    spread(full - 2)
    z_join(full)
    solve(full - 1)
    spread(full - 1)
    solve(full)
    spread(full)

    for copy in bulk:
        copy.wait_send()
    for k in range(steps):
        pl.when(has_up)(lambda k=k: z_copy(0, k, up).wait_send())
        pl.when(has_down)(lambda k=k: z_copy(1, k, down).wait_send())
        pl.when(jnp.logical_not(joins))(lambda k=k: core_copy(k).wait_send())
        x_copy(k).wait_send()


def fused(imagery, index, yields, mask):
    half, pixels = imagery.shape[2:]
    full = half // 64
    steps = full + 1
    rows = payload_starts(full)[1]
    size = 128 * steps
    shape = jax.ShapeDtypeStruct((1, pixels), F32)
    in_hbm = pl.BlockSpec(memory_space=pltpu.HBM)
    in_vmem = pl.BlockSpec(memory_space=pltpu.VMEM)
    dma = pltpu.SemaphoreType.DMA
    return pl.pallas_call(
        functools.partial(fused_kernel, lax.axis_size("tiles")),
        out_shape=(
            pltpu.VMEM((pixels // LANES, LANES), F32),
            pltpu.VMEM((1, pixels), F32),
            pltpu.VMEM((1, pixels), jnp.int32),
            pltpu.VMEM((1, pixels), F32),
        ),
        in_specs=[in_hbm] * 4,
        out_specs=(in_vmem,) * 4,
        scratch_shapes=[
            pltpu.VMEM((128 * full + 64, pixels), BF16),
            pltpu.VMEM((2, half, pixels), BF16),
            pltpu.VMEM((16, pixels // 2), BF16),
            pltpu.VMEM((16, pixels // 2), BF16),
            pltpu.VMEM((1, pixels), jnp.int32),
            pltpu.VMEM((1, pixels), F32),
            pltpu.VMEM((pixels // LANES, LANES), jnp.int32),
            pltpu.VMEM((16, pixels), BF16),
            pltpu.VMEM((16, pixels), BF16),
            pltpu.VMEM((size, 2 * LANES), F32),
            pltpu.VMEM((rows, LANES), F32),
            pltpu.VMEM((rows, LANES), F32),
            pltpu.VMEM((rows, LANES), F32),
            pltpu.VMEM((4, rows, LANES), F32),
            pltpu.VMEM((size, size), F32),
            pltpu.VMEM((2 * LANES, size), BF16),
            pltpu.VMEM((8, size), F32),
            pltpu.VMEM((LANES, 1), F32),
            pltpu.VMEM((8, pixels), F32),
            pltpu.VMEM((8, pixels), F32),
            dma((4 + steps,)),
            dma((steps + 1,)),
            dma((steps + 1,)),
            dma((2, steps)),
            dma((2, steps)),
            dma((steps,)),
            dma((steps,)),
            dma((steps,)),
            dma((steps,)),
        ],
        compiler_params=pltpu.CompilerParams(
            collective_id=1,
            has_side_effects=True,
            vmem_limit_bytes=56 * 1024 * 1024,
        ),
        name="fused",
    )(imagery, index, yields, mask)


def finish_kernel(
    fit_ref, spread_in, index_ref, yield_ref, fitted_ref, spread_ref, resid_ref
):
    rows = fit_ref.shape[0]
    fit = fit_ref[...]
    high, low = one_hots(index_ref[...], rows)
    low = jnp.where(low, 1.0, 0.0).astype(BF16)
    table = jnp.concatenate(split3(fit), 0)
    found = jnp.dot(table, low, preferred_element_type=F32)
    found = found[:rows] + (found[rows : 2 * rows] + found[2 * rows :])
    value = jnp.sum(jnp.where(high, found, 0.0), 0, keepdims=True)
    resid_ref[...] = yield_ref[...] - value
    for r in range(rows):
        fitted_ref[:, r * LANES : (r + 1) * LANES] = fit[r : r + 1]
    spread_ref[...] = spread_in[...]


def finish(fit, spread, index, yields):
    shape = jax.ShapeDtypeStruct(spread.shape, F32)
    return pl.pallas_call(
        finish_kernel,
        out_shape=(shape, shape, shape),
        compiler_params=pltpu.CompilerParams(vmem_limit_bytes=16 * 1024 * 1024),
        name="finish",
    )(fit, spread, index, yields)


def on_device_fused(imagery, pixel_mask, point_pixel, point_yield):
    pixels = imagery.shape[3]
    mask = pixel_mask.reshape(pixels // LANES, LANES)
    fitted, spread, resid = finish(*fused(imagery, point_pixel, point_yield, mask))
    return (fitted[None], spread[None], resid[None])


def solution(mesh):
    features = P(("groups", "tiles"), "cols", "dates", None)
    points = P(("groups", "tiles"), ("cols", "dates"), None)
    sizes = dict(mesh.shape)

    def body(imagery, pixel_mask, point_pixel, point_yield):
        pairs = sizes["cols"] == 2 and sizes["dates"] == 2
        one_tile = imagery.shape[:2] == (1, 2)
        if pairs and one_tile and imagery.shape[2] % 64 == 24:
            run = on_device_fused
        else:
            run = on_device
        return run(imagery, pixel_mask, point_pixel, point_yield)

    return jax.shard_map(
        body,
        mesh=mesh,
        in_specs=(features, points, points, points),
        out_specs=(points, points, points),
        check_vma=False,
    )
```

```python
import functools

import jax
import jax.numpy as jnp
from jax import lax
from jax.experimental import pallas as pl
from jax.experimental.pallas import tpu as pltpu
from jax.sharding import PartitionSpec as P

ridge_term = 0.05
LANES = 128
CHUNK = 512
PIECES = 8
SPAN = 4096
F32 = jnp.float32
BF16 = jnp.bfloat16
NT = (((1,), (1,)), ((), ()))


def split3(x):
    a = x.astype(BF16)
    rest = x - a.astype(F32)
    b = rest.astype(BF16)
    c = (rest - b.astype(F32)).astype(BF16)
    return a, b, c


def one_hots(index, rows):
    points = index.shape[1]
    high = lax.broadcasted_iota(jnp.int32, (rows, points), 0) == index // LANES
    low = lax.broadcasted_iota(jnp.int32, (LANES, points), 0) == index % LANES
    return high, low


def segment_kernel(index_ref, yield_ref, mask_ref, weight_ref, product_ref):
    rows = mask_ref.shape[0]
    high, low = one_hots(index_ref[...], rows)
    low = jnp.where(low, 1.0, 0.0).astype(BF16)
    pieces = [jnp.where(high, 1.0, 0.0).astype(BF16)]
    for piece in split3(yield_ref[...]):
        pieces.append(jnp.where(high, piece.astype(F32), 0.0).astype(BF16))
    sums = lax.dot_general(
        jnp.concatenate(pieces, 0), low, NT, preferred_element_type=F32
    )
    counts = sums[:rows]
    totals = sums[rows : 2 * rows] + sums[2 * rows : 3 * rows] + sums[3 * rows :]
    weight = jnp.where(counts > 0, mask_ref[...].astype(F32), 0.0)
    weight_ref[...] = weight
    product_ref[...] = weight * (totals / jnp.maximum(counts, 1.0))


def bands(width):
    blocks, offset = [], 0
    for i in range(pl.cdiv(width, LANES)):
        height = min(LANES, width - i * LANES)
        for j in range(i + 1):
            blocks.append((i, j, height, offset))
            offset += height
    return blocks, offset


def gram_kernel(feats_ref, weight_ref, product_ref, out_ref, acc):
    width, pixels = feats_ref.shape
    acc[...] = jnp.zeros_like(acc)

    def step(c, _):
        at = pl.multiple_of(c * CHUNK, CHUNK)
        feats = feats_ref[:, pl.ds(at, CHUNK)]
        left = []
        for s in range(CHUNK // LANES):
            row = pl.ds(c * (CHUNK // LANES) + s, 1)
            part = feats[:, s * LANES : (s + 1) * LANES]
            scaled = part * weight_ref[row, :].astype(BF16)
            a, b, d = (p.astype(F32) for p in split3(product_ref[row, :]))
            line = lax.broadcasted_iota(jnp.int32, (16, LANES), 0)
            extra = jnp.where(
                line == 0, a, jnp.where(line == 1, b, jnp.where(line == 2, d, 0.0))
            )
            left.append(jnp.concatenate([scaled, extra.astype(BF16)], 0))
        acc[...] += lax.dot_general(
            jnp.concatenate(left, 1), feats, NT, preferred_element_type=F32
        )
        return 0

    lax.fori_loop(0, pixels // CHUNK, step, 0)
    blocks, offset = bands(width)
    out_ref[...] = jnp.zeros_like(out_ref)
    for i, j, height, at in blocks:
        wide = min(LANES, width - j * LANES)
        out_ref[at : at + height, :wide] = acc[
            i * LANES : i * LANES + height, j * LANES : j * LANES + wide
        ]
    moment = acc[width : width + 1] + acc[width + 1 : width + 2]
    moment = moment + acc[width + 2 : width + 3]
    for j in range(pl.cdiv(width, LANES)):
        wide = min(LANES, width - j * LANES)
        out_ref[offset + j : offset + j + 1, :wide] = moment[
            :, j * LANES : j * LANES + wide
        ]


def small_inverse(p):
    n = len(p)
    for k in range(n):
        d = 1.0 / p[k][k]
        row = [d if j == k else p[k][j] * d for j in range(n)]
        new = []
        for i in range(n):
            if i == k:
                new.append(row)
            else:
                new.append(
                    [
                        -p[i][k] * d if j == k else p[i][j] - p[i][k] * row[j]
                        for j in range(n)
                    ]
                )
        p = new
    return p


def block_inverse(block, pivots, group=8):
    tiles = [block[8 * g : 8 * g + 8] for g in range(LANES // 8)]
    lane = lax.broadcasted_iota(jnp.int32, (8, LANES), 1)
    line = lax.broadcasted_iota(jnp.int32, (8, LANES), 0)
    for k in range(0, pivots, group):
        g, r = divmod(k, 8)
        cols = [
            [
                jnp.broadcast_to(t[:, k + j : k + j + 1], (8, LANES))
                for t in tiles
            ]
            for j in range(group)
        ]
        small = [
            [cols[j][g][r + i : r + i + 1] for j in range(group)]
            for i in range(group)
        ]
        small = small_inverse(small)
        rows = []
        for i in range(group):
            old = tiles[g][r + i : r + i + 1]
            old = jnp.where((lane[:1] >= k) & (lane[:1] < k + group), 0.0, old)
            rows.append(jnp.where(lane[:1] == k + i, 1.0, old))
        new_rows = []
        for i in range(group):
            total = small[i][0] * rows[0]
            for j in range(1, group):
                total = total + small[i][j] * rows[j]
            new_rows.append(jnp.broadcast_to(total, (8, LANES)))
        keep = (lane < k) | (lane >= k + group)
        for t in range(LANES // 8):
            value = jnp.where(keep, tiles[t], 0.0)
            for j in range(group):
                value = value - cols[j][t] * new_rows[j]
            if t == g:
                for i in range(group):
                    value = jnp.where(line == r + i, new_rows[i], value)
            tiles[t] = value
    return jnp.concatenate(tiles, 0)


NN = (((1,), (0,)), ((), ()))


def dot32(a, b, dims=NN):
    return lax.dot_general(
        a, b, dims, precision=lax.Precision.HIGHEST, preferred_element_type=F32
    )


def solve_kernel(
    packed_ref,
    feats_ref,
    index_ref,
    yield_ref,
    fitted_ref,
    spread_ref,
    resid_ref,
    system,
    base,
    high_ref,
    low_ref,
    fit,
):
    width, pixels = feats_ref.shape
    count = pl.cdiv(width, LANES)
    size = count * LANES
    blocks, offset = bands(width)
    scale = 1.0 / pixels
    line = lax.broadcasted_iota(jnp.int32, (LANES, LANES), 0)
    lane = lax.broadcasted_iota(jnp.int32, (LANES, LANES), 1)
    for i, j, height, at in blocks:
        value = packed_ref[at : at + height] * scale
        if height < LANES:
            value = jnp.concatenate(
                [value, jnp.zeros((LANES - height, LANES), F32)], 0
            )
        if i == j:
            diagonal = jnp.where(line < height, ridge_term, 1.0)
            value = value + jnp.where(line == lane, diagonal, 0.0)
        system[i * LANES : (i + 1) * LANES, j * LANES : (j + 1) * LANES] = value
        if i != j:
            system[j * LANES : (j + 1) * LANES, i * LANES : (i + 1) * LANES] = value.T

    base[...] = system[...]
    column = lax.broadcasted_iota(jnp.int32, (LANES, size), 1)
    wide_line = lax.broadcasted_iota(jnp.int32, (LANES, size), 0)

    def eliminate(k, pivots):
        at = k * LANES if isinstance(k, int) else pl.multiple_of(k * LANES, LANES)
        here = pl.ds(at, LANES)
        inverse = block_inverse(system[here, here], pivots)
        inside = (column >= at) & (column < at + LANES)
        unit = jnp.where(column == wide_line + at, 1.0, 0.0)
        right = dot32(inverse, jnp.where(inside, unit, system[here, :]))
        left = system[:, here]
        system[:, here] = jnp.zeros_like(left)
        system[...] -= dot32(left, right)
        system[here, :] = right

    full = width // LANES

    def body(k, _):
        eliminate(k, LANES)
        return 0

    lax.fori_loop(0, full, body, 0)
    if width % LANES:
        eliminate(full, width % LANES)

    rhs = jnp.concatenate(
        [packed_ref[offset + j : offset + j + 1] for j in range(count)], 1
    )
    rhs = jnp.broadcast_to(rhs * scale, (8, size))
    beta = dot32(rhs, system[...])
    beta = beta + dot32(rhs - dot32(beta, base[...]), system[...])
    beta = beta[:1, :width]
    inverse = system[:width, :width]
    upper = inverse.astype(BF16)
    a, b, d = (p.astype(F32) for p in split3(beta))
    row16 = lax.broadcasted_iota(jnp.int32, (16, width), 0)
    extra = jnp.where(row16 == 0, a, jnp.where(row16 == 1, b, jnp.where(row16 == 2, d, 0.0)))
    high_ref[...] = jnp.concatenate([upper, extra.astype(BF16)], 0)
    low_ref[...] = (inverse - upper.astype(F32)).astype(BF16)

    def step(c, _):
        at = pl.multiple_of(c * CHUNK, CHUNK)
        feats = feats_ref[:, pl.ds(at, CHUNK)]
        first = jnp.dot(high_ref[...], feats, preferred_element_type=F32)
        second = jnp.dot(low_ref[...], feats, preferred_element_type=F32)
        total = (first[:width] + second) * feats.astype(F32)
        spread_ref[:, pl.ds(at, CHUNK)] = jnp.sum(total, 0, keepdims=True) / width
        fitted = first[width : width + 1] + (
            first[width + 1 : width + 2] + first[width + 2 : width + 3]
        )
        fitted_ref[:, pl.ds(at, CHUNK)] = fitted
        for s in range(CHUNK // LANES):
            fit[pl.ds(c * (CHUNK // LANES) + s, 1), :] = fitted[
                :, s * LANES : (s + 1) * LANES
            ]
        return 0

    lax.fori_loop(0, pixels // CHUNK, step, 0)

    rows = pixels // LANES
    high, low = one_hots(index_ref[...], rows)
    low = jnp.where(low, 1.0, 0.0).astype(BF16)
    table = jnp.concatenate(split3(fit[...]), 0)
    found = jnp.dot(table, low, preferred_element_type=F32)
    found = found[:rows] + (found[rows : 2 * rows] + found[2 * rows :])
    value = jnp.sum(jnp.where(high, found, 0.0), 0, keepdims=True)
    resid_ref[...] = yield_ref[...] - value


PARAMS = pltpu.CompilerParams(vmem_limit_bytes=48 * 1024 * 1024)


def segments(index, yields, mask):
    shape = jax.ShapeDtypeStruct(mask.shape, F32)
    return pl.pallas_call(
        segment_kernel,
        out_shape=(shape, shape),
        compiler_params=PARAMS,
        cost_estimate=pl.CostEstimate(
            flops=2 * 128 * 128 * index.shape[1],
            bytes_accessed=16 * index.shape[1],
            transcendentals=0,
        ),
        name="segments",
    )(index, yields, mask)


def grams(feats, weight, product):
    width, pixels = feats.shape
    rows = bands(width)[1] + 8 * pl.cdiv(pl.cdiv(width, LANES), 8)
    return pl.pallas_call(
        gram_kernel,
        out_shape=jax.ShapeDtypeStruct((rows, LANES), F32),
        scratch_shapes=[pltpu.VMEM((width + 16, width), F32)],
        compiler_params=PARAMS,
        name="grams",
    )(feats, weight, product)


def solves(packed, feats, index, yields):
    width, pixels = feats.shape
    size = pl.cdiv(width, LANES) * LANES
    shape = jax.ShapeDtypeStruct((1, pixels), F32)
    return pl.pallas_call(
        solve_kernel,
        out_shape=(shape, shape, jax.ShapeDtypeStruct(yields.shape, F32)),
        scratch_shapes=[
            pltpu.VMEM((size, size), F32),
            pltpu.VMEM((size, size), F32),
            pltpu.VMEM((width + 16, width), BF16),
            pltpu.VMEM((width, width), BF16),
            pltpu.VMEM((pixels // LANES, LANES), F32),
        ],
        compiler_params=PARAMS,
        name="solves",
    )(packed, feats, index, yields)


def window_kernel(shape, own_ref, out_ref, landed, middle, send_sem, recv_sem):
    tiles, cols, dates = shape
    row = lax.axis_index("tiles")
    col = lax.axis_index("cols") * dates + lax.axis_index("dates")
    total = own_ref.shape[0]
    step = -(-total // (8 * PIECES)) * 8
    pieces = [pl.ds(at, min(step, total - at)) for at in range(0, total, step)]

    def place(c):
        return {"cols": c // dates, "dates": c % dates}

    links = (
        (row < tiles - 1, lambda: {"tiles": row + 1}, row > 0, lambda: {"tiles": row - 1}),
        (row > 0, lambda: {"tiles": row - 1}, row < tiles - 1, lambda: {"tiles": row + 1}),
        (col < cols * dates - 1, lambda: place(col + 1), col > 0, lambda: place(col - 1)),
        (col > 0, lambda: place(col - 1), col < cols * dates - 1, lambda: place(col + 1)),
    )

    def copy(d, i, source, device):
        return pltpu.make_async_remote_copy(
            src_ref=source.at[pieces[i]],
            dst_ref=landed.at[d, pieces[i]],
            send_sem=send_sem.at[d, i],
            recv_sem=recv_sem.at[d, i],
            device_id=device,
            device_id_type=pl.DeviceIdType.MESH,
        )

    barrier = pltpu.get_barrier_semaphore()
    for there, target, _, _ in links:

        @pl.when(there)
        def _(target=target):
            pl.semaphore_signal(
                barrier, inc=1, device_id=target(), device_id_type=pl.DeviceIdType.MESH
            )

    peers = sum(there.astype(jnp.int32) for there, _, _, _ in links)
    pl.semaphore_wait(barrier, peers)

    def send(d, i, source):
        there, target, _, _ = links[d]

        @pl.when(there)
        def _():
            copy(d, i, source, target()).start()

    def receive(d, i, source, into):
        _, _, there, origin = links[d]

        @pl.when(there)
        def _():
            copy(d, i, source, origin()).wait_recv()
            into[pieces[i]] += 0.5 * landed[d, pieces[i]]

    count = len(pieces)
    for i in range(count):
        send(0, i, own_ref)
        send(1, i, own_ref)
    for i in range(count):
        middle[pieces[i]] = own_ref[pieces[i]]
        receive(0, i, own_ref, middle)
        receive(1, i, own_ref, middle)
        send(2, i, middle)
        send(3, i, middle)
    for i in range(count):
        out_ref[pieces[i]] = middle[pieces[i]]
        receive(2, i, middle, out_ref)
        receive(3, i, middle, out_ref)
    for i in range(count):
        for d in range(4):
            there, target, _, _ = links[d]

            @pl.when(there)
            def _(d=d, i=i, target=target):
                copy(d, i, own_ref if d < 2 else middle, target()).wait_send()


def window(packed):
    shape = tuple(lax.axis_size(name) for name in ("tiles", "cols", "dates"))
    in_vmem = pl.BlockSpec(memory_space=pltpu.VMEM)
    return pl.pallas_call(
        functools.partial(window_kernel, shape),
        out_shape=jax.ShapeDtypeStruct(packed.shape, F32),
        in_specs=[in_vmem],
        out_specs=in_vmem,
        scratch_shapes=[
            pltpu.VMEM((4,) + packed.shape, F32),
            pltpu.VMEM(packed.shape, F32),
            pltpu.SemaphoreType.DMA((4, PIECES)),
            pltpu.SemaphoreType.DMA((4, PIECES)),
        ],
        compiler_params=pltpu.CompilerParams(
            collective_id=0,
            has_side_effects=True,
            vmem_limit_bytes=48 * 1024 * 1024,
        ),
        name="window",
    )(packed)


def on_device(imagery, pixel_mask, point_pixel, point_yield):
    whole = lax.all_to_all(imagery, "dates", split_axis=1, concat_axis=2, tiled=True)
    feats = whole[0, 0]
    pixels = feats.shape[1]
    index = point_pixel[0]
    yields = point_yield[0]
    mask = pixel_mask.reshape(pixels // LANES, LANES)
    weight, product = segments(index, yields, mask)
    packed = grams(feats, weight, product)
    packed = window(packed)
    fitted, spread, resid = solves(packed, feats, index, yields)
    return (fitted[None], spread[None], resid[None])


def step_rows(full, k):
    return 128 if k < full else 64


def payload_rows(full, k):
    return 128 * k + 64 + 8 if k < full else 48 * k + 24 + 8


def payload_starts(full):
    starts, at = [], 0
    for k in range(full + 1):
        starts.append(at)
        at += payload_rows(full, k)
    return starts, at


def pack_square(block):
    top, bottom = block[:64], block[64:]
    lane = lax.broadcasted_iota(jnp.int32, top.shape, 1)
    line = lax.broadcasted_iota(jnp.int32, top.shape, 0)
    packed = jnp.where(line >= lane - 64, bottom, pltpu.roll(top, 64, 1))
    diagonal = jnp.sum(jnp.where(line == lane, top, 0.0), 0, keepdims=True)
    return packed, diagonal


def unpack_square(packed, diagonal):
    lane = lax.broadcasted_iota(jnp.int32, packed.shape, 1)
    line = lax.broadcasted_iota(jnp.int32, packed.shape, 0)
    flipped = jnp.concatenate([packed, packed], 0).T
    corner = jnp.where(line < lane, pltpu.roll(packed, 64, 1), flipped[64:])
    corner = jnp.where(line == lane, diagonal, corner)
    top = jnp.where(lane < 64, corner, flipped[:64])
    bottom = jnp.where(line >= lane - 64, packed, flipped[64:])
    return jnp.concatenate([top, bottom], 0)


def fold(block):
    lane = lax.broadcasted_iota(jnp.int32, (24, LANES), 1)
    return jnp.where(lane < 64, block[:24], pltpu.roll(block[24:], 64, 1))


def unfold(block):
    lane = lax.broadcasted_iota(jnp.int32, (48, LANES), 1)
    both = jnp.concatenate([block, pltpu.roll(block, 64, 1)], 0)
    return jnp.where(lane < 64, both, 0.0)


def squeeze(block):
    return jnp.concatenate([block[0:24], block[32:56]], 0)


def stretch(block):
    gap = jnp.zeros((8, block.shape[1]), block.dtype)
    return jnp.concatenate([block[0:24], gap, block[24:48], gap], 0)


def factor8(small):
    line = lax.broadcasted_iota(jnp.int32, small.shape[1:], 0)
    lower = []
    pivots = jnp.zeros(small.shape[1:], F32)
    for p in range(0, 8, 2):
        one, two = line == p, line == p + 1
        first, second = small[p], small[p + 1]
        a, b, c = first[p : p + 1], second[p : p + 1], second[p + 1 : p + 2]
        det = a * c - b * b
        ra = 1.0 / a
        t = b * ra
        pivots = jnp.where(one, a, jnp.where(two, det * ra, pivots))
        lower = [
            jnp.where(
                one,
                small[j],
                jnp.where(two, small[j] - t * small[j][p : p + 1], lower[j]),
            )
            for j in range(p)
        ]
        lower.append(jnp.where(one, 1.0, jnp.where(two, -t, 0.0)))
        lower.append(jnp.where(two, 1.0, 0.0))
        r = 1.0 / det
        ea, eb, ec = c * r, -b * r, a * r
        left = first * ea + second * eb
        right = first * eb + second * ec
        left = jnp.where(one, -ea, jnp.where(two, -eb, left))
        right = jnp.where(one, -eb, jnp.where(two, -ec, right))
        base = jnp.where((one | two)[None], 0.0, small)
        rest = base - (
            left[None] * small[:, p : p + 1] + right[None] * small[:, p + 1 : p + 2]
        )
        parts = [rest[:p]] if p else []
        parts.append(jnp.stack([-left, -right]))
        if p < 6:
            parts.append(rest[p + 2 :])
        small = jnp.concatenate(parts, 0)
    return small, lower, lax.rsqrt(pivots)


def mix(planes, lines):
    terms = [planes[j] * lines[j : j + 1] for j in range(8)]
    while len(terms) > 1:
        terms = [a + b for a, b in zip(terms[::2], terms[1::2])]
    return terms[0]


def block_factor(block, groups):
    rows = block.shape[0]
    lane = lax.broadcasted_iota(jnp.int32, (8, LANES), 1)
    line = lax.broadcasted_iota(jnp.int32, (8, LANES), 0)
    result = [jnp.zeros((8, LANES), F32)] * (rows // 8)
    below, first = block, 0
    for g in groups:
        k = 8 * g
        below = below[k - first :]
        top = below[:8]
        small = jnp.stack(
            [jnp.broadcast_to(top[:, k + j : k + j + 1], (8, LANES)) for j in range(8)]
        )
        small, lower, root = factor8(small)
        inside = (lane >= k) & (lane < k + 8)
        top = jnp.where(inside, jnp.where(lane == line + k, 1.0, 0.0), top)
        result[g] = jnp.where(lane < k + 8, mix(lower, top) * root, 0.0)
        below = below[8:]
        first = k + 8
        if below.shape[0]:
            new = mix(small, top)
            cols = [below[:, k + j : k + j + 1] for j in range(8)]
            keep = (lane[:1] < k) | (lane[:1] >= k + 8)
            below = jnp.where(keep, below, 0.0)
            for j in range(0, 8, 2):
                below = below - (
                    cols[j] * new[j : j + 1] + cols[j + 1] * new[j + 1 : j + 2]
                )
    return jnp.concatenate(result, 0)


def split2(x):
    high = x.astype(BF16)
    return high, (x - high.astype(F32)).astype(BF16)


def fused_kernel(
    tiles,
    img,
    index_hbm,
    yield_hbm,
    mask_hbm,
    fit,
    spread_ref,
    index_out,
    yield_out,
    feats,
    whole,
    tail,
    tail_in,
    index_ref,
    yield_ref,
    mask_ref,
    weight_rows,
    product_rows,
    acc,
    own,
    middle,
    outgoing,
    landed,
    inverse,
    split_r,
    rhs_ref,
    z_ref,
    fit8,
    spread8,
    local_sem,
    bulk_send,
    bulk_recv,
    z_send,
    z_recv,
    core_send,
    core_recv,
    x_send,
    x_recv,
):
    half, pixels = img.shape[2:]
    full = half // 64
    steps = full + 1
    rows = pixels // LANES
    scale = 1.0 / pixels
    starts, _ = payload_starts(full)
    mesh_ids = pl.DeviceIdType.MESH

    z = lax.axis_index("tiles")
    c = lax.axis_index("cols")
    d = lax.axis_index("dates")
    across = {"dates": 1 - d}
    core = {"cols": 1 - c}
    up, down = {"tiles": z + 1}, {"tiles": z - 1}
    has_up, has_down = z < tiles - 1, z > 0
    joins = c == d

    def place(k, s):
        if k < full:
            return pl.multiple_of(128 * k + 64 * s, 16)
        return pl.multiple_of(128 * full + 32 * s, 16)

    height = [64] * full + [16]
    source_at = [64 * k for k in range(steps)]

    local = [
        pltpu.make_async_copy(index_hbm.at[0], index_ref, local_sem.at[0]),
        pltpu.make_async_copy(yield_hbm.at[0], yield_ref, local_sem.at[1]),
        pltpu.make_async_copy(mask_hbm, mask_ref, local_sem.at[2]),
        pltpu.make_async_copy(img.at[0], whole, local_sem.at[3]),
    ]
    for k in range(steps):
        local.append(
            pltpu.make_async_copy(
                img.at[0, d, pl.ds(source_at[k], height[k])],
                feats.at[pl.ds(place(k, d), height[k])],
                local_sem.at[4 + k],
            )
        )
    for copy in local:
        copy.start()

    barrier = pltpu.get_barrier_semaphore()
    peers = ((has_up, up), (has_down, down), (None, core), (None, across))
    for there, target in peers:

        def greet(target=target):
            pl.semaphore_signal(
                barrier, inc=1, device_id=target, device_id_type=mesh_ids
            )

        if there is None:
            greet()
        else:
            pl.when(there)(greet)
    pl.semaphore_wait(barrier, 2 + has_up.astype(jnp.int32) + has_down.astype(jnp.int32))

    bulk = []
    for k in range(steps):
        bulk.append(
            pltpu.make_async_remote_copy(
                src_ref=img.at[0, 1 - d, pl.ds(source_at[k], height[k])],
                dst_ref=feats.at[pl.ds(place(k, d), height[k])],
                send_sem=bulk_send.at[k],
                recv_sem=bulk_recv.at[k],
                device_id=across,
                device_id_type=mesh_ids,
            )
        )
    bulk.append(
        pltpu.make_async_remote_copy(
            src_ref=tail,
            dst_ref=tail_in,
            send_sem=bulk_send.at[steps],
            recv_sem=bulk_recv.at[steps],
            device_id=across,
            device_id_type=mesh_ids,
        )
    )
    bulk[0].start()
    bulk[1].start()

    for copy in local[:4]:
        copy.wait()
    end = whole[1 - d][half - 8 : half]
    tail[...] = jnp.concatenate([end[:, : pixels // 2], end[:, pixels // 2 :]], 0)

    def put_tail(s, end):
        at = pl.ds(pl.multiple_of(128 * full + 32 * s + 16, 16), 16)
        feats[at, :] = jnp.concatenate([end, jnp.zeros_like(end)], 0)

    put_tail(d, whole[d][half - 8 : half])

    high, low = one_hots(index_ref[...], rows)
    low = jnp.where(low, 1.0, 0.0).astype(BF16)
    index_out[...] = index_ref[...]
    yield_out[...] = yield_ref[...]
    parts = [jnp.where(high, 1.0, 0.0).astype(BF16)]
    for piece in split3(yield_ref[...]):
        parts.append(jnp.where(high, piece.astype(F32), 0.0).astype(BF16))
    sums = lax.dot_general(
        jnp.concatenate(parts, 0), low, NT, preferred_element_type=F32
    )
    counts = sums[:rows]
    totals = sums[rows : 2 * rows] + sums[2 * rows : 3 * rows] + sums[3 * rows :]
    weight = jnp.where(counts > 0, mask_ref[...].astype(F32), 0.0)
    product = weight * (totals / jnp.maximum(counts, 1.0))
    pa, pb, pc = (p.astype(F32) for p in split3(product))
    line16 = lax.broadcasted_iota(jnp.int32, (16, LANES), 0)
    for r in range(rows):
        at = slice(r * LANES, (r + 1) * LANES)
        weight_rows[:, at] = jnp.broadcast_to(weight[r : r + 1], (16, LANES)).astype(BF16)
        extra = jnp.where(
            line16 == 0,
            pa[r : r + 1],
            jnp.where(
                line16 == 1,
                pb[r : r + 1],
                jnp.where(line16 == 2, pc[r : r + 1], 0.0),
            ),
        )
        product_rows[:, at] = extra.astype(BF16)

    acc[...] = jnp.zeros_like(acc)
    inverse[...] = jnp.zeros_like(inverse)
    fit8[...] = jnp.zeros_like(fit8)
    spread8[...] = jnp.zeros_like(spread8)

    def payload(k):
        return pl.ds(starts[k], payload_rows(full, k))

    def z_copy(way, k, target):
        return pltpu.make_async_remote_copy(
            src_ref=own.at[payload(k)],
            dst_ref=landed.at[way, payload(k)],
            send_sem=z_send.at[way, k],
            recv_sem=z_recv.at[way, k],
            device_id=target,
            device_id_type=mesh_ids,
        )

    def core_copy(k):
        return pltpu.make_async_remote_copy(
            src_ref=middle.at[payload(k)],
            dst_ref=landed.at[2, payload(k)],
            send_sem=core_send.at[k],
            recv_sem=core_recv.at[k],
            device_id=core,
            device_id_type=mesh_ids,
        )

    def x_copy(k):
        return pltpu.make_async_remote_copy(
            src_ref=outgoing.at[payload(k)],
            dst_ref=landed.at[3, payload(k)],
            send_sem=x_send.at[k],
            recv_sem=x_recv.at[k],
            device_id=across,
            device_id_type=mesh_ids,
        )

    def gram(k):
        count = step_rows(full, k)
        base, end = 128 * k, 128 * k + count
        local[4 + k].wait()
        bulk[k].wait_recv()
        if k == full:
            bulk[steps].wait_recv()
            folded = tail_in[...]
            put_tail(1 - d, jnp.concatenate([folded[:8], folded[8:]], 1))
        wide = count + 16
        acc[:end, :wide] = jnp.zeros((end, wide), F32)

        def chunk(i, _):
            at = pl.ds(pl.multiple_of(i * SPAN, SPAN), SPAN)
            weights = jnp.concatenate([weight_rows[:, at]] * (count // 16), 0)
            left = jnp.concatenate(
                [feats[base:end, at] * weights, product_rows[:, at]], 0
            )
            acc[:end, :wide] += lax.dot_general(
                feats[:end, at], left, NT, preferred_element_type=F32
            )
            return 0

        lax.fori_loop(0, pixels // SPAN, chunk, 0)
        at = starts[k]
        diagonal = jnp.zeros((1, LANES), F32)
        for j in range(k + 1):
            block = acc[128 * j : 128 * j + 128, :LANES]
            if k == full:
                block = squeeze(block.T)
            if j == k and k < full:
                block, diagonal = pack_square(block)
            if j == k and k == full:
                block = fold(block)
            own[at : at + block.shape[0]] = block
            at += block.shape[0]
        moment = acc[base : base + 128, count : count + 1]
        moment = moment + acc[base : base + 128, count + 1 : count + 2]
        moment = moment + acc[base : base + 128, count + 2 : count + 3]
        moment = jnp.broadcast_to(moment, (LANES, LANES)).T
        line8 = lax.broadcasted_iota(jnp.int32, (8, LANES), 0)
        own[at : at + 8] = jnp.where(line8 == 0, moment[:8], diagonal)
        pl.when(has_up)(lambda: z_copy(0, k, up).start())
        pl.when(has_down)(lambda: z_copy(1, k, down).start())

    def z_join(k):
        at = payload(k)
        middle[at] = own[at]

        @pl.when(has_down)
        def _():
            z_copy(0, k, down).wait_recv()
            middle[at] += 0.5 * landed[0, at]

        @pl.when(has_up)
        def _():
            z_copy(1, k, up).wait_recv()
            middle[at] += 0.5 * landed[1, at]

        @pl.when(jnp.logical_not(joins))
        def _():
            core_copy(k).start()
            outgoing[at] = middle[at]

        @pl.when(joins)
        def _():
            core_copy(k).wait_recv()
            outgoing[at] = middle[at] + landed[2, at]

        x_copy(k).start()
        if k + 2 < steps:
            bulk[k + 2].start()
        if k + 2 == full:
            bulk[steps].start()

    def solve(k):
        at = payload(k)
        x_copy(k).wait_recv()
        count = step_rows(full, k)
        base = 128 * k
        window = (middle[at] + 0.5 * landed[3, at]) * scale
        step = 128 if k < full else 48
        blocks = [window[j * step : (j + 1) * step] for j in range(k)]
        ends = window[payload_rows(full, k) - 8 :]
        rhs_ref[:, base : base + 128] = ends
        square = window[k * step : payload_rows(full, k) - 8]
        if k < full:
            blocks.append(unpack_square(square, ends[1:2]))
        else:
            blocks.append(unfold(square))
            blocks = [stretch(block) for block in blocks]
        lane = lax.broadcasted_iota(jnp.int32, (count, LANES), 1)
        line = lax.broadcasted_iota(jnp.int32, (count, LANES), 0)
        pivot = blocks[k] + jnp.where(lane == line, ridge_term, 0.0)
        if k:
            known = inverse[:base, :base]
            if k < full:
                raised = dot32(known, jnp.concatenate(blocks[:k], 0))
                factor = jnp.concatenate(
                    [raised[128 * j : 128 * j + 128].T for j in range(k)], 1
                )
                drop = dot32(factor, raised)
            else:
                factor = dot32(jnp.concatenate(blocks[:k], 1), known, NT)
                drop = dot32(factor, factor, NT)
            coupling = dot32(factor, known)
            if count < LANES:
                drop = jnp.concatenate(
                    [drop, jnp.zeros((count, LANES - count), F32)], 1
                )
            pivot = pivot - drop
        groups = range(16) if k < full else (0, 1, 2, 4, 5, 6)
        lower = block_factor(pivot, groups)
        if k:
            lower = jnp.concatenate([-dot32(lower[:, :count], coupling), lower], 1)
        z_ref[:count] = jnp.sum(
            lower * rhs_ref[:1, : base + 128], 1, keepdims=True
        )
        high, low = split2(lower)
        split_r[:count, : base + 128] = high
        split_r[count : 2 * count, : base + 128] = low
        if k < full:
            inverse[base : base + count, : base + 128] = lower

    def spread(k):
        count = step_rows(full, k)
        end = 128 * k + count
        last = k == full

        def chunk(i, _):
            at = pl.ds(pl.multiple_of(i * SPAN, SPAN), SPAN)
            part = feats[:end, at]
            both = jnp.dot(
                split_r[: 2 * count, :end], part, preferred_element_type=F32
            )
            value = both[:count] + both[count:]
            square = (value * value).reshape(count // 8, 8, SPAN)
            linear = (value * z_ref[:count]).reshape(count // 8, 8, SPAN)
            square = spread8[:, at] + jnp.sum(square, 0)
            linear = fit8[:, at] + jnp.sum(linear, 0)
            if last:
                spread_ref[:, at] = jnp.sum(square, 0, keepdims=True) / (2 * half)
                fitted = jnp.sum(linear, 0, keepdims=True)
                for s in range(SPAN // LANES):
                    fit[pl.ds(i * (SPAN // LANES) + s, 1), :] = fitted[
                        :, s * LANES : (s + 1) * LANES
                    ]
            else:
                spread8[:, at] = square
                fit8[:, at] = linear
            return 0

        lax.fori_loop(0, pixels // SPAN, chunk, 0)

    gram(0)
    z_join(0)
    for k in range(1, steps - 1):
        gram(k)
        solve(k - 1)
        z_join(k)
        if k < steps - 2:
            spread(k - 1)
    gram(full)
    spread(full - 2)
    z_join(full)
    solve(full - 1)
    spread(full - 1)
    solve(full)
    spread(full)

    for copy in bulk:
        copy.wait_send()
    for k in range(steps):
        pl.when(has_up)(lambda k=k: z_copy(0, k, up).wait_send())
        pl.when(has_down)(lambda k=k: z_copy(1, k, down).wait_send())
        pl.when(jnp.logical_not(joins))(lambda k=k: core_copy(k).wait_send())
        x_copy(k).wait_send()


def fused(imagery, index, yields, mask):
    half, pixels = imagery.shape[2:]
    full = half // 64
    steps = full + 1
    rows = payload_starts(full)[1]
    size = 128 * steps
    shape = jax.ShapeDtypeStruct((1, pixels), F32)
    in_hbm = pl.BlockSpec(memory_space=pltpu.HBM)
    in_vmem = pl.BlockSpec(memory_space=pltpu.VMEM)
    dma = pltpu.SemaphoreType.DMA
    return pl.pallas_call(
        functools.partial(fused_kernel, lax.axis_size("tiles")),
        out_shape=(
            pltpu.VMEM((pixels // LANES, LANES), F32),
            pltpu.VMEM((1, pixels), F32),
            pltpu.VMEM((1, pixels), jnp.int32),
            pltpu.VMEM((1, pixels), F32),
        ),
        in_specs=[in_hbm] * 4,
        out_specs=(in_vmem,) * 4,
        scratch_shapes=[
            pltpu.VMEM((128 * full + 64, pixels), BF16),
            pltpu.VMEM((2, half, pixels), BF16),
            pltpu.VMEM((16, pixels // 2), BF16),
            pltpu.VMEM((16, pixels // 2), BF16),
            pltpu.VMEM((1, pixels), jnp.int32),
            pltpu.VMEM((1, pixels), F32),
            pltpu.VMEM((pixels // LANES, LANES), jnp.int32),
            pltpu.VMEM((16, pixels), BF16),
            pltpu.VMEM((16, pixels), BF16),
            pltpu.VMEM((size, 2 * LANES), F32),
            pltpu.VMEM((rows, LANES), F32),
            pltpu.VMEM((rows, LANES), F32),
            pltpu.VMEM((rows, LANES), F32),
            pltpu.VMEM((4, rows, LANES), F32),
            pltpu.VMEM((size, size), F32),
            pltpu.VMEM((2 * LANES, size), BF16),
            pltpu.VMEM((8, size), F32),
            pltpu.VMEM((LANES, 1), F32),
            pltpu.VMEM((8, pixels), F32),
            pltpu.VMEM((8, pixels), F32),
            dma((4 + steps,)),
            dma((steps + 1,)),
            dma((steps + 1,)),
            dma((2, steps)),
            dma((2, steps)),
            dma((steps,)),
            dma((steps,)),
            dma((steps,)),
            dma((steps,)),
        ],
        compiler_params=pltpu.CompilerParams(
            collective_id=1,
            has_side_effects=True,
            vmem_limit_bytes=56 * 1024 * 1024,
        ),
        name="fused",
    )(imagery, index, yields, mask)


def finish_kernel(
    fit_ref, spread_in, index_ref, yield_ref, fitted_ref, spread_ref, resid_ref
):
    rows = fit_ref.shape[0]
    fit = fit_ref[...]
    high, low = one_hots(index_ref[...], rows)
    low = jnp.where(low, 1.0, 0.0).astype(BF16)
    table = jnp.concatenate(split3(fit), 0)
    found = jnp.dot(table, low, preferred_element_type=F32)
    found = found[:rows] + (found[rows : 2 * rows] + found[2 * rows :])
    value = jnp.sum(jnp.where(high, found, 0.0), 0, keepdims=True)
    resid_ref[...] = yield_ref[...] - value
    for r in range(rows):
        fitted_ref[:, r * LANES : (r + 1) * LANES] = fit[r : r + 1]
    spread_ref[...] = spread_in[...]


def finish(fit, spread, index, yields):
    shape = jax.ShapeDtypeStruct(spread.shape, F32)
    return pl.pallas_call(
        finish_kernel,
        out_shape=(shape, shape, shape),
        compiler_params=pltpu.CompilerParams(vmem_limit_bytes=16 * 1024 * 1024),
        name="finish",
    )(fit, spread, index, yields)


def on_device_fused(imagery, pixel_mask, point_pixel, point_yield):
    pixels = imagery.shape[3]
    mask = pixel_mask.reshape(pixels // LANES, LANES)
    fitted, spread, resid = finish(*fused(imagery, point_pixel, point_yield, mask))
    return (fitted[None], spread[None], resid[None])


def solution(mesh):
    features = P(("groups", "tiles"), "cols", "dates", None)
    points = P(("groups", "tiles"), ("cols", "dates"), None)
    sizes = dict(mesh.shape)

    def body(imagery, pixel_mask, point_pixel, point_yield):
        pairs = sizes["cols"] == 2 and sizes["dates"] == 2
        one_tile = imagery.shape[:2] == (1, 2)
        if pairs and one_tile and imagery.shape[2] % 64 == 24:
            run = on_device_fused
        else:
            run = on_device
        return run(imagery, pixel_mask, point_pixel, point_yield)

    return jax.shard_map(
        body,
        mesh=mesh,
        in_specs=(features, points, points, points),
        out_specs=(points, points, points),
        check_vma=False,
    )
```

```python
import functools

import jax
import jax.numpy as jnp
from jax import lax
from jax.experimental import pallas as pl
from jax.experimental.pallas import tpu as pltpu
from jax.sharding import PartitionSpec as P

ridge_term = 0.05
LANES = 128
CHUNK = 512
PIECES = 8
SPAN = 4096
F32 = jnp.float32
BF16 = jnp.bfloat16
NT = (((1,), (1,)), ((), ()))


def split3(x):
    a = x.astype(BF16)
    rest = x - a.astype(F32)
    b = rest.astype(BF16)
    c = (rest - b.astype(F32)).astype(BF16)
    return a, b, c


def one_hots(index, rows):
    points = index.shape[1]
    high = lax.broadcasted_iota(jnp.int32, (rows, points), 0) == index // LANES
    low = lax.broadcasted_iota(jnp.int32, (LANES, points), 0) == index % LANES
    return high, low


def segment_kernel(index_ref, yield_ref, mask_ref, weight_ref, product_ref):
    rows = mask_ref.shape[0]
    high, low = one_hots(index_ref[...], rows)
    low = jnp.where(low, 1.0, 0.0).astype(BF16)
    pieces = [jnp.where(high, 1.0, 0.0).astype(BF16)]
    for piece in split3(yield_ref[...]):
        pieces.append(jnp.where(high, piece.astype(F32), 0.0).astype(BF16))
    sums = lax.dot_general(
        jnp.concatenate(pieces, 0), low, NT, preferred_element_type=F32
    )
    counts = sums[:rows]
    totals = sums[rows : 2 * rows] + sums[2 * rows : 3 * rows] + sums[3 * rows :]
    weight = jnp.where(counts > 0, mask_ref[...].astype(F32), 0.0)
    weight_ref[...] = weight
    product_ref[...] = weight * (totals / jnp.maximum(counts, 1.0))


def bands(width):
    blocks, offset = [], 0
    for i in range(pl.cdiv(width, LANES)):
        height = min(LANES, width - i * LANES)
        for j in range(i + 1):
            blocks.append((i, j, height, offset))
            offset += height
    return blocks, offset


def gram_kernel(feats_ref, weight_ref, product_ref, out_ref, acc):
    width, pixels = feats_ref.shape
    acc[...] = jnp.zeros_like(acc)

    def step(c, _):
        at = pl.multiple_of(c * CHUNK, CHUNK)
        feats = feats_ref[:, pl.ds(at, CHUNK)]
        left = []
        for s in range(CHUNK // LANES):
            row = pl.ds(c * (CHUNK // LANES) + s, 1)
            part = feats[:, s * LANES : (s + 1) * LANES]
            scaled = part * weight_ref[row, :].astype(BF16)
            a, b, d = (p.astype(F32) for p in split3(product_ref[row, :]))
            line = lax.broadcasted_iota(jnp.int32, (16, LANES), 0)
            extra = jnp.where(
                line == 0, a, jnp.where(line == 1, b, jnp.where(line == 2, d, 0.0))
            )
            left.append(jnp.concatenate([scaled, extra.astype(BF16)], 0))
        acc[...] += lax.dot_general(
            jnp.concatenate(left, 1), feats, NT, preferred_element_type=F32
        )
        return 0

    lax.fori_loop(0, pixels // CHUNK, step, 0)
    blocks, offset = bands(width)
    out_ref[...] = jnp.zeros_like(out_ref)
    for i, j, height, at in blocks:
        wide = min(LANES, width - j * LANES)
        out_ref[at : at + height, :wide] = acc[
            i * LANES : i * LANES + height, j * LANES : j * LANES + wide
        ]
    moment = acc[width : width + 1] + acc[width + 1 : width + 2]
    moment = moment + acc[width + 2 : width + 3]
    for j in range(pl.cdiv(width, LANES)):
        wide = min(LANES, width - j * LANES)
        out_ref[offset + j : offset + j + 1, :wide] = moment[
            :, j * LANES : j * LANES + wide
        ]


def small_inverse(p):
    n = len(p)
    for k in range(n):
        d = 1.0 / p[k][k]
        row = [d if j == k else p[k][j] * d for j in range(n)]
        new = []
        for i in range(n):
            if i == k:
                new.append(row)
            else:
                new.append(
                    [
                        -p[i][k] * d if j == k else p[i][j] - p[i][k] * row[j]
                        for j in range(n)
                    ]
                )
        p = new
    return p


def block_inverse(block, pivots, group=8):
    tiles = [block[8 * g : 8 * g + 8] for g in range(LANES // 8)]
    lane = lax.broadcasted_iota(jnp.int32, (8, LANES), 1)
    line = lax.broadcasted_iota(jnp.int32, (8, LANES), 0)
    for k in range(0, pivots, group):
        g, r = divmod(k, 8)
        cols = [
            [
                jnp.broadcast_to(t[:, k + j : k + j + 1], (8, LANES))
                for t in tiles
            ]
            for j in range(group)
        ]
        small = [
            [cols[j][g][r + i : r + i + 1] for j in range(group)]
            for i in range(group)
        ]
        small = small_inverse(small)
        rows = []
        for i in range(group):
            old = tiles[g][r + i : r + i + 1]
            old = jnp.where((lane[:1] >= k) & (lane[:1] < k + group), 0.0, old)
            rows.append(jnp.where(lane[:1] == k + i, 1.0, old))
        new_rows = []
        for i in range(group):
            total = small[i][0] * rows[0]
            for j in range(1, group):
                total = total + small[i][j] * rows[j]
            new_rows.append(jnp.broadcast_to(total, (8, LANES)))
        keep = (lane < k) | (lane >= k + group)
        for t in range(LANES // 8):
            value = jnp.where(keep, tiles[t], 0.0)
            for j in range(group):
                value = value - cols[j][t] * new_rows[j]
            if t == g:
                for i in range(group):
                    value = jnp.where(line == r + i, new_rows[i], value)
            tiles[t] = value
    return jnp.concatenate(tiles, 0)


NN = (((1,), (0,)), ((), ()))


def dot32(a, b, dims=NN):
    return lax.dot_general(
        a, b, dims, precision=lax.Precision.HIGHEST, preferred_element_type=F32
    )


def solve_kernel(
    packed_ref,
    feats_ref,
    index_ref,
    yield_ref,
    fitted_ref,
    spread_ref,
    resid_ref,
    system,
    base,
    high_ref,
    low_ref,
    fit,
):
    width, pixels = feats_ref.shape
    count = pl.cdiv(width, LANES)
    size = count * LANES
    blocks, offset = bands(width)
    scale = 1.0 / pixels
    line = lax.broadcasted_iota(jnp.int32, (LANES, LANES), 0)
    lane = lax.broadcasted_iota(jnp.int32, (LANES, LANES), 1)
    for i, j, height, at in blocks:
        value = packed_ref[at : at + height] * scale
        if height < LANES:
            value = jnp.concatenate(
                [value, jnp.zeros((LANES - height, LANES), F32)], 0
            )
        if i == j:
            diagonal = jnp.where(line < height, ridge_term, 1.0)
            value = value + jnp.where(line == lane, diagonal, 0.0)
        system[i * LANES : (i + 1) * LANES, j * LANES : (j + 1) * LANES] = value
        if i != j:
            system[j * LANES : (j + 1) * LANES, i * LANES : (i + 1) * LANES] = value.T

    base[...] = system[...]
    column = lax.broadcasted_iota(jnp.int32, (LANES, size), 1)
    wide_line = lax.broadcasted_iota(jnp.int32, (LANES, size), 0)

    def eliminate(k, pivots):
        at = k * LANES if isinstance(k, int) else pl.multiple_of(k * LANES, LANES)
        here = pl.ds(at, LANES)
        inverse = block_inverse(system[here, here], pivots)
        inside = (column >= at) & (column < at + LANES)
        unit = jnp.where(column == wide_line + at, 1.0, 0.0)
        right = dot32(inverse, jnp.where(inside, unit, system[here, :]))
        left = system[:, here]
        system[:, here] = jnp.zeros_like(left)
        system[...] -= dot32(left, right)
        system[here, :] = right

    full = width // LANES

    def body(k, _):
        eliminate(k, LANES)
        return 0

    lax.fori_loop(0, full, body, 0)
    if width % LANES:
        eliminate(full, width % LANES)

    rhs = jnp.concatenate(
        [packed_ref[offset + j : offset + j + 1] for j in range(count)], 1
    )
    rhs = jnp.broadcast_to(rhs * scale, (8, size))
    beta = dot32(rhs, system[...])
    beta = beta + dot32(rhs - dot32(beta, base[...]), system[...])
    beta = beta[:1, :width]
    inverse = system[:width, :width]
    upper = inverse.astype(BF16)
    a, b, d = (p.astype(F32) for p in split3(beta))
    row16 = lax.broadcasted_iota(jnp.int32, (16, width), 0)
    extra = jnp.where(row16 == 0, a, jnp.where(row16 == 1, b, jnp.where(row16 == 2, d, 0.0)))
    high_ref[...] = jnp.concatenate([upper, extra.astype(BF16)], 0)
    low_ref[...] = (inverse - upper.astype(F32)).astype(BF16)

    def step(c, _):
        at = pl.multiple_of(c * CHUNK, CHUNK)
        feats = feats_ref[:, pl.ds(at, CHUNK)]
        first = jnp.dot(high_ref[...], feats, preferred_element_type=F32)
        second = jnp.dot(low_ref[...], feats, preferred_element_type=F32)
        total = (first[:width] + second) * feats.astype(F32)
        spread_ref[:, pl.ds(at, CHUNK)] = jnp.sum(total, 0, keepdims=True) / width
        fitted = first[width : width + 1] + (
            first[width + 1 : width + 2] + first[width + 2 : width + 3]
        )
        fitted_ref[:, pl.ds(at, CHUNK)] = fitted
        for s in range(CHUNK // LANES):
            fit[pl.ds(c * (CHUNK // LANES) + s, 1), :] = fitted[
                :, s * LANES : (s + 1) * LANES
            ]
        return 0

    lax.fori_loop(0, pixels // CHUNK, step, 0)

    rows = pixels // LANES
    high, low = one_hots(index_ref[...], rows)
    low = jnp.where(low, 1.0, 0.0).astype(BF16)
    table = jnp.concatenate(split3(fit[...]), 0)
    found = jnp.dot(table, low, preferred_element_type=F32)
    found = found[:rows] + (found[rows : 2 * rows] + found[2 * rows :])
    value = jnp.sum(jnp.where(high, found, 0.0), 0, keepdims=True)
    resid_ref[...] = yield_ref[...] - value


PARAMS = pltpu.CompilerParams(vmem_limit_bytes=48 * 1024 * 1024)


def segments(index, yields, mask):
    shape = jax.ShapeDtypeStruct(mask.shape, F32)
    return pl.pallas_call(
        segment_kernel,
        out_shape=(shape, shape),
        compiler_params=PARAMS,
        cost_estimate=pl.CostEstimate(
            flops=2 * 128 * 128 * index.shape[1],
            bytes_accessed=16 * index.shape[1],
            transcendentals=0,
        ),
        name="segments",
    )(index, yields, mask)


def grams(feats, weight, product):
    width, pixels = feats.shape
    rows = bands(width)[1] + 8 * pl.cdiv(pl.cdiv(width, LANES), 8)
    return pl.pallas_call(
        gram_kernel,
        out_shape=jax.ShapeDtypeStruct((rows, LANES), F32),
        scratch_shapes=[pltpu.VMEM((width + 16, width), F32)],
        compiler_params=PARAMS,
        name="grams",
    )(feats, weight, product)


def solves(packed, feats, index, yields):
    width, pixels = feats.shape
    size = pl.cdiv(width, LANES) * LANES
    shape = jax.ShapeDtypeStruct((1, pixels), F32)
    return pl.pallas_call(
        solve_kernel,
        out_shape=(shape, shape, jax.ShapeDtypeStruct(yields.shape, F32)),
        scratch_shapes=[
            pltpu.VMEM((size, size), F32),
            pltpu.VMEM((size, size), F32),
            pltpu.VMEM((width + 16, width), BF16),
            pltpu.VMEM((width, width), BF16),
            pltpu.VMEM((pixels // LANES, LANES), F32),
        ],
        compiler_params=PARAMS,
        name="solves",
    )(packed, feats, index, yields)


def window_kernel(shape, own_ref, out_ref, landed, middle, send_sem, recv_sem):
    tiles, cols, dates = shape
    row = lax.axis_index("tiles")
    col = lax.axis_index("cols") * dates + lax.axis_index("dates")
    total = own_ref.shape[0]
    step = -(-total // (8 * PIECES)) * 8
    pieces = [pl.ds(at, min(step, total - at)) for at in range(0, total, step)]

    def place(c):
        return {"cols": c // dates, "dates": c % dates}

    links = (
        (row < tiles - 1, lambda: {"tiles": row + 1}, row > 0, lambda: {"tiles": row - 1}),
        (row > 0, lambda: {"tiles": row - 1}, row < tiles - 1, lambda: {"tiles": row + 1}),
        (col < cols * dates - 1, lambda: place(col + 1), col > 0, lambda: place(col - 1)),
        (col > 0, lambda: place(col - 1), col < cols * dates - 1, lambda: place(col + 1)),
    )

    def copy(d, i, source, device):
        return pltpu.make_async_remote_copy(
            src_ref=source.at[pieces[i]],
            dst_ref=landed.at[d, pieces[i]],
            send_sem=send_sem.at[d, i],
            recv_sem=recv_sem.at[d, i],
            device_id=device,
            device_id_type=pl.DeviceIdType.MESH,
        )

    barrier = pltpu.get_barrier_semaphore()
    for there, target, _, _ in links:

        @pl.when(there)
        def _(target=target):
            pl.semaphore_signal(
                barrier, inc=1, device_id=target(), device_id_type=pl.DeviceIdType.MESH
            )

    peers = sum(there.astype(jnp.int32) for there, _, _, _ in links)
    pl.semaphore_wait(barrier, peers)

    def send(d, i, source):
        there, target, _, _ = links[d]

        @pl.when(there)
        def _():
            copy(d, i, source, target()).start()

    def receive(d, i, source, into):
        _, _, there, origin = links[d]

        @pl.when(there)
        def _():
            copy(d, i, source, origin()).wait_recv()
            into[pieces[i]] += 0.5 * landed[d, pieces[i]]

    count = len(pieces)
    for i in range(count):
        send(0, i, own_ref)
        send(1, i, own_ref)
    for i in range(count):
        middle[pieces[i]] = own_ref[pieces[i]]
        receive(0, i, own_ref, middle)
        receive(1, i, own_ref, middle)
        send(2, i, middle)
        send(3, i, middle)
    for i in range(count):
        out_ref[pieces[i]] = middle[pieces[i]]
        receive(2, i, middle, out_ref)
        receive(3, i, middle, out_ref)
    for i in range(count):
        for d in range(4):
            there, target, _, _ = links[d]

            @pl.when(there)
            def _(d=d, i=i, target=target):
                copy(d, i, own_ref if d < 2 else middle, target()).wait_send()


def window(packed):
    shape = tuple(lax.axis_size(name) for name in ("tiles", "cols", "dates"))
    in_vmem = pl.BlockSpec(memory_space=pltpu.VMEM)
    return pl.pallas_call(
        functools.partial(window_kernel, shape),
        out_shape=jax.ShapeDtypeStruct(packed.shape, F32),
        in_specs=[in_vmem],
        out_specs=in_vmem,
        scratch_shapes=[
            pltpu.VMEM((4,) + packed.shape, F32),
            pltpu.VMEM(packed.shape, F32),
            pltpu.SemaphoreType.DMA((4, PIECES)),
            pltpu.SemaphoreType.DMA((4, PIECES)),
        ],
        compiler_params=pltpu.CompilerParams(
            collective_id=0,
            has_side_effects=True,
            vmem_limit_bytes=48 * 1024 * 1024,
        ),
        name="window",
    )(packed)


def on_device(imagery, pixel_mask, point_pixel, point_yield):
    whole = lax.all_to_all(imagery, "dates", split_axis=1, concat_axis=2, tiled=True)
    feats = whole[0, 0]
    pixels = feats.shape[1]
    index = point_pixel[0]
    yields = point_yield[0]
    mask = pixel_mask.reshape(pixels // LANES, LANES)
    weight, product = segments(index, yields, mask)
    packed = grams(feats, weight, product)
    packed = window(packed)
    fitted, spread, resid = solves(packed, feats, index, yields)
    return (fitted[None], spread[None], resid[None])


def step_rows(full, k):
    return 128 if k < full else 64


def payload_rows(full, k):
    return 128 * k + 64 + 8 if k < full else 48 * k + 24 + 8


def payload_starts(full):
    starts, at = [], 0
    for k in range(full + 1):
        starts.append(at)
        at += payload_rows(full, k)
    return starts, at


def pack_square(block):
    top, bottom = block[:64], block[64:]
    lane = lax.broadcasted_iota(jnp.int32, top.shape, 1)
    line = lax.broadcasted_iota(jnp.int32, top.shape, 0)
    packed = jnp.where(line >= lane - 64, bottom, pltpu.roll(top, 64, 1))
    diagonal = jnp.sum(jnp.where(line == lane, top, 0.0), 0, keepdims=True)
    return packed, diagonal


def unpack_square(packed, diagonal):
    lane = lax.broadcasted_iota(jnp.int32, packed.shape, 1)
    line = lax.broadcasted_iota(jnp.int32, packed.shape, 0)
    flipped = jnp.concatenate([packed, packed], 0).T
    corner = jnp.where(line < lane, pltpu.roll(packed, 64, 1), flipped[64:])
    corner = jnp.where(line == lane, diagonal, corner)
    top = jnp.where(lane < 64, corner, flipped[:64])
    bottom = jnp.where(line >= lane - 64, packed, flipped[64:])
    return jnp.concatenate([top, bottom], 0)


def fold(block):
    lane = lax.broadcasted_iota(jnp.int32, (24, LANES), 1)
    return jnp.where(lane < 64, block[:24], pltpu.roll(block[24:], 64, 1))


def unfold(block):
    lane = lax.broadcasted_iota(jnp.int32, (48, LANES), 1)
    both = jnp.concatenate([block, pltpu.roll(block, 64, 1)], 0)
    return jnp.where(lane < 64, both, 0.0)


def squeeze(block):
    return jnp.concatenate([block[0:24], block[32:56]], 0)


def stretch(block):
    gap = jnp.zeros((8, block.shape[1]), block.dtype)
    return jnp.concatenate([block[0:24], gap, block[24:48], gap], 0)


def factor8(small):
    line = lax.broadcasted_iota(jnp.int32, small.shape[1:], 0)
    lower = []
    pivots = jnp.zeros(small.shape[1:], F32)
    for p in range(0, 8, 2):
        one, two = line == p, line == p + 1
        first, second = small[p], small[p + 1]
        a, b, c = first[p : p + 1], second[p : p + 1], second[p + 1 : p + 2]
        det = a * c - b * b
        ra = 1.0 / a
        t = b * ra
        pivots = jnp.where(one, a, jnp.where(two, det * ra, pivots))
        lower = [
            jnp.where(
                one,
                small[j],
                jnp.where(two, small[j] - t * small[j][p : p + 1], lower[j]),
            )
            for j in range(p)
        ]
        lower.append(jnp.where(one, 1.0, jnp.where(two, -t, 0.0)))
        lower.append(jnp.where(two, 1.0, 0.0))
        r = 1.0 / det
        ea, eb, ec = c * r, -b * r, a * r
        left = first * ea + second * eb
        right = first * eb + second * ec
        left = jnp.where(one, -ea, jnp.where(two, -eb, left))
        right = jnp.where(one, -eb, jnp.where(two, -ec, right))
        base = jnp.where((one | two)[None], 0.0, small)
        rest = base - (
            left[None] * small[:, p : p + 1] + right[None] * small[:, p + 1 : p + 2]
        )
        parts = [rest[:p]] if p else []
        parts.append(jnp.stack([-left, -right]))
        if p < 6:
            parts.append(rest[p + 2 :])
        small = jnp.concatenate(parts, 0)
    return small, lower, lax.rsqrt(pivots)


def mix(planes, lines):
    terms = [planes[j] * lines[j : j + 1] for j in range(8)]
    while len(terms) > 1:
        terms = [a + b for a, b in zip(terms[::2], terms[1::2])]
    return terms[0]


def block_factor(block, groups, midway=None):
    rows = block.shape[0]
    lane = lax.broadcasted_iota(jnp.int32, (8, LANES), 1)
    line = lax.broadcasted_iota(jnp.int32, (8, LANES), 0)
    result = [jnp.zeros((8, LANES), F32)] * (rows // 8)
    below, first = block, 0
    for g in groups:
        if midway is not None and g == 12:
            midway()
        k = 8 * g
        below = below[k - first :]
        top = below[:8]
        small = jnp.stack(
            [jnp.broadcast_to(top[:, k + j : k + j + 1], (8, LANES)) for j in range(8)]
        )
        small, lower, root = factor8(small)
        inside = (lane >= k) & (lane < k + 8)
        top = jnp.where(inside, jnp.where(lane == line + k, 1.0, 0.0), top)
        result[g] = jnp.where(lane < k + 8, mix(lower, top) * root, 0.0)
        below = below[8:]
        first = k + 8
        if below.shape[0]:
            new = mix(small, top)
            cols = [below[:, k + j : k + j + 1] for j in range(8)]
            keep = (lane[:1] < k) | (lane[:1] >= k + 8)
            below = jnp.where(keep, below, 0.0)
            for j in range(0, 8, 2):
                below = below - (
                    cols[j] * new[j : j + 1] + cols[j + 1] * new[j + 1 : j + 2]
                )
    return jnp.concatenate(result, 0)


def split2(x):
    high = x.astype(BF16)
    return high, (x - high.astype(F32)).astype(BF16)


def fused_kernel(
    tiles,
    img,
    index_hbm,
    yield_hbm,
    mask_hbm,
    fit,
    spread_ref,
    index_out,
    yield_out,
    feats,
    whole,
    tail,
    tail_in,
    index_ref,
    yield_ref,
    mask_ref,
    weight_rows,
    product_rows,
    acc,
    own,
    middle,
    outgoing,
    landed,
    inverse,
    split_r,
    rhs_ref,
    z_ref,
    fit8,
    spread8,
    local_sem,
    bulk_send,
    bulk_recv,
    z_send,
    z_recv,
    core_send,
    core_recv,
    x_send,
    x_recv,
):
    half, pixels = img.shape[2:]
    full = half // 64
    steps = full + 1
    rows = pixels // LANES
    scale = 1.0 / pixels
    starts, _ = payload_starts(full)
    mesh_ids = pl.DeviceIdType.MESH

    z = lax.axis_index("tiles")
    c = lax.axis_index("cols")
    d = lax.axis_index("dates")
    across = {"dates": 1 - d}
    core = {"cols": 1 - c}
    up, down = {"tiles": z + 1}, {"tiles": z - 1}
    has_up, has_down = z < tiles - 1, z > 0
    joins = c == d

    def place(k, s):
        if k < full:
            return pl.multiple_of(128 * k + 64 * s, 16)
        return pl.multiple_of(128 * full + 32 * s, 16)

    height = [64] * full + [16]
    source_at = [64 * k for k in range(steps)]

    local = [
        pltpu.make_async_copy(index_hbm.at[0], index_ref, local_sem.at[0]),
        pltpu.make_async_copy(yield_hbm.at[0], yield_ref, local_sem.at[1]),
        pltpu.make_async_copy(mask_hbm, mask_ref, local_sem.at[2]),
        pltpu.make_async_copy(img.at[0], whole, local_sem.at[3]),
    ]
    for k in range(steps):
        local.append(
            pltpu.make_async_copy(
                img.at[0, d, pl.ds(source_at[k], height[k])],
                feats.at[pl.ds(place(k, d), height[k])],
                local_sem.at[4 + k],
            )
        )
    for copy in local:
        copy.start()

    barrier = pltpu.get_barrier_semaphore()
    peers = ((has_up, up), (has_down, down), (None, core), (None, across))
    for there, target in peers:

        def greet(target=target):
            pl.semaphore_signal(
                barrier, inc=1, device_id=target, device_id_type=mesh_ids
            )

        if there is None:
            greet()
        else:
            pl.when(there)(greet)
    pl.semaphore_wait(barrier, 2 + has_up.astype(jnp.int32) + has_down.astype(jnp.int32))

    bulk = []
    for k in range(steps):
        bulk.append(
            pltpu.make_async_remote_copy(
                src_ref=img.at[0, 1 - d, pl.ds(source_at[k], height[k])],
                dst_ref=feats.at[pl.ds(place(k, d), height[k])],
                send_sem=bulk_send.at[k],
                recv_sem=bulk_recv.at[k],
                device_id=across,
                device_id_type=mesh_ids,
            )
        )
    bulk.append(
        pltpu.make_async_remote_copy(
            src_ref=tail,
            dst_ref=tail_in,
            send_sem=bulk_send.at[steps],
            recv_sem=bulk_recv.at[steps],
            device_id=across,
            device_id_type=mesh_ids,
        )
    )
    bulk[0].start()
    bulk[1].start()

    for copy in local[:4]:
        copy.wait()
    end = whole[1 - d][half - 8 : half]
    tail[...] = jnp.concatenate([end[:, : pixels // 2], end[:, pixels // 2 :]], 0)

    def put_tail(s, end):
        at = pl.ds(pl.multiple_of(128 * full + 32 * s + 16, 16), 16)
        feats[at, :] = jnp.concatenate([end, jnp.zeros_like(end)], 0)

    put_tail(d, whole[d][half - 8 : half])

    high, low = one_hots(index_ref[...], rows)
    low = jnp.where(low, 1.0, 0.0).astype(BF16)
    index_out[...] = index_ref[...]
    yield_out[...] = yield_ref[...]
    parts = [jnp.where(high, 1.0, 0.0).astype(BF16)]
    for piece in split3(yield_ref[...]):
        parts.append(jnp.where(high, piece.astype(F32), 0.0).astype(BF16))
    sums = lax.dot_general(
        jnp.concatenate(parts, 0), low, NT, preferred_element_type=F32
    )
    counts = sums[:rows]
    totals = sums[rows : 2 * rows] + sums[2 * rows : 3 * rows] + sums[3 * rows :]
    weight = jnp.where(counts > 0, mask_ref[...].astype(F32), 0.0)
    product = weight * (totals / jnp.maximum(counts, 1.0))
    pa, pb, pc = (p.astype(F32) for p in split3(product))
    line16 = lax.broadcasted_iota(jnp.int32, (16, LANES), 0)
    for r in range(rows):
        at = slice(r * LANES, (r + 1) * LANES)
        weight_rows[:, at] = jnp.broadcast_to(weight[r : r + 1], (16, LANES)).astype(BF16)
        extra = jnp.where(
            line16 == 0,
            pa[r : r + 1],
            jnp.where(
                line16 == 1,
                pb[r : r + 1],
                jnp.where(line16 == 2, pc[r : r + 1], 0.0),
            ),
        )
        product_rows[:, at] = extra.astype(BF16)

    acc[...] = jnp.zeros_like(acc)
    inverse[...] = jnp.zeros_like(inverse)
    fit8[...] = jnp.zeros_like(fit8)
    spread8[...] = jnp.zeros_like(spread8)

    def payload(k, h):
        count = payload_rows(full, k)
        first = count // 16 * 8
        if h == 0:
            return pl.ds(starts[k], first)
        return pl.ds(starts[k] + first, count - first)

    def z_copy(way, k, h, target):
        return pltpu.make_async_remote_copy(
            src_ref=own.at[payload(k, h)],
            dst_ref=landed.at[way, payload(k, h)],
            send_sem=z_send.at[way, 2 * k + h],
            recv_sem=z_recv.at[way, 2 * k + h],
            device_id=target,
            device_id_type=mesh_ids,
        )

    def core_copy(k, h):
        return pltpu.make_async_remote_copy(
            src_ref=middle.at[payload(k, h)],
            dst_ref=landed.at[2, payload(k, h)],
            send_sem=core_send.at[2 * k + h],
            recv_sem=core_recv.at[2 * k + h],
            device_id=core,
            device_id_type=mesh_ids,
        )

    def x_copy(k, h, source=outgoing):
        return pltpu.make_async_remote_copy(
            src_ref=source.at[payload(k, h)],
            dst_ref=landed.at[3, payload(k, h)],
            send_sem=x_send.at[2 * k + h],
            recv_sem=x_recv.at[2 * k + h],
            device_id=across,
            device_id_type=mesh_ids,
        )

    def gram(k):
        count = step_rows(full, k)
        base, end = 128 * k, 128 * k + count
        local[4 + k].wait()
        bulk[k].wait_recv()
        if k == full:
            bulk[steps].wait_recv()
            folded = tail_in[...]
            put_tail(1 - d, jnp.concatenate([folded[:8], folded[8:]], 1))
        wide = count + 16
        acc[:end, :wide] = jnp.zeros((end, wide), F32)

        def chunk(i, _):
            at = pl.ds(pl.multiple_of(i * SPAN, SPAN), SPAN)
            weights = jnp.concatenate([weight_rows[:, at]] * (count // 16), 0)
            left = jnp.concatenate(
                [feats[base:end, at] * weights, product_rows[:, at]], 0
            )
            acc[:end, :wide] += lax.dot_general(
                feats[:end, at], left, NT, preferred_element_type=F32
            )
            return 0

        lax.fori_loop(0, pixels // SPAN, chunk, 0)
        at = starts[k]
        diagonal = jnp.zeros((1, LANES), F32)
        for j in range(k + 1):
            block = acc[128 * j : 128 * j + 128, :LANES]
            if k == full:
                block = squeeze(block.T)
            if j == k and k < full:
                block, diagonal = pack_square(block)
            if j == k and k == full:
                block = fold(block)
            own[at : at + block.shape[0]] = block
            at += block.shape[0]
        moment = acc[base : base + 128, count : count + 1]
        moment = moment + acc[base : base + 128, count + 1 : count + 2]
        moment = moment + acc[base : base + 128, count + 2 : count + 3]
        moment = jnp.broadcast_to(moment, (LANES, LANES)).T
        line8 = lax.broadcasted_iota(jnp.int32, (8, LANES), 0)
        own[at : at + 8] = jnp.where(line8 == 0, moment[:8], diagonal)
        for h in range(2):
            pl.when(has_up)(lambda h=h: z_copy(0, k, h, up).start())
            pl.when(has_down)(lambda h=h: z_copy(1, k, h, down).start())

    def z_join(k):
        for h in range(2):
            at = payload(k, h)

            @pl.when(has_down)
            def _(h=h, at=at):
                z_copy(0, k, h, down).wait_recv()
                middle[at] = own[at] + 0.5 * landed[0, at]

            @pl.when(jnp.logical_not(has_down))
            def _(at=at):
                middle[at] = own[at]

            @pl.when(has_up)
            def _(h=h, at=at):
                z_copy(1, k, h, up).wait_recv()
                middle[at] += 0.5 * landed[1, at]

            @pl.when(jnp.logical_not(joins))
            def _(h=h):
                core_copy(k, h).start()
                x_copy(k, h, middle).start()

        @pl.when(joins)
        def _():
            for h in range(2):
                at = payload(k, h)
                core_copy(k, h).wait_recv()
                outgoing[at] = middle[at] + landed[2, at]
                x_copy(k, h).start()

        if k + 2 < steps:
            bulk[k + 2].start()
        if k + 2 == full:
            bulk[steps].start()

    def solve(k, midway=None):
        at = pl.ds(starts[k], payload_rows(full, k))
        for h in range(2):
            x_copy(k, h).wait_recv()
        count = step_rows(full, k)
        base = 128 * k
        window = (middle[at] + 0.5 * landed[3, at]) * scale
        step = 128 if k < full else 48
        blocks = [window[j * step : (j + 1) * step] for j in range(k)]
        ends = window[payload_rows(full, k) - 8 :]
        rhs_ref[:, base : base + 128] = ends
        square = window[k * step : payload_rows(full, k) - 8]
        if k < full:
            blocks.append(unpack_square(square, ends[1:2]))
        else:
            blocks.append(unfold(square))
            blocks = [stretch(block) for block in blocks]
        lane = lax.broadcasted_iota(jnp.int32, (count, LANES), 1)
        line = lax.broadcasted_iota(jnp.int32, (count, LANES), 0)
        pivot = blocks[k] + jnp.where(lane == line, ridge_term, 0.0)
        if k:
            known = inverse[:base, :base]
            if k < full:
                raised = dot32(known, jnp.concatenate(blocks[:k], 0))
                factor = jnp.concatenate(
                    [raised[128 * j : 128 * j + 128].T for j in range(k)], 1
                )
                drop = dot32(factor, raised)
            else:
                factor = dot32(jnp.concatenate(blocks[:k], 1), known, NT)
                drop = dot32(factor, factor, NT)
            coupling = dot32(factor, known)
            if count < LANES:
                drop = jnp.concatenate(
                    [drop, jnp.zeros((count, LANES - count), F32)], 1
                )
            pivot = pivot - drop
        groups = range(16) if k < full else (0, 1, 2, 4, 5, 6)
        lower = block_factor(pivot, groups, midway)
        if k:
            lower = jnp.concatenate([-dot32(lower[:, :count], coupling), lower], 1)
        z_ref[:count] = jnp.sum(
            lower * rhs_ref[:1, : base + 128], 1, keepdims=True
        )
        high, low = split2(lower)
        split_r[:count, : base + 128] = high
        split_r[count : 2 * count, : base + 128] = low
        if k < full:
            inverse[base : base + count, : base + 128] = lower

    def spread(k):
        count = step_rows(full, k)
        end = 128 * k + count
        last = k == full

        def chunk(i, _):
            at = pl.ds(pl.multiple_of(i * SPAN, SPAN), SPAN)
            part = feats[:end, at]
            both = jnp.dot(
                split_r[: 2 * count, :end], part, preferred_element_type=F32
            )
            value = both[:count] + both[count:]
            square = (value * value).reshape(count // 8, 8, SPAN)
            linear = (value * z_ref[:count]).reshape(count // 8, 8, SPAN)
            square = spread8[:, at] + jnp.sum(square, 0)
            linear = fit8[:, at] + jnp.sum(linear, 0)
            if last:
                spread_ref[:, at] = jnp.sum(square, 0, keepdims=True) / (2 * half)
                fitted = jnp.sum(linear, 0, keepdims=True)
                for s in range(SPAN // LANES):
                    fit[pl.ds(i * (SPAN // LANES) + s, 1), :] = fitted[
                        :, s * LANES : (s + 1) * LANES
                    ]
            else:
                spread8[:, at] = square
                fit8[:, at] = linear
            return 0

        lax.fori_loop(0, pixels // SPAN, chunk, 0)

    gram(0)
    z_join(0)
    for k in range(1, steps):
        gram(k)
        if k == full:
            spread(k - 2)
        solve(k - 1, lambda k=k: z_join(k))
        if k != full - 1:
            spread(k - 1)
    solve(full)
    spread(full)

    for copy in bulk:
        copy.wait_send()
    for k in range(steps):
        for h in range(2):
            pl.when(has_up)(lambda k=k, h=h: z_copy(0, k, h, up).wait_send())
            pl.when(has_down)(lambda k=k, h=h: z_copy(1, k, h, down).wait_send())
            pl.when(jnp.logical_not(joins))(
                lambda k=k, h=h: core_copy(k, h).wait_send()
            )
            x_copy(k, h).wait_send()


def fused(imagery, index, yields, mask):
    half, pixels = imagery.shape[2:]
    full = half // 64
    steps = full + 1
    rows = payload_starts(full)[1]
    size = 128 * steps
    shape = jax.ShapeDtypeStruct((1, pixels), F32)
    in_hbm = pl.BlockSpec(memory_space=pltpu.HBM)
    in_vmem = pl.BlockSpec(memory_space=pltpu.VMEM)
    dma = pltpu.SemaphoreType.DMA
    return pl.pallas_call(
        functools.partial(fused_kernel, lax.axis_size("tiles")),
        out_shape=(
            pltpu.VMEM((pixels // LANES, LANES), F32),
            pltpu.VMEM((1, pixels), F32),
            pltpu.VMEM((1, pixels), jnp.int32),
            pltpu.VMEM((1, pixels), F32),
        ),
        in_specs=[in_hbm] * 4,
        out_specs=(in_vmem,) * 4,
        scratch_shapes=[
            pltpu.VMEM((128 * full + 64, pixels), BF16),
            pltpu.VMEM((2, half, pixels), BF16),
            pltpu.VMEM((16, pixels // 2), BF16),
            pltpu.VMEM((16, pixels // 2), BF16),
            pltpu.VMEM((1, pixels), jnp.int32),
            pltpu.VMEM((1, pixels), F32),
            pltpu.VMEM((pixels // LANES, LANES), jnp.int32),
            pltpu.VMEM((16, pixels), BF16),
            pltpu.VMEM((16, pixels), BF16),
            pltpu.VMEM((size, 2 * LANES), F32),
            pltpu.VMEM((rows, LANES), F32),
            pltpu.VMEM((rows, LANES), F32),
            pltpu.VMEM((rows, LANES), F32),
            pltpu.VMEM((4, rows, LANES), F32),
            pltpu.VMEM((size, size), F32),
            pltpu.VMEM((2 * LANES, size), BF16),
            pltpu.VMEM((8, size), F32),
            pltpu.VMEM((LANES, 1), F32),
            pltpu.VMEM((8, pixels), F32),
            pltpu.VMEM((8, pixels), F32),
            dma((4 + steps,)),
            dma((steps + 1,)),
            dma((steps + 1,)),
            dma((2, 2 * steps)),
            dma((2, 2 * steps)),
            dma((2 * steps,)),
            dma((2 * steps,)),
            dma((2 * steps,)),
            dma((2 * steps,)),
        ],
        compiler_params=pltpu.CompilerParams(
            collective_id=1,
            has_side_effects=True,
            vmem_limit_bytes=56 * 1024 * 1024,
        ),
        name="fused",
    )(imagery, index, yields, mask)


def finish_kernel(
    fit_ref, spread_in, index_ref, yield_ref, fitted_ref, spread_ref, resid_ref
):
    rows = fit_ref.shape[0]
    fit = fit_ref[...]
    high, low = one_hots(index_ref[...], rows)
    low = jnp.where(low, 1.0, 0.0).astype(BF16)
    table = jnp.concatenate(split3(fit), 0)
    found = jnp.dot(table, low, preferred_element_type=F32)
    found = found[:rows] + (found[rows : 2 * rows] + found[2 * rows :])
    value = jnp.sum(jnp.where(high, found, 0.0), 0, keepdims=True)
    resid_ref[...] = yield_ref[...] - value
    for r in range(rows):
        fitted_ref[:, r * LANES : (r + 1) * LANES] = fit[r : r + 1]
    spread_ref[...] = spread_in[...]


def finish(fit, spread, index, yields):
    shape = jax.ShapeDtypeStruct(spread.shape, F32)
    return pl.pallas_call(
        finish_kernel,
        out_shape=(shape, shape, shape),
        compiler_params=pltpu.CompilerParams(vmem_limit_bytes=16 * 1024 * 1024),
        name="finish",
    )(fit, spread, index, yields)


def on_device_fused(imagery, pixel_mask, point_pixel, point_yield):
    pixels = imagery.shape[3]
    mask = pixel_mask.reshape(pixels // LANES, LANES)
    fitted, spread, resid = finish(*fused(imagery, point_pixel, point_yield, mask))
    return (fitted[None], spread[None], resid[None])


def solution(mesh):
    features = P(("groups", "tiles"), "cols", "dates", None)
    points = P(("groups", "tiles"), ("cols", "dates"), None)
    sizes = dict(mesh.shape)

    def body(imagery, pixel_mask, point_pixel, point_yield):
        pairs = sizes["cols"] == 2 and sizes["dates"] == 2
        one_tile = imagery.shape[:2] == (1, 2)
        if pairs and one_tile and imagery.shape[2] % 64 == 24:
            run = on_device_fused
        else:
            run = on_device
        return run(imagery, pixel_mask, point_pixel, point_yield)

    return jax.shard_map(
        body,
        mesh=mesh,
        in_specs=(features, points, points, points),
        out_specs=(points, points, points),
        check_vma=False,
    )
```

```python
import functools

import jax
import jax.numpy as jnp
from jax import lax
from jax.experimental import pallas as pl
from jax.experimental.pallas import tpu as pltpu
from jax.sharding import PartitionSpec as P

ridge_term = 0.05
LANES = 128
CHUNK = 512
PIECES = 8
SPAN = 4096
F32 = jnp.float32
BF16 = jnp.bfloat16
NT = (((1,), (1,)), ((), ()))


def split3(x):
    a = x.astype(BF16)
    rest = x - a.astype(F32)
    b = rest.astype(BF16)
    c = (rest - b.astype(F32)).astype(BF16)
    return a, b, c


def one_hots(index, rows):
    points = index.shape[1]
    high = lax.broadcasted_iota(jnp.int32, (rows, points), 0) == index // LANES
    low = lax.broadcasted_iota(jnp.int32, (LANES, points), 0) == index % LANES
    return high, low


def segment_kernel(index_ref, yield_ref, mask_ref, weight_ref, product_ref):
    rows = mask_ref.shape[0]
    high, low = one_hots(index_ref[...], rows)
    low = jnp.where(low, 1.0, 0.0).astype(BF16)
    pieces = [jnp.where(high, 1.0, 0.0).astype(BF16)]
    for piece in split3(yield_ref[...]):
        pieces.append(jnp.where(high, piece.astype(F32), 0.0).astype(BF16))
    sums = lax.dot_general(
        jnp.concatenate(pieces, 0), low, NT, preferred_element_type=F32
    )
    counts = sums[:rows]
    totals = sums[rows : 2 * rows] + sums[2 * rows : 3 * rows] + sums[3 * rows :]
    weight = jnp.where(counts > 0, mask_ref[...].astype(F32), 0.0)
    weight_ref[...] = weight
    product_ref[...] = weight * (totals / jnp.maximum(counts, 1.0))


def bands(width):
    blocks, offset = [], 0
    for i in range(pl.cdiv(width, LANES)):
        height = min(LANES, width - i * LANES)
        for j in range(i + 1):
            blocks.append((i, j, height, offset))
            offset += height
    return blocks, offset


def gram_kernel(feats_ref, weight_ref, product_ref, out_ref, acc):
    width, pixels = feats_ref.shape
    acc[...] = jnp.zeros_like(acc)

    def step(c, _):
        at = pl.multiple_of(c * CHUNK, CHUNK)
        feats = feats_ref[:, pl.ds(at, CHUNK)]
        left = []
        for s in range(CHUNK // LANES):
            row = pl.ds(c * (CHUNK // LANES) + s, 1)
            part = feats[:, s * LANES : (s + 1) * LANES]
            scaled = part * weight_ref[row, :].astype(BF16)
            a, b, d = (p.astype(F32) for p in split3(product_ref[row, :]))
            line = lax.broadcasted_iota(jnp.int32, (16, LANES), 0)
            extra = jnp.where(
                line == 0, a, jnp.where(line == 1, b, jnp.where(line == 2, d, 0.0))
            )
            left.append(jnp.concatenate([scaled, extra.astype(BF16)], 0))
        acc[...] += lax.dot_general(
            jnp.concatenate(left, 1), feats, NT, preferred_element_type=F32
        )
        return 0

    lax.fori_loop(0, pixels // CHUNK, step, 0)
    blocks, offset = bands(width)
    out_ref[...] = jnp.zeros_like(out_ref)
    for i, j, height, at in blocks:
        wide = min(LANES, width - j * LANES)
        out_ref[at : at + height, :wide] = acc[
            i * LANES : i * LANES + height, j * LANES : j * LANES + wide
        ]
    moment = acc[width : width + 1] + acc[width + 1 : width + 2]
    moment = moment + acc[width + 2 : width + 3]
    for j in range(pl.cdiv(width, LANES)):
        wide = min(LANES, width - j * LANES)
        out_ref[offset + j : offset + j + 1, :wide] = moment[
            :, j * LANES : j * LANES + wide
        ]


def small_inverse(p):
    n = len(p)
    for k in range(n):
        d = 1.0 / p[k][k]
        row = [d if j == k else p[k][j] * d for j in range(n)]
        new = []
        for i in range(n):
            if i == k:
                new.append(row)
            else:
                new.append(
                    [
                        -p[i][k] * d if j == k else p[i][j] - p[i][k] * row[j]
                        for j in range(n)
                    ]
                )
        p = new
    return p


def block_inverse(block, pivots, group=8):
    tiles = [block[8 * g : 8 * g + 8] for g in range(LANES // 8)]
    lane = lax.broadcasted_iota(jnp.int32, (8, LANES), 1)
    line = lax.broadcasted_iota(jnp.int32, (8, LANES), 0)
    for k in range(0, pivots, group):
        g, r = divmod(k, 8)
        cols = [
            [
                jnp.broadcast_to(t[:, k + j : k + j + 1], (8, LANES))
                for t in tiles
            ]
            for j in range(group)
        ]
        small = [
            [cols[j][g][r + i : r + i + 1] for j in range(group)]
            for i in range(group)
        ]
        small = small_inverse(small)
        rows = []
        for i in range(group):
            old = tiles[g][r + i : r + i + 1]
            old = jnp.where((lane[:1] >= k) & (lane[:1] < k + group), 0.0, old)
            rows.append(jnp.where(lane[:1] == k + i, 1.0, old))
        new_rows = []
        for i in range(group):
            total = small[i][0] * rows[0]
            for j in range(1, group):
                total = total + small[i][j] * rows[j]
            new_rows.append(jnp.broadcast_to(total, (8, LANES)))
        keep = (lane < k) | (lane >= k + group)
        for t in range(LANES // 8):
            value = jnp.where(keep, tiles[t], 0.0)
            for j in range(group):
                value = value - cols[j][t] * new_rows[j]
            if t == g:
                for i in range(group):
                    value = jnp.where(line == r + i, new_rows[i], value)
            tiles[t] = value
    return jnp.concatenate(tiles, 0)


NN = (((1,), (0,)), ((), ()))


def dot32(a, b, dims=NN):
    return lax.dot_general(
        a, b, dims, precision=lax.Precision.HIGHEST, preferred_element_type=F32
    )


def solve_kernel(
    packed_ref,
    feats_ref,
    index_ref,
    yield_ref,
    fitted_ref,
    spread_ref,
    resid_ref,
    system,
    base,
    high_ref,
    low_ref,
    fit,
):
    width, pixels = feats_ref.shape
    count = pl.cdiv(width, LANES)
    size = count * LANES
    blocks, offset = bands(width)
    scale = 1.0 / pixels
    line = lax.broadcasted_iota(jnp.int32, (LANES, LANES), 0)
    lane = lax.broadcasted_iota(jnp.int32, (LANES, LANES), 1)
    for i, j, height, at in blocks:
        value = packed_ref[at : at + height] * scale
        if height < LANES:
            value = jnp.concatenate(
                [value, jnp.zeros((LANES - height, LANES), F32)], 0
            )
        if i == j:
            diagonal = jnp.where(line < height, ridge_term, 1.0)
            value = value + jnp.where(line == lane, diagonal, 0.0)
        system[i * LANES : (i + 1) * LANES, j * LANES : (j + 1) * LANES] = value
        if i != j:
            system[j * LANES : (j + 1) * LANES, i * LANES : (i + 1) * LANES] = value.T

    base[...] = system[...]
    column = lax.broadcasted_iota(jnp.int32, (LANES, size), 1)
    wide_line = lax.broadcasted_iota(jnp.int32, (LANES, size), 0)

    def eliminate(k, pivots):
        at = k * LANES if isinstance(k, int) else pl.multiple_of(k * LANES, LANES)
        here = pl.ds(at, LANES)
        inverse = block_inverse(system[here, here], pivots)
        inside = (column >= at) & (column < at + LANES)
        unit = jnp.where(column == wide_line + at, 1.0, 0.0)
        right = dot32(inverse, jnp.where(inside, unit, system[here, :]))
        left = system[:, here]
        system[:, here] = jnp.zeros_like(left)
        system[...] -= dot32(left, right)
        system[here, :] = right

    full = width // LANES

    def body(k, _):
        eliminate(k, LANES)
        return 0

    lax.fori_loop(0, full, body, 0)
    if width % LANES:
        eliminate(full, width % LANES)

    rhs = jnp.concatenate(
        [packed_ref[offset + j : offset + j + 1] for j in range(count)], 1
    )
    rhs = jnp.broadcast_to(rhs * scale, (8, size))
    beta = dot32(rhs, system[...])
    beta = beta + dot32(rhs - dot32(beta, base[...]), system[...])
    beta = beta[:1, :width]
    inverse = system[:width, :width]
    upper = inverse.astype(BF16)
    a, b, d = (p.astype(F32) for p in split3(beta))
    row16 = lax.broadcasted_iota(jnp.int32, (16, width), 0)
    extra = jnp.where(row16 == 0, a, jnp.where(row16 == 1, b, jnp.where(row16 == 2, d, 0.0)))
    high_ref[...] = jnp.concatenate([upper, extra.astype(BF16)], 0)
    low_ref[...] = (inverse - upper.astype(F32)).astype(BF16)

    def step(c, _):
        at = pl.multiple_of(c * CHUNK, CHUNK)
        feats = feats_ref[:, pl.ds(at, CHUNK)]
        first = jnp.dot(high_ref[...], feats, preferred_element_type=F32)
        second = jnp.dot(low_ref[...], feats, preferred_element_type=F32)
        total = (first[:width] + second) * feats.astype(F32)
        spread_ref[:, pl.ds(at, CHUNK)] = jnp.sum(total, 0, keepdims=True) / width
        fitted = first[width : width + 1] + (
            first[width + 1 : width + 2] + first[width + 2 : width + 3]
        )
        fitted_ref[:, pl.ds(at, CHUNK)] = fitted
        for s in range(CHUNK // LANES):
            fit[pl.ds(c * (CHUNK // LANES) + s, 1), :] = fitted[
                :, s * LANES : (s + 1) * LANES
            ]
        return 0

    lax.fori_loop(0, pixels // CHUNK, step, 0)

    rows = pixels // LANES
    high, low = one_hots(index_ref[...], rows)
    low = jnp.where(low, 1.0, 0.0).astype(BF16)
    table = jnp.concatenate(split3(fit[...]), 0)
    found = jnp.dot(table, low, preferred_element_type=F32)
    found = found[:rows] + (found[rows : 2 * rows] + found[2 * rows :])
    value = jnp.sum(jnp.where(high, found, 0.0), 0, keepdims=True)
    resid_ref[...] = yield_ref[...] - value


PARAMS = pltpu.CompilerParams(vmem_limit_bytes=48 * 1024 * 1024)


def segments(index, yields, mask):
    shape = jax.ShapeDtypeStruct(mask.shape, F32)
    return pl.pallas_call(
        segment_kernel,
        out_shape=(shape, shape),
        compiler_params=PARAMS,
        cost_estimate=pl.CostEstimate(
            flops=2 * 128 * 128 * index.shape[1],
            bytes_accessed=16 * index.shape[1],
            transcendentals=0,
        ),
        name="segments",
    )(index, yields, mask)


def grams(feats, weight, product):
    width, pixels = feats.shape
    rows = bands(width)[1] + 8 * pl.cdiv(pl.cdiv(width, LANES), 8)
    return pl.pallas_call(
        gram_kernel,
        out_shape=jax.ShapeDtypeStruct((rows, LANES), F32),
        scratch_shapes=[pltpu.VMEM((width + 16, width), F32)],
        compiler_params=PARAMS,
        name="grams",
    )(feats, weight, product)


def solves(packed, feats, index, yields):
    width, pixels = feats.shape
    size = pl.cdiv(width, LANES) * LANES
    shape = jax.ShapeDtypeStruct((1, pixels), F32)
    return pl.pallas_call(
        solve_kernel,
        out_shape=(shape, shape, jax.ShapeDtypeStruct(yields.shape, F32)),
        scratch_shapes=[
            pltpu.VMEM((size, size), F32),
            pltpu.VMEM((size, size), F32),
            pltpu.VMEM((width + 16, width), BF16),
            pltpu.VMEM((width, width), BF16),
            pltpu.VMEM((pixels // LANES, LANES), F32),
        ],
        compiler_params=PARAMS,
        name="solves",
    )(packed, feats, index, yields)


def window_kernel(shape, own_ref, out_ref, landed, middle, send_sem, recv_sem):
    tiles, cols, dates = shape
    row = lax.axis_index("tiles")
    col = lax.axis_index("cols") * dates + lax.axis_index("dates")
    total = own_ref.shape[0]
    step = -(-total // (8 * PIECES)) * 8
    pieces = [pl.ds(at, min(step, total - at)) for at in range(0, total, step)]

    def place(c):
        return {"cols": c // dates, "dates": c % dates}

    links = (
        (row < tiles - 1, lambda: {"tiles": row + 1}, row > 0, lambda: {"tiles": row - 1}),
        (row > 0, lambda: {"tiles": row - 1}, row < tiles - 1, lambda: {"tiles": row + 1}),
        (col < cols * dates - 1, lambda: place(col + 1), col > 0, lambda: place(col - 1)),
        (col > 0, lambda: place(col - 1), col < cols * dates - 1, lambda: place(col + 1)),
    )

    def copy(d, i, source, device):
        return pltpu.make_async_remote_copy(
            src_ref=source.at[pieces[i]],
            dst_ref=landed.at[d, pieces[i]],
            send_sem=send_sem.at[d, i],
            recv_sem=recv_sem.at[d, i],
            device_id=device,
            device_id_type=pl.DeviceIdType.MESH,
        )

    barrier = pltpu.get_barrier_semaphore()
    for there, target, _, _ in links:

        @pl.when(there)
        def _(target=target):
            pl.semaphore_signal(
                barrier, inc=1, device_id=target(), device_id_type=pl.DeviceIdType.MESH
            )

    peers = sum(there.astype(jnp.int32) for there, _, _, _ in links)
    pl.semaphore_wait(barrier, peers)

    def send(d, i, source):
        there, target, _, _ = links[d]

        @pl.when(there)
        def _():
            copy(d, i, source, target()).start()

    def receive(d, i, source, into):
        _, _, there, origin = links[d]

        @pl.when(there)
        def _():
            copy(d, i, source, origin()).wait_recv()
            into[pieces[i]] += 0.5 * landed[d, pieces[i]]

    count = len(pieces)
    for i in range(count):
        send(0, i, own_ref)
        send(1, i, own_ref)
    for i in range(count):
        middle[pieces[i]] = own_ref[pieces[i]]
        receive(0, i, own_ref, middle)
        receive(1, i, own_ref, middle)
        send(2, i, middle)
        send(3, i, middle)
    for i in range(count):
        out_ref[pieces[i]] = middle[pieces[i]]
        receive(2, i, middle, out_ref)
        receive(3, i, middle, out_ref)
    for i in range(count):
        for d in range(4):
            there, target, _, _ = links[d]

            @pl.when(there)
            def _(d=d, i=i, target=target):
                copy(d, i, own_ref if d < 2 else middle, target()).wait_send()


def window(packed):
    shape = tuple(lax.axis_size(name) for name in ("tiles", "cols", "dates"))
    in_vmem = pl.BlockSpec(memory_space=pltpu.VMEM)
    return pl.pallas_call(
        functools.partial(window_kernel, shape),
        out_shape=jax.ShapeDtypeStruct(packed.shape, F32),
        in_specs=[in_vmem],
        out_specs=in_vmem,
        scratch_shapes=[
            pltpu.VMEM((4,) + packed.shape, F32),
            pltpu.VMEM(packed.shape, F32),
            pltpu.SemaphoreType.DMA((4, PIECES)),
            pltpu.SemaphoreType.DMA((4, PIECES)),
        ],
        compiler_params=pltpu.CompilerParams(
            collective_id=0,
            has_side_effects=True,
            vmem_limit_bytes=48 * 1024 * 1024,
        ),
        name="window",
    )(packed)


def on_device(imagery, pixel_mask, point_pixel, point_yield):
    whole = lax.all_to_all(imagery, "dates", split_axis=1, concat_axis=2, tiled=True)
    feats = whole[0, 0]
    pixels = feats.shape[1]
    index = point_pixel[0]
    yields = point_yield[0]
    mask = pixel_mask.reshape(pixels // LANES, LANES)
    weight, product = segments(index, yields, mask)
    packed = grams(feats, weight, product)
    packed = window(packed)
    fitted, spread, resid = solves(packed, feats, index, yields)
    return (fitted[None], spread[None], resid[None])


def step_rows(full, k):
    return 128 if k < full else 64


def payload_rows(full, k):
    return 128 * k + 64 + 8 if k < full else 48 * k + 24 + 8


def payload_starts(full):
    starts, at = [], 0
    for k in range(full + 1):
        starts.append(at)
        at += payload_rows(full, k)
    return starts, at


def pack_square(block):
    top, bottom = block[:64], block[64:]
    lane = lax.broadcasted_iota(jnp.int32, top.shape, 1)
    line = lax.broadcasted_iota(jnp.int32, top.shape, 0)
    packed = jnp.where(line >= lane - 64, bottom, pltpu.roll(top, 64, 1))
    diagonal = jnp.sum(jnp.where(line == lane, top, 0.0), 0, keepdims=True)
    return packed, diagonal


def unpack_square(packed, diagonal):
    lane = lax.broadcasted_iota(jnp.int32, packed.shape, 1)
    line = lax.broadcasted_iota(jnp.int32, packed.shape, 0)
    flipped = jnp.concatenate([packed, packed], 0).T
    corner = jnp.where(line < lane, pltpu.roll(packed, 64, 1), flipped[64:])
    corner = jnp.where(line == lane, diagonal, corner)
    top = jnp.where(lane < 64, corner, flipped[:64])
    bottom = jnp.where(line >= lane - 64, packed, flipped[64:])
    return jnp.concatenate([top, bottom], 0)


def fold(block):
    lane = lax.broadcasted_iota(jnp.int32, (24, LANES), 1)
    return jnp.where(lane < 64, block[:24], pltpu.roll(block[24:], 64, 1))


def unfold(block):
    lane = lax.broadcasted_iota(jnp.int32, (48, LANES), 1)
    both = jnp.concatenate([block, pltpu.roll(block, 64, 1)], 0)
    return jnp.where(lane < 64, both, 0.0)


def squeeze(block):
    return jnp.concatenate([block[0:24], block[32:56]], 0)


def stretch(block):
    gap = jnp.zeros((8, block.shape[1]), block.dtype)
    return jnp.concatenate([block[0:24], gap, block[24:48], gap], 0)


def factor8(small):
    line = lax.broadcasted_iota(jnp.int32, small.shape[1:], 0)
    lower = []
    pivots = jnp.zeros(small.shape[1:], F32)
    for p in range(0, 8, 2):
        one, two = line == p, line == p + 1
        first, second = small[p], small[p + 1]
        a, b, c = first[p : p + 1], second[p : p + 1], second[p + 1 : p + 2]
        det = a * c - b * b
        ra = 1.0 / a
        t = b * ra
        pivots = jnp.where(one, a, jnp.where(two, det * ra, pivots))
        lower = [
            jnp.where(
                one,
                small[j],
                jnp.where(two, small[j] - t * small[j][p : p + 1], lower[j]),
            )
            for j in range(p)
        ]
        lower.append(jnp.where(one, 1.0, jnp.where(two, -t, 0.0)))
        lower.append(jnp.where(two, 1.0, 0.0))
        r = 1.0 / det
        ea, eb, ec = c * r, -b * r, a * r
        left = first * ea + second * eb
        right = first * eb + second * ec
        left = jnp.where(one, -ea, jnp.where(two, -eb, left))
        right = jnp.where(one, -eb, jnp.where(two, -ec, right))
        base = jnp.where((one | two)[None], 0.0, small)
        rest = base - (
            left[None] * small[:, p : p + 1] + right[None] * small[:, p + 1 : p + 2]
        )
        parts = [rest[:p]] if p else []
        parts.append(jnp.stack([-left, -right]))
        if p < 6:
            parts.append(rest[p + 2 :])
        small = jnp.concatenate(parts, 0)
    return small, lower, lax.rsqrt(pivots)


def mix(planes, lines):
    terms = [planes[j] * lines[j : j + 1] for j in range(8)]
    while len(terms) > 1:
        terms = [a + b for a, b in zip(terms[::2], terms[1::2])]
    return terms[0]


def block_factor(block, groups, midway=None):
    rows = block.shape[0]
    lane = lax.broadcasted_iota(jnp.int32, (8, LANES), 1)
    line = lax.broadcasted_iota(jnp.int32, (8, LANES), 0)
    result = [jnp.zeros((8, LANES), F32)] * (rows // 8)
    below, first = block, 0
    for g in groups:
        if midway is not None and g == 12:
            midway()
        k = 8 * g
        below = below[k - first :]
        top = below[:8]
        small = jnp.stack(
            [jnp.broadcast_to(top[:, k + j : k + j + 1], (8, LANES)) for j in range(8)]
        )
        small, lower, root = factor8(small)
        inside = (lane >= k) & (lane < k + 8)
        top = jnp.where(inside, jnp.where(lane == line + k, 1.0, 0.0), top)
        result[g] = jnp.where(lane < k + 8, mix(lower, top) * root, 0.0)
        below = below[8:]
        first = k + 8
        if below.shape[0]:
            new = mix(small, top)
            cols = [below[:, k + j : k + j + 1] for j in range(8)]
            keep = (lane[:1] < k) | (lane[:1] >= k + 8)
            below = jnp.where(keep, below, 0.0)
            for j in range(0, 8, 2):
                below = below - (
                    cols[j] * new[j : j + 1] + cols[j + 1] * new[j + 1 : j + 2]
                )
    return jnp.concatenate(result, 0)


def split2(x):
    high = x.astype(BF16)
    return high, (x - high.astype(F32)).astype(BF16)


def fused_kernel(
    tiles,
    img,
    index_hbm,
    yield_hbm,
    mask_hbm,
    fit,
    spread_ref,
    index_out,
    yield_out,
    feats,
    whole,
    tail,
    tail_in,
    index_ref,
    yield_ref,
    mask_ref,
    weight_rows,
    product_rows,
    acc,
    own,
    middle,
    outgoing,
    landed,
    inverse,
    split_r,
    rhs_ref,
    z_ref,
    fit8,
    spread8,
    local_sem,
    bulk_send,
    bulk_recv,
    z_send,
    z_recv,
    core_send,
    core_recv,
    x_send,
    x_recv,
):
    half, pixels = img.shape[2:]
    full = half // 64
    steps = full + 1
    rows = pixels // LANES
    scale = 1.0 / pixels
    starts, _ = payload_starts(full)
    mesh_ids = pl.DeviceIdType.MESH

    z = lax.axis_index("tiles")
    c = lax.axis_index("cols")
    d = lax.axis_index("dates")
    across = {"dates": 1 - d}
    core = {"cols": 1 - c}
    up, down = {"tiles": z + 1}, {"tiles": z - 1}
    has_up, has_down = z < tiles - 1, z > 0
    joins = c == d

    def place(k, s):
        if k < full:
            return pl.multiple_of(128 * k + 64 * s, 16)
        return pl.multiple_of(128 * full + 32 * s, 16)

    height = [64] * full + [16]
    source_at = [64 * k for k in range(steps)]

    local = [
        pltpu.make_async_copy(index_hbm.at[0], index_ref, local_sem.at[0]),
        pltpu.make_async_copy(yield_hbm.at[0], yield_ref, local_sem.at[1]),
        pltpu.make_async_copy(mask_hbm, mask_ref, local_sem.at[2]),
        pltpu.make_async_copy(img.at[0], whole, local_sem.at[3]),
    ]
    for k in range(steps):
        local.append(
            pltpu.make_async_copy(
                img.at[0, d, pl.ds(source_at[k], height[k])],
                feats.at[pl.ds(place(k, d), height[k])],
                local_sem.at[4 + k],
            )
        )
    for copy in local:
        copy.start()

    barrier = pltpu.get_barrier_semaphore()
    peers = ((has_up, up), (has_down, down), (None, core), (None, across))
    for there, target in peers:

        def greet(target=target):
            pl.semaphore_signal(
                barrier, inc=1, device_id=target, device_id_type=mesh_ids
            )

        if there is None:
            greet()
        else:
            pl.when(there)(greet)
    pl.semaphore_wait(barrier, 2 + has_up.astype(jnp.int32) + has_down.astype(jnp.int32))

    bulk = []
    for k in range(steps):
        bulk.append(
            pltpu.make_async_remote_copy(
                src_ref=img.at[0, 1 - d, pl.ds(source_at[k], height[k])],
                dst_ref=feats.at[pl.ds(place(k, d), height[k])],
                send_sem=bulk_send.at[k],
                recv_sem=bulk_recv.at[k],
                device_id=across,
                device_id_type=mesh_ids,
            )
        )
    bulk.append(
        pltpu.make_async_remote_copy(
            src_ref=tail,
            dst_ref=tail_in,
            send_sem=bulk_send.at[steps],
            recv_sem=bulk_recv.at[steps],
            device_id=across,
            device_id_type=mesh_ids,
        )
    )
    bulk[0].start()
    bulk[1].start()

    for copy in local[:4]:
        copy.wait()
    end = whole[1 - d][half - 8 : half]
    tail[...] = jnp.concatenate([end[:, : pixels // 2], end[:, pixels // 2 :]], 0)

    def put_tail(s, end):
        at = pl.ds(pl.multiple_of(128 * full + 32 * s + 16, 16), 16)
        feats[at, :] = jnp.concatenate([end, jnp.zeros_like(end)], 0)

    put_tail(d, whole[d][half - 8 : half])

    high, low = one_hots(index_ref[...], rows)
    low = jnp.where(low, 1.0, 0.0).astype(BF16)
    index_out[...] = index_ref[...]
    yield_out[...] = yield_ref[...]
    parts = [jnp.where(high, 1.0, 0.0).astype(BF16)]
    for piece in split3(yield_ref[...]):
        parts.append(jnp.where(high, piece.astype(F32), 0.0).astype(BF16))
    sums = lax.dot_general(
        jnp.concatenate(parts, 0), low, NT, preferred_element_type=F32
    )
    counts = sums[:rows]
    totals = sums[rows : 2 * rows] + sums[2 * rows : 3 * rows] + sums[3 * rows :]
    weight = jnp.where(counts > 0, mask_ref[...].astype(F32), 0.0)
    product = weight * (totals / jnp.maximum(counts, 1.0))
    pa, pb, pc = (p.astype(F32) for p in split3(product))
    line16 = lax.broadcasted_iota(jnp.int32, (16, LANES), 0)
    for r in range(rows):
        at = slice(r * LANES, (r + 1) * LANES)
        weight_rows[:, at] = jnp.broadcast_to(weight[r : r + 1], (16, LANES)).astype(BF16)
        extra = jnp.where(
            line16 == 0,
            pa[r : r + 1],
            jnp.where(
                line16 == 1,
                pb[r : r + 1],
                jnp.where(line16 == 2, pc[r : r + 1], 0.0),
            ),
        )
        product_rows[:, at] = extra.astype(BF16)

    acc[...] = jnp.zeros_like(acc)
    inverse[...] = jnp.zeros_like(inverse)
    fit8[...] = jnp.zeros_like(fit8)
    spread8[...] = jnp.zeros_like(spread8)

    def payload(k, h):
        count = payload_rows(full, k)
        first = count // 16 * 8
        if h == 0:
            return pl.ds(starts[k], first)
        return pl.ds(starts[k] + first, count - first)

    def z_copy(way, k, h, target):
        return pltpu.make_async_remote_copy(
            src_ref=own.at[payload(k, h)],
            dst_ref=landed.at[way, payload(k, h)],
            send_sem=z_send.at[way, 2 * k + h],
            recv_sem=z_recv.at[way, 2 * k + h],
            device_id=target,
            device_id_type=mesh_ids,
        )

    def core_copy(k, h):
        return pltpu.make_async_remote_copy(
            src_ref=middle.at[payload(k, h)],
            dst_ref=landed.at[2, payload(k, h)],
            send_sem=core_send.at[2 * k + h],
            recv_sem=core_recv.at[2 * k + h],
            device_id=core,
            device_id_type=mesh_ids,
        )

    def x_copy(k, h, source=outgoing):
        return pltpu.make_async_remote_copy(
            src_ref=source.at[payload(k, h)],
            dst_ref=landed.at[3, payload(k, h)],
            send_sem=x_send.at[2 * k + h],
            recv_sem=x_recv.at[2 * k + h],
            device_id=across,
            device_id_type=mesh_ids,
        )

    def gram(k):
        count = step_rows(full, k)
        base, end = 128 * k, 128 * k + count
        local[4 + k].wait()
        bulk[k].wait_recv()
        if k == full:
            bulk[steps].wait_recv()
            folded = tail_in[...]
            put_tail(1 - d, jnp.concatenate([folded[:8], folded[8:]], 1))
        wide = count + 16
        acc[:end, :wide] = jnp.zeros((end, wide), F32)

        def chunk(i, _):
            at = pl.ds(pl.multiple_of(i * SPAN, SPAN), SPAN)
            weights = jnp.concatenate([weight_rows[:, at]] * (count // 16), 0)
            left = jnp.concatenate(
                [feats[base:end, at] * weights, product_rows[:, at]], 0
            )
            acc[:end, :wide] += lax.dot_general(
                feats[:end, at], left, NT, preferred_element_type=F32
            )
            return 0

        lax.fori_loop(0, pixels // SPAN, chunk, 0)
        at = starts[k]
        diagonal = jnp.zeros((1, LANES), F32)
        for j in range(k + 1):
            block = acc[128 * j : 128 * j + 128, :LANES]
            if k == full:
                block = squeeze(block.T)
            if j == k and k < full:
                block, diagonal = pack_square(block)
            if j == k and k == full:
                block = fold(block)
            own[at : at + block.shape[0]] = block
            at += block.shape[0]
        moment = acc[base : base + 128, count : count + 1]
        moment = moment + acc[base : base + 128, count + 1 : count + 2]
        moment = moment + acc[base : base + 128, count + 2 : count + 3]
        moment = jnp.broadcast_to(moment, (LANES, LANES)).T
        line8 = lax.broadcasted_iota(jnp.int32, (8, LANES), 0)
        own[at : at + 8] = jnp.where(line8 == 0, moment[:8], diagonal)
        for h in range(2):
            pl.when(has_up)(lambda h=h: z_copy(0, k, h, up).start())
            pl.when(has_down)(lambda h=h: z_copy(1, k, h, down).start())

    def z_join(k):
        for h in range(2):
            at = payload(k, h)

            @pl.when(has_down)
            def _(h=h, at=at):
                z_copy(0, k, h, down).wait_recv()
                middle[at] = own[at] + 0.5 * landed[0, at]

            @pl.when(jnp.logical_not(has_down))
            def _(at=at):
                middle[at] = own[at]

            @pl.when(has_up)
            def _(h=h, at=at):
                z_copy(1, k, h, up).wait_recv()
                middle[at] += 0.5 * landed[1, at]

            @pl.when(jnp.logical_not(joins))
            def _(h=h):
                core_copy(k, h).start()
                x_copy(k, h, middle).start()

        @pl.when(joins)
        def _():
            for h in range(2):
                at = payload(k, h)
                core_copy(k, h).wait_recv()
                outgoing[at] = middle[at] + landed[2, at]
                x_copy(k, h).start()

        if k + 2 < steps:
            bulk[k + 2].start()
        if k + 2 == full:
            bulk[steps].start()

    def solve(k, midway=None):
        at = pl.ds(starts[k], payload_rows(full, k))
        for h in range(2):
            x_copy(k, h).wait_recv()
        count = step_rows(full, k)
        base = 128 * k
        window = (middle[at] + 0.5 * landed[3, at]) * scale
        step = 128 if k < full else 48
        blocks = [window[j * step : (j + 1) * step] for j in range(k)]
        ends = window[payload_rows(full, k) - 8 :]
        rhs_ref[:, base : base + 128] = ends
        square = window[k * step : payload_rows(full, k) - 8]
        if k < full:
            blocks.append(unpack_square(square, ends[1:2]))
        else:
            blocks.append(unfold(square))
            blocks = [stretch(block) for block in blocks]
        lane = lax.broadcasted_iota(jnp.int32, (count, LANES), 1)
        line = lax.broadcasted_iota(jnp.int32, (count, LANES), 0)
        pivot = blocks[k] + jnp.where(lane == line, ridge_term, 0.0)
        if k:
            known = inverse[:base, :base]
            if k < full:
                raised = dot32(known, jnp.concatenate(blocks[:k], 0))
                factor = jnp.concatenate(
                    [raised[128 * j : 128 * j + 128].T for j in range(k)], 1
                )
                drop = dot32(factor, raised)
            else:
                factor = dot32(jnp.concatenate(blocks[:k], 1), known, NT)
                drop = dot32(factor, factor, NT)
            coupling = dot32(factor, known)
            if count < LANES:
                drop = jnp.concatenate(
                    [drop, jnp.zeros((count, LANES - count), F32)], 1
                )
            pivot = pivot - drop
        groups = range(16) if k < full else (0, 1, 2, 4, 5, 6)
        lower = block_factor(pivot, groups, midway)
        if k:
            lower = jnp.concatenate([-dot32(lower[:, :count], coupling), lower], 1)
        row = 128 if k == full else 0
        low_at = (192 if k >= full - 1 else count) + row
        z_ref[row : row + count] = jnp.sum(
            lower * rhs_ref[:1, : base + 128], 1, keepdims=True
        )
        high, low = split2(lower)
        split_r[row : row + count, : base + 128] = high
        split_r[low_at : low_at + count, : base + 128] = low
        if k == full - 1:
            gap = jnp.zeros((count, 128), BF16)
            split_r[:count, base + 128 :] = gap
            split_r[low_at : low_at + count, base + 128 :] = gap
        if k < full:
            inverse[base : base + count, : base + 128] = lower

    def spread(k):
        count = step_rows(full, k)
        end = 128 * k + count
        last = k == full
        if last:
            count = 192

        def chunk(i, _):
            at = pl.ds(pl.multiple_of(i * SPAN, SPAN), SPAN)
            part = feats[:end, at]
            both = jnp.dot(
                split_r[: 2 * count, :end], part, preferred_element_type=F32
            )
            value = both[:count] + both[count:]
            square = (value * value).reshape(count // 8, 8, SPAN)
            linear = (value * z_ref[:count]).reshape(count // 8, 8, SPAN)
            square = spread8[:, at] + jnp.sum(square, 0)
            linear = fit8[:, at] + jnp.sum(linear, 0)
            if last:
                spread_ref[:, at] = jnp.sum(square, 0, keepdims=True) / (2 * half)
                fitted = jnp.sum(linear, 0, keepdims=True)
                for s in range(SPAN // LANES):
                    fit[pl.ds(i * (SPAN // LANES) + s, 1), :] = fitted[
                        :, s * LANES : (s + 1) * LANES
                    ]
            else:
                spread8[:, at] = square
                fit8[:, at] = linear
            return 0

        lax.fori_loop(0, pixels // SPAN, chunk, 0)

    gram(0)
    z_join(0)
    for k in range(1, steps):
        gram(k)
        if k == full:
            spread(k - 2)
        solve(k - 1, lambda k=k: z_join(k))
        if k == 1:
            spread(k - 1)
    solve(full)
    spread(full)

    for copy in bulk:
        copy.wait_send()
    for k in range(steps):
        for h in range(2):
            pl.when(has_up)(lambda k=k, h=h: z_copy(0, k, h, up).wait_send())
            pl.when(has_down)(lambda k=k, h=h: z_copy(1, k, h, down).wait_send())
            pl.when(jnp.logical_not(joins))(
                lambda k=k, h=h: core_copy(k, h).wait_send()
            )
            x_copy(k, h).wait_send()


def fused(imagery, index, yields, mask):
    half, pixels = imagery.shape[2:]
    full = half // 64
    steps = full + 1
    rows = payload_starts(full)[1]
    size = 128 * steps
    shape = jax.ShapeDtypeStruct((1, pixels), F32)
    in_hbm = pl.BlockSpec(memory_space=pltpu.HBM)
    in_vmem = pl.BlockSpec(memory_space=pltpu.VMEM)
    dma = pltpu.SemaphoreType.DMA
    return pl.pallas_call(
        functools.partial(fused_kernel, lax.axis_size("tiles")),
        out_shape=(
            pltpu.VMEM((pixels // LANES, LANES), F32),
            pltpu.VMEM((1, pixels), F32),
            pltpu.VMEM((1, pixels), jnp.int32),
            pltpu.VMEM((1, pixels), F32),
        ),
        in_specs=[in_hbm] * 4,
        out_specs=(in_vmem,) * 4,
        scratch_shapes=[
            pltpu.VMEM((128 * full + 64, pixels), BF16),
            pltpu.VMEM((2, half, pixels), BF16),
            pltpu.VMEM((16, pixels // 2), BF16),
            pltpu.VMEM((16, pixels // 2), BF16),
            pltpu.VMEM((1, pixels), jnp.int32),
            pltpu.VMEM((1, pixels), F32),
            pltpu.VMEM((pixels // LANES, LANES), jnp.int32),
            pltpu.VMEM((16, pixels), BF16),
            pltpu.VMEM((16, pixels), BF16),
            pltpu.VMEM((size, 2 * LANES), F32),
            pltpu.VMEM((rows, LANES), F32),
            pltpu.VMEM((rows, LANES), F32),
            pltpu.VMEM((rows, LANES), F32),
            pltpu.VMEM((4, rows, LANES), F32),
            pltpu.VMEM((size, size), F32),
            pltpu.VMEM((3 * LANES, size), BF16),
            pltpu.VMEM((8, size), F32),
            pltpu.VMEM((192, 1), F32),
            pltpu.VMEM((8, pixels), F32),
            pltpu.VMEM((8, pixels), F32),
            dma((4 + steps,)),
            dma((steps + 1,)),
            dma((steps + 1,)),
            dma((2, 2 * steps)),
            dma((2, 2 * steps)),
            dma((2 * steps,)),
            dma((2 * steps,)),
            dma((2 * steps,)),
            dma((2 * steps,)),
        ],
        compiler_params=pltpu.CompilerParams(
            collective_id=1,
            has_side_effects=True,
            vmem_limit_bytes=56 * 1024 * 1024,
        ),
        name="fused",
    )(imagery, index, yields, mask)


def finish_kernel(
    fit_ref, spread_in, index_ref, yield_ref, fitted_ref, spread_ref, resid_ref
):
    rows = fit_ref.shape[0]
    fit = fit_ref[...]
    high, low = one_hots(index_ref[...], rows)
    low = jnp.where(low, 1.0, 0.0).astype(BF16)
    table = jnp.concatenate(split3(fit), 0)
    found = jnp.dot(table, low, preferred_element_type=F32)
    found = found[:rows] + (found[rows : 2 * rows] + found[2 * rows :])
    value = jnp.sum(jnp.where(high, found, 0.0), 0, keepdims=True)
    resid_ref[...] = yield_ref[...] - value
    for r in range(rows):
        fitted_ref[:, r * LANES : (r + 1) * LANES] = fit[r : r + 1]
    spread_ref[...] = spread_in[...]


def finish(fit, spread, index, yields):
    shape = jax.ShapeDtypeStruct(spread.shape, F32)
    return pl.pallas_call(
        finish_kernel,
        out_shape=(shape, shape, shape),
        compiler_params=pltpu.CompilerParams(vmem_limit_bytes=16 * 1024 * 1024),
        name="finish",
    )(fit, spread, index, yields)


def on_device_fused(imagery, pixel_mask, point_pixel, point_yield):
    pixels = imagery.shape[3]
    mask = pixel_mask.reshape(pixels // LANES, LANES)
    fitted, spread, resid = finish(*fused(imagery, point_pixel, point_yield, mask))
    return (fitted[None], spread[None], resid[None])


def solution(mesh):
    features = P(("groups", "tiles"), "cols", "dates", None)
    points = P(("groups", "tiles"), ("cols", "dates"), None)
    sizes = dict(mesh.shape)

    def body(imagery, pixel_mask, point_pixel, point_yield):
        pairs = sizes["cols"] == 2 and sizes["dates"] == 2
        one_tile = imagery.shape[:2] == (1, 2)
        if pairs and one_tile and imagery.shape[2] % 64 == 24:
            run = on_device_fused
        else:
            run = on_device
        return run(imagery, pixel_mask, point_pixel, point_yield)

    return jax.shard_map(
        body,
        mesh=mesh,
        in_specs=(features, points, points, points),
        out_specs=(points, points, points),
        check_vma=False,
    )
```

```python
import functools

import jax
import jax.numpy as jnp
from jax import lax
from jax.experimental import pallas as pl
from jax.experimental.pallas import tpu as pltpu
from jax.sharding import PartitionSpec as P

ridge_term = 0.05
LANES = 128
CHUNK = 512
PIECES = 8
SPAN = 4096
F32 = jnp.float32
BF16 = jnp.bfloat16
NT = (((1,), (1,)), ((), ()))


def split3(x):
    a = x.astype(BF16)
    rest = x - a.astype(F32)
    b = rest.astype(BF16)
    c = (rest - b.astype(F32)).astype(BF16)
    return a, b, c


def one_hots(index, rows):
    points = index.shape[1]
    high = lax.broadcasted_iota(jnp.int32, (rows, points), 0) == index // LANES
    low = lax.broadcasted_iota(jnp.int32, (LANES, points), 0) == index % LANES
    return high, low


def segment_kernel(index_ref, yield_ref, mask_ref, weight_ref, product_ref):
    rows = mask_ref.shape[0]
    high, low = one_hots(index_ref[...], rows)
    low = jnp.where(low, 1.0, 0.0).astype(BF16)
    pieces = [jnp.where(high, 1.0, 0.0).astype(BF16)]
    for piece in split3(yield_ref[...]):
        pieces.append(jnp.where(high, piece.astype(F32), 0.0).astype(BF16))
    sums = lax.dot_general(
        jnp.concatenate(pieces, 0), low, NT, preferred_element_type=F32
    )
    counts = sums[:rows]
    totals = sums[rows : 2 * rows] + sums[2 * rows : 3 * rows] + sums[3 * rows :]
    weight = jnp.where(counts > 0, mask_ref[...].astype(F32), 0.0)
    weight_ref[...] = weight
    product_ref[...] = weight * (totals / jnp.maximum(counts, 1.0))


def bands(width):
    blocks, offset = [], 0
    for i in range(pl.cdiv(width, LANES)):
        height = min(LANES, width - i * LANES)
        for j in range(i + 1):
            blocks.append((i, j, height, offset))
            offset += height
    return blocks, offset


def gram_kernel(feats_ref, weight_ref, product_ref, out_ref, acc):
    width, pixels = feats_ref.shape
    acc[...] = jnp.zeros_like(acc)

    def step(c, _):
        at = pl.multiple_of(c * CHUNK, CHUNK)
        feats = feats_ref[:, pl.ds(at, CHUNK)]
        left = []
        for s in range(CHUNK // LANES):
            row = pl.ds(c * (CHUNK // LANES) + s, 1)
            part = feats[:, s * LANES : (s + 1) * LANES]
            scaled = part * weight_ref[row, :].astype(BF16)
            a, b, d = (p.astype(F32) for p in split3(product_ref[row, :]))
            line = lax.broadcasted_iota(jnp.int32, (16, LANES), 0)
            extra = jnp.where(
                line == 0, a, jnp.where(line == 1, b, jnp.where(line == 2, d, 0.0))
            )
            left.append(jnp.concatenate([scaled, extra.astype(BF16)], 0))
        acc[...] += lax.dot_general(
            jnp.concatenate(left, 1), feats, NT, preferred_element_type=F32
        )
        return 0

    lax.fori_loop(0, pixels // CHUNK, step, 0)
    blocks, offset = bands(width)
    out_ref[...] = jnp.zeros_like(out_ref)
    for i, j, height, at in blocks:
        wide = min(LANES, width - j * LANES)
        out_ref[at : at + height, :wide] = acc[
            i * LANES : i * LANES + height, j * LANES : j * LANES + wide
        ]
    moment = acc[width : width + 1] + acc[width + 1 : width + 2]
    moment = moment + acc[width + 2 : width + 3]
    for j in range(pl.cdiv(width, LANES)):
        wide = min(LANES, width - j * LANES)
        out_ref[offset + j : offset + j + 1, :wide] = moment[
            :, j * LANES : j * LANES + wide
        ]


def small_inverse(p):
    n = len(p)
    for k in range(n):
        d = 1.0 / p[k][k]
        row = [d if j == k else p[k][j] * d for j in range(n)]
        new = []
        for i in range(n):
            if i == k:
                new.append(row)
            else:
                new.append(
                    [
                        -p[i][k] * d if j == k else p[i][j] - p[i][k] * row[j]
                        for j in range(n)
                    ]
                )
        p = new
    return p


def block_inverse(block, pivots, group=8):
    tiles = [block[8 * g : 8 * g + 8] for g in range(LANES // 8)]
    lane = lax.broadcasted_iota(jnp.int32, (8, LANES), 1)
    line = lax.broadcasted_iota(jnp.int32, (8, LANES), 0)
    for k in range(0, pivots, group):
        g, r = divmod(k, 8)
        cols = [
            [
                jnp.broadcast_to(t[:, k + j : k + j + 1], (8, LANES))
                for t in tiles
            ]
            for j in range(group)
        ]
        small = [
            [cols[j][g][r + i : r + i + 1] for j in range(group)]
            for i in range(group)
        ]
        small = small_inverse(small)
        rows = []
        for i in range(group):
            old = tiles[g][r + i : r + i + 1]
            old = jnp.where((lane[:1] >= k) & (lane[:1] < k + group), 0.0, old)
            rows.append(jnp.where(lane[:1] == k + i, 1.0, old))
        new_rows = []
        for i in range(group):
            total = small[i][0] * rows[0]
            for j in range(1, group):
                total = total + small[i][j] * rows[j]
            new_rows.append(jnp.broadcast_to(total, (8, LANES)))
        keep = (lane < k) | (lane >= k + group)
        for t in range(LANES // 8):
            value = jnp.where(keep, tiles[t], 0.0)
            for j in range(group):
                value = value - cols[j][t] * new_rows[j]
            if t == g:
                for i in range(group):
                    value = jnp.where(line == r + i, new_rows[i], value)
            tiles[t] = value
    return jnp.concatenate(tiles, 0)


NN = (((1,), (0,)), ((), ()))


def dot32(a, b, dims=NN):
    return lax.dot_general(
        a, b, dims, precision=lax.Precision.HIGHEST, preferred_element_type=F32
    )


def solve_kernel(
    packed_ref,
    feats_ref,
    index_ref,
    yield_ref,
    fitted_ref,
    spread_ref,
    resid_ref,
    system,
    base,
    high_ref,
    low_ref,
    fit,
):
    width, pixels = feats_ref.shape
    count = pl.cdiv(width, LANES)
    size = count * LANES
    blocks, offset = bands(width)
    scale = 1.0 / pixels
    line = lax.broadcasted_iota(jnp.int32, (LANES, LANES), 0)
    lane = lax.broadcasted_iota(jnp.int32, (LANES, LANES), 1)
    for i, j, height, at in blocks:
        value = packed_ref[at : at + height] * scale
        if height < LANES:
            value = jnp.concatenate(
                [value, jnp.zeros((LANES - height, LANES), F32)], 0
            )
        if i == j:
            diagonal = jnp.where(line < height, ridge_term, 1.0)
            value = value + jnp.where(line == lane, diagonal, 0.0)
        system[i * LANES : (i + 1) * LANES, j * LANES : (j + 1) * LANES] = value
        if i != j:
            system[j * LANES : (j + 1) * LANES, i * LANES : (i + 1) * LANES] = value.T

    base[...] = system[...]
    column = lax.broadcasted_iota(jnp.int32, (LANES, size), 1)
    wide_line = lax.broadcasted_iota(jnp.int32, (LANES, size), 0)

    def eliminate(k, pivots):
        at = k * LANES if isinstance(k, int) else pl.multiple_of(k * LANES, LANES)
        here = pl.ds(at, LANES)
        inverse = block_inverse(system[here, here], pivots)
        inside = (column >= at) & (column < at + LANES)
        unit = jnp.where(column == wide_line + at, 1.0, 0.0)
        right = dot32(inverse, jnp.where(inside, unit, system[here, :]))
        left = system[:, here]
        system[:, here] = jnp.zeros_like(left)
        system[...] -= dot32(left, right)
        system[here, :] = right

    full = width // LANES

    def body(k, _):
        eliminate(k, LANES)
        return 0

    lax.fori_loop(0, full, body, 0)
    if width % LANES:
        eliminate(full, width % LANES)

    rhs = jnp.concatenate(
        [packed_ref[offset + j : offset + j + 1] for j in range(count)], 1
    )
    rhs = jnp.broadcast_to(rhs * scale, (8, size))
    beta = dot32(rhs, system[...])
    beta = beta + dot32(rhs - dot32(beta, base[...]), system[...])
    beta = beta[:1, :width]
    inverse = system[:width, :width]
    upper = inverse.astype(BF16)
    a, b, d = (p.astype(F32) for p in split3(beta))
    row16 = lax.broadcasted_iota(jnp.int32, (16, width), 0)
    extra = jnp.where(row16 == 0, a, jnp.where(row16 == 1, b, jnp.where(row16 == 2, d, 0.0)))
    high_ref[...] = jnp.concatenate([upper, extra.astype(BF16)], 0)
    low_ref[...] = (inverse - upper.astype(F32)).astype(BF16)

    def step(c, _):
        at = pl.multiple_of(c * CHUNK, CHUNK)
        feats = feats_ref[:, pl.ds(at, CHUNK)]
        first = jnp.dot(high_ref[...], feats, preferred_element_type=F32)
        second = jnp.dot(low_ref[...], feats, preferred_element_type=F32)
        total = (first[:width] + second) * feats.astype(F32)
        spread_ref[:, pl.ds(at, CHUNK)] = jnp.sum(total, 0, keepdims=True) / width
        fitted = first[width : width + 1] + (
            first[width + 1 : width + 2] + first[width + 2 : width + 3]
        )
        fitted_ref[:, pl.ds(at, CHUNK)] = fitted
        for s in range(CHUNK // LANES):
            fit[pl.ds(c * (CHUNK // LANES) + s, 1), :] = fitted[
                :, s * LANES : (s + 1) * LANES
            ]
        return 0

    lax.fori_loop(0, pixels // CHUNK, step, 0)

    rows = pixels // LANES
    high, low = one_hots(index_ref[...], rows)
    low = jnp.where(low, 1.0, 0.0).astype(BF16)
    table = jnp.concatenate(split3(fit[...]), 0)
    found = jnp.dot(table, low, preferred_element_type=F32)
    found = found[:rows] + (found[rows : 2 * rows] + found[2 * rows :])
    value = jnp.sum(jnp.where(high, found, 0.0), 0, keepdims=True)
    resid_ref[...] = yield_ref[...] - value


PARAMS = pltpu.CompilerParams(vmem_limit_bytes=48 * 1024 * 1024)


def segments(index, yields, mask):
    shape = jax.ShapeDtypeStruct(mask.shape, F32)
    return pl.pallas_call(
        segment_kernel,
        out_shape=(shape, shape),
        compiler_params=PARAMS,
        cost_estimate=pl.CostEstimate(
            flops=2 * 128 * 128 * index.shape[1],
            bytes_accessed=16 * index.shape[1],
            transcendentals=0,
        ),
        name="segments",
    )(index, yields, mask)


def grams(feats, weight, product):
    width, pixels = feats.shape
    rows = bands(width)[1] + 8 * pl.cdiv(pl.cdiv(width, LANES), 8)
    return pl.pallas_call(
        gram_kernel,
        out_shape=jax.ShapeDtypeStruct((rows, LANES), F32),
        scratch_shapes=[pltpu.VMEM((width + 16, width), F32)],
        compiler_params=PARAMS,
        name="grams",
    )(feats, weight, product)


def solves(packed, feats, index, yields):
    width, pixels = feats.shape
    size = pl.cdiv(width, LANES) * LANES
    shape = jax.ShapeDtypeStruct((1, pixels), F32)
    return pl.pallas_call(
        solve_kernel,
        out_shape=(shape, shape, jax.ShapeDtypeStruct(yields.shape, F32)),
        scratch_shapes=[
            pltpu.VMEM((size, size), F32),
            pltpu.VMEM((size, size), F32),
            pltpu.VMEM((width + 16, width), BF16),
            pltpu.VMEM((width, width), BF16),
            pltpu.VMEM((pixels // LANES, LANES), F32),
        ],
        compiler_params=PARAMS,
        name="solves",
    )(packed, feats, index, yields)


def window_kernel(shape, own_ref, out_ref, landed, middle, send_sem, recv_sem):
    tiles, cols, dates = shape
    row = lax.axis_index("tiles")
    col = lax.axis_index("cols") * dates + lax.axis_index("dates")
    total = own_ref.shape[0]
    step = -(-total // (8 * PIECES)) * 8
    pieces = [pl.ds(at, min(step, total - at)) for at in range(0, total, step)]

    def place(c):
        return {"cols": c // dates, "dates": c % dates}

    links = (
        (row < tiles - 1, lambda: {"tiles": row + 1}, row > 0, lambda: {"tiles": row - 1}),
        (row > 0, lambda: {"tiles": row - 1}, row < tiles - 1, lambda: {"tiles": row + 1}),
        (col < cols * dates - 1, lambda: place(col + 1), col > 0, lambda: place(col - 1)),
        (col > 0, lambda: place(col - 1), col < cols * dates - 1, lambda: place(col + 1)),
    )

    def copy(d, i, source, device):
        return pltpu.make_async_remote_copy(
            src_ref=source.at[pieces[i]],
            dst_ref=landed.at[d, pieces[i]],
            send_sem=send_sem.at[d, i],
            recv_sem=recv_sem.at[d, i],
            device_id=device,
            device_id_type=pl.DeviceIdType.MESH,
        )

    barrier = pltpu.get_barrier_semaphore()
    for there, target, _, _ in links:

        @pl.when(there)
        def _(target=target):
            pl.semaphore_signal(
                barrier, inc=1, device_id=target(), device_id_type=pl.DeviceIdType.MESH
            )

    peers = sum(there.astype(jnp.int32) for there, _, _, _ in links)
    pl.semaphore_wait(barrier, peers)

    def send(d, i, source):
        there, target, _, _ = links[d]

        @pl.when(there)
        def _():
            copy(d, i, source, target()).start()

    def receive(d, i, source, into):
        _, _, there, origin = links[d]

        @pl.when(there)
        def _():
            copy(d, i, source, origin()).wait_recv()
            into[pieces[i]] += 0.5 * landed[d, pieces[i]]

    count = len(pieces)
    for i in range(count):
        send(0, i, own_ref)
        send(1, i, own_ref)
    for i in range(count):
        middle[pieces[i]] = own_ref[pieces[i]]
        receive(0, i, own_ref, middle)
        receive(1, i, own_ref, middle)
        send(2, i, middle)
        send(3, i, middle)
    for i in range(count):
        out_ref[pieces[i]] = middle[pieces[i]]
        receive(2, i, middle, out_ref)
        receive(3, i, middle, out_ref)
    for i in range(count):
        for d in range(4):
            there, target, _, _ = links[d]

            @pl.when(there)
            def _(d=d, i=i, target=target):
                copy(d, i, own_ref if d < 2 else middle, target()).wait_send()


def window(packed):
    shape = tuple(lax.axis_size(name) for name in ("tiles", "cols", "dates"))
    in_vmem = pl.BlockSpec(memory_space=pltpu.VMEM)
    return pl.pallas_call(
        functools.partial(window_kernel, shape),
        out_shape=jax.ShapeDtypeStruct(packed.shape, F32),
        in_specs=[in_vmem],
        out_specs=in_vmem,
        scratch_shapes=[
            pltpu.VMEM((4,) + packed.shape, F32),
            pltpu.VMEM(packed.shape, F32),
            pltpu.SemaphoreType.DMA((4, PIECES)),
            pltpu.SemaphoreType.DMA((4, PIECES)),
        ],
        compiler_params=pltpu.CompilerParams(
            collective_id=0,
            has_side_effects=True,
            vmem_limit_bytes=48 * 1024 * 1024,
        ),
        name="window",
    )(packed)


def on_device(imagery, pixel_mask, point_pixel, point_yield):
    whole = lax.all_to_all(imagery, "dates", split_axis=1, concat_axis=2, tiled=True)
    feats = whole[0, 0]
    pixels = feats.shape[1]
    index = point_pixel[0]
    yields = point_yield[0]
    mask = pixel_mask.reshape(pixels // LANES, LANES)
    weight, product = segments(index, yields, mask)
    packed = grams(feats, weight, product)
    packed = window(packed)
    fitted, spread, resid = solves(packed, feats, index, yields)
    return (fitted[None], spread[None], resid[None])


def step_rows(full, k):
    return 128 if k < full else 64


def payload_rows(full, k):
    return 128 * k + 64 + 8 if k < full else 48 * k + 24 + 8


def payload_starts(full):
    starts, at = [], 0
    for k in range(full + 1):
        starts.append(at)
        at += payload_rows(full, k)
    return starts, at


def pack_square(block):
    top, bottom = block[:64], block[64:]
    lane = lax.broadcasted_iota(jnp.int32, top.shape, 1)
    line = lax.broadcasted_iota(jnp.int32, top.shape, 0)
    packed = jnp.where(line >= lane - 64, bottom, pltpu.roll(top, 64, 1))
    diagonal = jnp.sum(jnp.where(line == lane, top, 0.0), 0, keepdims=True)
    return packed, diagonal


def unpack_square(packed, diagonal):
    lane = lax.broadcasted_iota(jnp.int32, packed.shape, 1)
    line = lax.broadcasted_iota(jnp.int32, packed.shape, 0)
    flipped = jnp.concatenate([packed, packed], 0).T
    corner = jnp.where(line < lane, pltpu.roll(packed, 64, 1), flipped[64:])
    corner = jnp.where(line == lane, diagonal, corner)
    top = jnp.where(lane < 64, corner, flipped[:64])
    bottom = jnp.where(line >= lane - 64, packed, flipped[64:])
    return jnp.concatenate([top, bottom], 0)


def fold(block):
    lane = lax.broadcasted_iota(jnp.int32, (24, LANES), 1)
    return jnp.where(lane < 64, block[:24], pltpu.roll(block[24:], 64, 1))


def unfold(block):
    lane = lax.broadcasted_iota(jnp.int32, (48, LANES), 1)
    both = jnp.concatenate([block, pltpu.roll(block, 64, 1)], 0)
    return jnp.where(lane < 64, both, 0.0)


def squeeze(block):
    return jnp.concatenate([block[0:24], block[32:56]], 0)


def stretch(block):
    gap = jnp.zeros((8, block.shape[1]), block.dtype)
    return jnp.concatenate([block[0:24], gap, block[24:48], gap], 0)


def factor8(small):
    line = lax.broadcasted_iota(jnp.int32, small.shape[1:], 0)
    lower = []
    pivots = jnp.zeros(small.shape[1:], F32)
    for p in range(0, 8, 2):
        one, two = line == p, line == p + 1
        first, second = small[p], small[p + 1]
        a, b, c = first[p : p + 1], second[p : p + 1], second[p + 1 : p + 2]
        det = a * c - b * b
        ra = 1.0 / a
        t = b * ra
        pivots = jnp.where(one, a, jnp.where(two, det * ra, pivots))
        lower = [
            jnp.where(
                one,
                small[j],
                jnp.where(two, small[j] - t * small[j][p : p + 1], lower[j]),
            )
            for j in range(p)
        ]
        lower.append(jnp.where(one, 1.0, jnp.where(two, -t, 0.0)))
        lower.append(jnp.where(two, 1.0, 0.0))
        r = 1.0 / det
        ea, eb, ec = c * r, -b * r, a * r
        left = first * ea + second * eb
        right = first * eb + second * ec
        left = jnp.where(one, -ea, jnp.where(two, -eb, left))
        right = jnp.where(one, -eb, jnp.where(two, -ec, right))
        base = jnp.where((one | two)[None], 0.0, small)
        rest = base - (
            left[None] * small[:, p : p + 1] + right[None] * small[:, p + 1 : p + 2]
        )
        parts = [rest[:p]] if p else []
        parts.append(jnp.stack([-left, -right]))
        if p < 6:
            parts.append(rest[p + 2 :])
        small = jnp.concatenate(parts, 0)
    return small, lower, lax.rsqrt(pivots)


def mix(planes, lines):
    terms = [planes[j] * lines[j : j + 1] for j in range(8)]
    while len(terms) > 1:
        terms = [a + b for a, b in zip(terms[::2], terms[1::2])]
    return terms[0]


def block_factor(block, groups, midway=None):
    rows = block.shape[0]
    lane = lax.broadcasted_iota(jnp.int32, (8, LANES), 1)
    line = lax.broadcasted_iota(jnp.int32, (8, LANES), 0)
    result = [jnp.zeros((8, LANES), F32)] * (rows // 8)
    below, first = block, 0
    for g in groups:
        if midway is not None and g == 10:
            midway()
        k = 8 * g
        below = below[k - first :]
        top = below[:8]
        small = jnp.stack(
            [jnp.broadcast_to(top[:, k + j : k + j + 1], (8, LANES)) for j in range(8)]
        )
        small, lower, root = factor8(small)
        inside = (lane >= k) & (lane < k + 8)
        top = jnp.where(inside, jnp.where(lane == line + k, 1.0, 0.0), top)
        result[g] = jnp.where(lane < k + 8, mix(lower, top) * root, 0.0)
        below = below[8:]
        first = k + 8
        if below.shape[0]:
            new = mix(small, top)
            cols = [below[:, k + j : k + j + 1] for j in range(8)]
            keep = (lane[:1] < k) | (lane[:1] >= k + 8)
            below = jnp.where(keep, below, 0.0)
            for j in range(0, 8, 2):
                below = below - (
                    cols[j] * new[j : j + 1] + cols[j + 1] * new[j + 1 : j + 2]
                )
    return jnp.concatenate(result, 0)


def split2(x):
    high = x.astype(BF16)
    return high, (x - high.astype(F32)).astype(BF16)


def fused_kernel(
    tiles,
    img,
    index_hbm,
    yield_hbm,
    mask_hbm,
    fit,
    spread_ref,
    index_out,
    yield_out,
    feats,
    whole,
    tail,
    tail_in,
    index_ref,
    yield_ref,
    mask_ref,
    weight_rows,
    product_rows,
    acc,
    own,
    middle,
    outgoing,
    landed,
    inverse,
    split_r,
    rhs_ref,
    z_ref,
    fit8,
    spread8,
    local_sem,
    bulk_send,
    bulk_recv,
    z_send,
    z_recv,
    core_send,
    core_recv,
    x_send,
    x_recv,
):
    half, pixels = img.shape[2:]
    full = half // 64
    steps = full + 1
    rows = pixels // LANES
    scale = 1.0 / pixels
    starts, _ = payload_starts(full)
    mesh_ids = pl.DeviceIdType.MESH

    z = lax.axis_index("tiles")
    c = lax.axis_index("cols")
    d = lax.axis_index("dates")
    across = {"dates": 1 - d}
    core = {"cols": 1 - c}
    up, down = {"tiles": z + 1}, {"tiles": z - 1}
    has_up, has_down = z < tiles - 1, z > 0
    joins = c == d

    def place(k, s):
        if k < full:
            return pl.multiple_of(128 * k + 64 * s, 16)
        return pl.multiple_of(128 * full + 32 * s, 16)

    height = [64] * full + [16]
    source_at = [64 * k for k in range(steps)]

    local = [
        pltpu.make_async_copy(index_hbm.at[0], index_ref, local_sem.at[0]),
        pltpu.make_async_copy(yield_hbm.at[0], yield_ref, local_sem.at[1]),
        pltpu.make_async_copy(mask_hbm, mask_ref, local_sem.at[2]),
        pltpu.make_async_copy(img.at[0], whole, local_sem.at[3]),
    ]
    for k in range(steps):
        local.append(
            pltpu.make_async_copy(
                img.at[0, d, pl.ds(source_at[k], height[k])],
                feats.at[pl.ds(place(k, d), height[k])],
                local_sem.at[4 + k],
            )
        )
    for copy in local:
        copy.start()

    barrier = pltpu.get_barrier_semaphore()
    peers = ((has_up, up), (has_down, down), (None, core), (None, across))
    for there, target in peers:

        def greet(target=target):
            pl.semaphore_signal(
                barrier, inc=1, device_id=target, device_id_type=mesh_ids
            )

        if there is None:
            greet()
        else:
            pl.when(there)(greet)
    pl.semaphore_wait(barrier, 2 + has_up.astype(jnp.int32) + has_down.astype(jnp.int32))

    bulk = []
    for k in range(steps):
        bulk.append(
            pltpu.make_async_remote_copy(
                src_ref=img.at[0, 1 - d, pl.ds(source_at[k], height[k])],
                dst_ref=feats.at[pl.ds(place(k, d), height[k])],
                send_sem=bulk_send.at[k],
                recv_sem=bulk_recv.at[k],
                device_id=across,
                device_id_type=mesh_ids,
            )
        )
    bulk.append(
        pltpu.make_async_remote_copy(
            src_ref=tail,
            dst_ref=tail_in,
            send_sem=bulk_send.at[steps],
            recv_sem=bulk_recv.at[steps],
            device_id=across,
            device_id_type=mesh_ids,
        )
    )
    bulk[0].start()
    bulk[1].start()

    for copy in local[:4]:
        copy.wait()
    end = whole[1 - d][half - 8 : half]
    tail[...] = jnp.concatenate([end[:, : pixels // 2], end[:, pixels // 2 :]], 0)

    def put_tail(s, end):
        at = pl.ds(pl.multiple_of(128 * full + 32 * s + 16, 16), 16)
        feats[at, :] = jnp.concatenate([end, jnp.zeros_like(end)], 0)

    put_tail(d, whole[d][half - 8 : half])

    high, low = one_hots(index_ref[...], rows)
    low = jnp.where(low, 1.0, 0.0).astype(BF16)
    index_out[...] = index_ref[...]
    yield_out[...] = yield_ref[...]
    parts = [jnp.where(high, 1.0, 0.0).astype(BF16)]
    for piece in split3(yield_ref[...]):
        parts.append(jnp.where(high, piece.astype(F32), 0.0).astype(BF16))
    sums = lax.dot_general(
        jnp.concatenate(parts, 0), low, NT, preferred_element_type=F32
    )
    counts = sums[:rows]
    totals = sums[rows : 2 * rows] + sums[2 * rows : 3 * rows] + sums[3 * rows :]
    weight = jnp.where(counts > 0, mask_ref[...].astype(F32), 0.0)
    product = weight * (totals / jnp.maximum(counts, 1.0))
    pa, pb, pc = (p.astype(F32) for p in split3(product))
    line16 = lax.broadcasted_iota(jnp.int32, (16, LANES), 0)
    for r in range(rows):
        at = slice(r * LANES, (r + 1) * LANES)
        weight_rows[:, at] = jnp.broadcast_to(weight[r : r + 1], (16, LANES)).astype(BF16)
        extra = jnp.where(
            line16 == 0,
            pa[r : r + 1],
            jnp.where(
                line16 == 1,
                pb[r : r + 1],
                jnp.where(line16 == 2, pc[r : r + 1], 0.0),
            ),
        )
        product_rows[:, at] = extra.astype(BF16)

    acc[...] = jnp.zeros_like(acc)
    inverse[...] = jnp.zeros_like(inverse)
    fit8[...] = jnp.zeros_like(fit8)
    spread8[...] = jnp.zeros_like(spread8)

    def payload(k, h):
        count = payload_rows(full, k)
        first = count // 16 * 8
        if h == 0:
            return pl.ds(starts[k], first)
        return pl.ds(starts[k] + first, count - first)

    def z_copy(way, k, h, target):
        return pltpu.make_async_remote_copy(
            src_ref=own.at[payload(k, h)],
            dst_ref=landed.at[way, payload(k, h)],
            send_sem=z_send.at[way, 2 * k + h],
            recv_sem=z_recv.at[way, 2 * k + h],
            device_id=target,
            device_id_type=mesh_ids,
        )

    def core_copy(k, h):
        return pltpu.make_async_remote_copy(
            src_ref=middle.at[payload(k, h)],
            dst_ref=landed.at[2, payload(k, h)],
            send_sem=core_send.at[2 * k + h],
            recv_sem=core_recv.at[2 * k + h],
            device_id=core,
            device_id_type=mesh_ids,
        )

    def x_copy(k, h, source=outgoing):
        return pltpu.make_async_remote_copy(
            src_ref=source.at[payload(k, h)],
            dst_ref=landed.at[3, payload(k, h)],
            send_sem=x_send.at[2 * k + h],
            recv_sem=x_recv.at[2 * k + h],
            device_id=across,
            device_id_type=mesh_ids,
        )

    def gram(k):
        count = step_rows(full, k)
        base, end = 128 * k, 128 * k + count
        local[4 + k].wait()
        bulk[k].wait_recv()
        if k == full:
            bulk[steps].wait_recv()
            folded = tail_in[...]
            put_tail(1 - d, jnp.concatenate([folded[:8], folded[8:]], 1))
        wide = count + 16
        acc[:end, :wide] = jnp.zeros((end, wide), F32)

        def chunk(i, _):
            at = pl.ds(pl.multiple_of(i * SPAN, SPAN), SPAN)
            weights = jnp.concatenate([weight_rows[:, at]] * (count // 16), 0)
            left = jnp.concatenate(
                [feats[base:end, at] * weights, product_rows[:, at]], 0
            )
            acc[:end, :wide] += lax.dot_general(
                feats[:end, at], left, NT, preferred_element_type=F32
            )
            return 0

        lax.fori_loop(0, pixels // SPAN, chunk, 0)
        at = starts[k]
        diagonal = jnp.zeros((1, LANES), F32)
        for j in range(k + 1):
            block = acc[128 * j : 128 * j + 128, :LANES]
            if k == full:
                block = squeeze(block.T)
            if j == k and k < full:
                block, diagonal = pack_square(block)
            if j == k and k == full:
                block = fold(block)
            own[at : at + block.shape[0]] = block
            at += block.shape[0]
        moment = acc[base : base + 128, count : count + 1]
        moment = moment + acc[base : base + 128, count + 1 : count + 2]
        moment = moment + acc[base : base + 128, count + 2 : count + 3]
        moment = jnp.broadcast_to(moment, (LANES, LANES)).T
        line8 = lax.broadcasted_iota(jnp.int32, (8, LANES), 0)
        own[at : at + 8] = jnp.where(line8 == 0, moment[:8], diagonal)
        for h in range(2):
            pl.when(has_up)(lambda h=h: z_copy(0, k, h, up).start())
            pl.when(has_down)(lambda h=h: z_copy(1, k, h, down).start())

    def z_join(k):
        for h in range(2):
            at = payload(k, h)

            @pl.when(has_down)
            def _(h=h, at=at):
                z_copy(0, k, h, down).wait_recv()
                middle[at] = own[at] + 0.5 * landed[0, at]

            @pl.when(jnp.logical_not(has_down))
            def _(at=at):
                middle[at] = own[at]

            @pl.when(has_up)
            def _(h=h, at=at):
                z_copy(1, k, h, up).wait_recv()
                middle[at] += 0.5 * landed[1, at]

            @pl.when(jnp.logical_not(joins))
            def _(h=h):
                core_copy(k, h).start()
                x_copy(k, h, middle).start()

        @pl.when(joins)
        def _():
            for h in range(2):
                at = payload(k, h)
                core_copy(k, h).wait_recv()
                outgoing[at] = middle[at] + landed[2, at]
                x_copy(k, h).start()

        if k + 2 < steps:
            bulk[k + 2].start()
        if k + 2 == full:
            bulk[steps].start()

    def solve(k, midway=None):
        at = pl.ds(starts[k], payload_rows(full, k))
        for h in range(2):
            x_copy(k, h).wait_recv()
        count = step_rows(full, k)
        base = 128 * k
        window = (middle[at] + 0.5 * landed[3, at]) * scale
        step = 128 if k < full else 48
        blocks = [window[j * step : (j + 1) * step] for j in range(k)]
        ends = window[payload_rows(full, k) - 8 :]
        rhs_ref[:, base : base + 128] = ends
        square = window[k * step : payload_rows(full, k) - 8]
        if k < full:
            blocks.append(unpack_square(square, ends[1:2]))
        else:
            blocks.append(unfold(square))
            blocks = [stretch(block) for block in blocks]
        lane = lax.broadcasted_iota(jnp.int32, (count, LANES), 1)
        line = lax.broadcasted_iota(jnp.int32, (count, LANES), 0)
        pivot = blocks[k] + jnp.where(lane == line, ridge_term, 0.0)
        if k:
            known = inverse[:base, :base]
            if k < full:
                raised = dot32(known, jnp.concatenate(blocks[:k], 0))
                factor = jnp.concatenate(
                    [raised[128 * j : 128 * j + 128].T for j in range(k)], 1
                )
                drop = dot32(factor, raised)
            else:
                factor = dot32(jnp.concatenate(blocks[:k], 1), known, NT)
                drop = dot32(factor, factor, NT)
            coupling = dot32(factor, known)
            if count < LANES:
                drop = jnp.concatenate(
                    [drop, jnp.zeros((count, LANES - count), F32)], 1
                )
            pivot = pivot - drop
        groups = range(16) if k < full else (0, 1, 2, 4, 5, 6)
        lower = block_factor(pivot, groups, midway)
        if k:
            lower = jnp.concatenate([-dot32(lower[:, :count], coupling), lower], 1)
        z_ref[:count] = jnp.sum(
            lower * rhs_ref[:1, : base + 128], 1, keepdims=True
        )
        high, low = split2(lower)
        split_r[:count, : base + 128] = high
        split_r[count : 2 * count, : base + 128] = low
        if k < full:
            inverse[base : base + count, : base + 128] = lower

    def spread(k):
        count = step_rows(full, k)
        end = 128 * k + count
        last = k == full

        def chunk(i, _):
            at = pl.ds(pl.multiple_of(i * SPAN, SPAN), SPAN)
            part = feats[:end, at]
            both = jnp.dot(
                split_r[: 2 * count, :end], part, preferred_element_type=F32
            )
            value = both[:count] + both[count:]
            square = (value * value).reshape(count // 8, 8, SPAN)
            linear = (value * z_ref[:count]).reshape(count // 8, 8, SPAN)
            square = spread8[:, at] + jnp.sum(square, 0)
            linear = fit8[:, at] + jnp.sum(linear, 0)
            if last:
                spread_ref[:, at] = jnp.sum(square, 0, keepdims=True) / (2 * half)
                fitted = jnp.sum(linear, 0, keepdims=True)
                for s in range(SPAN // LANES):
                    fit[pl.ds(i * (SPAN // LANES) + s, 1), :] = fitted[
                        :, s * LANES : (s + 1) * LANES
                    ]
            else:
                spread8[:, at] = square
                fit8[:, at] = linear
            return 0

        lax.fori_loop(0, pixels // SPAN, chunk, 0)

    gram(0)
    z_join(0)
    for k in range(1, steps):
        gram(k)
        if k == full:
            spread(k - 2)
        solve(k - 1, lambda k=k: z_join(k))
        if k != full - 1:
            spread(k - 1)
    solve(full)
    spread(full)

    for copy in bulk:
        copy.wait_send()
    for k in range(steps):
        for h in range(2):
            pl.when(has_up)(lambda k=k, h=h: z_copy(0, k, h, up).wait_send())
            pl.when(has_down)(lambda k=k, h=h: z_copy(1, k, h, down).wait_send())
            pl.when(jnp.logical_not(joins))(
                lambda k=k, h=h: core_copy(k, h).wait_send()
            )
            x_copy(k, h).wait_send()


def fused(imagery, index, yields, mask):
    half, pixels = imagery.shape[2:]
    full = half // 64
    steps = full + 1
    rows = payload_starts(full)[1]
    size = 128 * steps
    shape = jax.ShapeDtypeStruct((1, pixels), F32)
    in_hbm = pl.BlockSpec(memory_space=pltpu.HBM)
    in_vmem = pl.BlockSpec(memory_space=pltpu.VMEM)
    dma = pltpu.SemaphoreType.DMA
    return pl.pallas_call(
        functools.partial(fused_kernel, lax.axis_size("tiles")),
        out_shape=(
            pltpu.VMEM((pixels // LANES, LANES), F32),
            pltpu.VMEM((1, pixels), F32),
            pltpu.VMEM((1, pixels), jnp.int32),
            pltpu.VMEM((1, pixels), F32),
        ),
        in_specs=[in_hbm] * 4,
        out_specs=(in_vmem,) * 4,
        scratch_shapes=[
            pltpu.VMEM((128 * full + 64, pixels), BF16),
            pltpu.VMEM((2, half, pixels), BF16),
            pltpu.VMEM((16, pixels // 2), BF16),
            pltpu.VMEM((16, pixels // 2), BF16),
            pltpu.VMEM((1, pixels), jnp.int32),
            pltpu.VMEM((1, pixels), F32),
            pltpu.VMEM((pixels // LANES, LANES), jnp.int32),
            pltpu.VMEM((16, pixels), BF16),
            pltpu.VMEM((16, pixels), BF16),
            pltpu.VMEM((size, 2 * LANES), F32),
            pltpu.VMEM((rows, LANES), F32),
            pltpu.VMEM((rows, LANES), F32),
            pltpu.VMEM((rows, LANES), F32),
            pltpu.VMEM((4, rows, LANES), F32),
            pltpu.VMEM((size, size), F32),
            pltpu.VMEM((2 * LANES, size), BF16),
            pltpu.VMEM((8, size), F32),
            pltpu.VMEM((LANES, 1), F32),
            pltpu.VMEM((8, pixels), F32),
            pltpu.VMEM((8, pixels), F32),
            dma((4 + steps,)),
            dma((steps + 1,)),
            dma((steps + 1,)),
            dma((2, 2 * steps)),
            dma((2, 2 * steps)),
            dma((2 * steps,)),
            dma((2 * steps,)),
            dma((2 * steps,)),
            dma((2 * steps,)),
        ],
        compiler_params=pltpu.CompilerParams(
            collective_id=1,
            has_side_effects=True,
            vmem_limit_bytes=56 * 1024 * 1024,
        ),
        name="fused",
    )(imagery, index, yields, mask)


def finish_kernel(
    fit_ref, spread_in, index_ref, yield_ref, fitted_ref, spread_ref, resid_ref
):
    rows = fit_ref.shape[0]
    fit = fit_ref[...]
    high, low = one_hots(index_ref[...], rows)
    low = jnp.where(low, 1.0, 0.0).astype(BF16)
    table = jnp.concatenate(split3(fit), 0)
    found = jnp.dot(table, low, preferred_element_type=F32)
    found = found[:rows] + (found[rows : 2 * rows] + found[2 * rows :])
    value = jnp.sum(jnp.where(high, found, 0.0), 0, keepdims=True)
    resid_ref[...] = yield_ref[...] - value
    for r in range(rows):
        fitted_ref[:, r * LANES : (r + 1) * LANES] = fit[r : r + 1]
    spread_ref[...] = spread_in[...]


def finish(fit, spread, index, yields):
    shape = jax.ShapeDtypeStruct(spread.shape, F32)
    return pl.pallas_call(
        finish_kernel,
        out_shape=(shape, shape, shape),
        compiler_params=pltpu.CompilerParams(vmem_limit_bytes=16 * 1024 * 1024),
        name="finish",
    )(fit, spread, index, yields)


def on_device_fused(imagery, pixel_mask, point_pixel, point_yield):
    pixels = imagery.shape[3]
    mask = pixel_mask.reshape(pixels // LANES, LANES)
    fitted, spread, resid = finish(*fused(imagery, point_pixel, point_yield, mask))
    return (fitted[None], spread[None], resid[None])


def solution(mesh):
    features = P(("groups", "tiles"), "cols", "dates", None)
    points = P(("groups", "tiles"), ("cols", "dates"), None)
    sizes = dict(mesh.shape)

    def body(imagery, pixel_mask, point_pixel, point_yield):
        pairs = sizes["cols"] == 2 and sizes["dates"] == 2
        one_tile = imagery.shape[:2] == (1, 2)
        if pairs and one_tile and imagery.shape[2] % 64 == 24:
            run = on_device_fused
        else:
            run = on_device
        return run(imagery, pixel_mask, point_pixel, point_yield)

    return jax.shard_map(
        body,
        mesh=mesh,
        in_specs=(features, points, points, points),
        out_specs=(points, points, points),
        check_vma=False,
    )
```
